32 devices in a mesh: wide: 8 (over z, core), narrow: 4 (over y, x).
Axes of the slice: x: 2, y: 2, z: 4, core: 2. Of those that a mesh axis runs over, the one named last changes fastest.
Arguments:
- image_tokens: bfloat16 [32, 1024, 1024], P(('wide', 'narrow')), may hold values from -6 to 6
- text_states: bfloat16 [8, 128, 1024], P('wide', 'narrow'), may hold values from -6 to 6
- text_segments: int32 [8, 128], P('wide'), may hold values from 0 to 3, never falling along the last dimension, each value on 1 to 64 neighbouring positions
- image_segment: int32 [8, 4], P('wide', 'narrow'), may hold values from 0 to 3, each once within a row
- out_grad: bfloat16 [32, 1024, 1024], P(('wide', 'narrow')), may hold values from -6 to 6
- norm1_gain: bfloat16 [1024], P(('wide', 'narrow')), may hold values from 0.5 to 1.5
- norm1_bias: bfloat16 [1024], P(('wide', 'narrow')), may hold values from -1.75 to 1.75
- self_query: bfloat16 [1024, 1024], P(('wide', 'narrow')), may hold values from -0.1875 to 0.1875
- self_key: bfloat16 [1024, 1024], P(('wide', 'narrow')), may hold values from -0.1875 to 0.1875
- self_value: bfloat16 [1024, 1024], P(('wide', 'narrow')), may hold values from -0.1875 to 0.1875
- self_output: bfloat16 [1024, 1024], P(('wide', 'narrow')), may hold values from -0.5 to 0.5
- norm2_gain: bfloat16 [1024], P(('wide', 'narrow')), may hold values from 0.5 to 1.5
- norm2_bias: bfloat16 [1024], P(('wide', 'narrow')), may hold values from -1.75 to 1.75
- cross_query: bfloat16 [1024, 1024], P(('wide', 'narrow')), may hold values from -0.1875 to 0.1875
- cross_key: bfloat16 [1024, 1024], P(('wide', 'narrow')), may hold values from -0.1875 to 0.1875
- cross_value: bfloat16 [1024, 1024], P(('wide', 'narrow')), may hold values from -0.1875 to 0.1875
- cross_output: bfloat16 [1024, 1024], P(('wide', 'narrow')), may hold values from -0.375 to 0.375
- norm3_gain: bfloat16 [1024], P(('wide', 'narrow')), may hold values from 0.5 to 1.5
- norm3_bias: bfloat16 [1024], P(('wide', 'narrow')), may hold values from -1.75 to 1.75
- mlp_in: bfloat16 [1024, 4096], P(('wide', 'narrow')), may hold values from -0.1875 to 0.1875
- mlp_in_bias: bfloat16 [4096], P(('wide', 'narrow')), may hold values from -1.75 to 1.75
- mlp_out: bfloat16 [4096, 1024], P(('wide', 'narrow')), may hold values from -0.09375 to 0.09375
- mlp_out_bias: bfloat16 [1024], P(('wide', 'narrow')), may hold values from -1.75 to 1.75
Outputs:
- block_out: bfloat16 [32, 1024, 1024], P(('wide', 'narrow'))
- image_grad: float32 [32, 1024, 1024], P(('wide', 'narrow'))
- text_grad: float32 [8, 128, 1024], P('wide', 'narrow')
- grad_norm1_gain: float32 [1024], P(('wide', 'narrow'))
- grad_norm1_bias: float32 [1024], P(('wide', 'narrow'))
- grad_self_query: float32 [1024, 1024], P(('wide', 'narrow'))
- grad_self_key: float32 [1024, 1024], P(('wide', 'narrow'))
- grad_self_value: float32 [1024, 1024], P(('wide', 'narrow'))
- grad_self_output: float32 [1024, 1024], P(('wide', 'narrow'))
- grad_norm2_gain: float32 [1024], P(('wide', 'narrow'))
- grad_norm2_bias: float32 [1024], P(('wide', 'narrow'))
- grad_cross_query: float32 [1024, 1024], P(('wide', 'narrow'))
- grad_cross_key: float32 [1024, 1024], P(('wide', 'narrow'))
- grad_cross_value: float32 [1024, 1024], P(('wide', 'narrow'))
- grad_cross_output: float32 [1024, 1024], P(('wide', 'narrow'))
- grad_norm3_gain: float32 [1024], P(('wide', 'narrow'))
- grad_norm3_bias: float32 [1024], P(('wide', 'narrow'))
- grad_mlp_in: float32 [1024, 4096], P(('wide', 'narrow'))
- grad_mlp_in_bias: float32 [4096], P(('wide', 'narrow'))
- grad_mlp_out: float32 [4096, 1024], P(('wide', 'narrow'))
- grad_mlp_out_bias: float32 [1024], P(('wide', 'narrow'))
The draws below stay inside these ranges and needn't reach their ends.
Inputs may be any that keep to these rules, and one draw needn't show every extreme that they name: `text_segments`: within a text row slot caption numbers never fall; each of the 4 captions fills 1 to 64 slots, and one fills exactly 64. `image_segment`: the 4 images of a text row name its captions, each caption once.
All inputs are finite; a program needn't handle non-finite values.
Results may differ from the reference program's by a relative error of at most 0.015.
Values may be sent and summed in bfloat16 or wider, within the bound.
A program may use at most 320 MiB of HBM per device.

```python
import math
import jax
import jax.numpy as jnp
import numpy as np
from jax import lax

D = 1024
HEADS = 16
HEAD_DIM = 64
FF = 4096
IMG_LEN = 1024
SLOTS = 128
CAPTIONS = 4
ROWS = 8
IMAGES = 32
CAP_MOST = 64


def block_scale(own_key, dims, cuts, smallest, largest):
    factor_of, own = 1.0, jax.random.fold_in(own_key, 6)
    for axis_at, shards_of in cuts:
        draws = jnp.exp(jax.random.uniform(jax.random.fold_in(own, axis_at), (shards_of,), jnp.float32, smallest / len(cuts), largest / len(cuts)))
        factor_of = factor_of * jnp.repeat(draws, dims[axis_at] // shards_of).reshape([-1 if axis == axis_at else 1 for axis in range(len(dims))])
    return factor_of


def split_up(number_of, total, limit, slope):
    portions = [(1 << 20) // math.isqrt(standing ** slope) + 1 for standing in range(2, number_of + 1)]
    rest, given = total - limit - (number_of - 1), [1] * (number_of - 1)
    while rest > 0:
        free = [i for i in range(number_of - 1) if given[i] < limit]
        whole, remaining = sum([portions[i] for i in free]), rest
        for i in free:
            more = min(limit - given[i], max(1, remaining * portions[i] // whole), rest)
            given[i] = given[i] + more
            rest = rest - more
    return np.array([limit] + given)


def uneven_parts(key, count, total, limit, lean):
    if count == 2:
        one = jax.random.randint(key, (), max(1, total - limit), min(limit, total - 1) + 1)
        return jnp.stack([one, total - one])
    sizes = jnp.asarray(split_up(count, total, limit, lean), jnp.int32)
    pairs = (count - 1) // 2
    source_of, receiver = sizes[1:1 + 2 * pairs:2], sizes[2:2 + 2 * pairs:2]
    margin = jnp.minimum(source_of - 1, limit - receiver)
    moved = jax.random.randint(jax.random.fold_in(key, 1), (pairs,), 0, 1 << 20) % (margin + 1)
    sizes = sizes.at[1:1 + 2 * pairs:2].set(source_of - moved).at[2:2 + 2 * pairs:2].set(receiver + moved)
    return sizes[jax.random.permutation(jax.random.fold_in(key, 2), count)]


def scatter_about(stream_key, shape, scale, most, split=(), held_as=jnp.bfloat16):
    entries = scale * jax.random.normal(stream_key, shape, jnp.float32)
    if split:
        entries = entries * block_scale(stream_key, shape, split, -0.22, 0.18)
    return jnp.clip(entries, -most, most).astype(held_as)


def setup_inputs(seed: int = 0) -> dict:
    seeds = jax.random.split(jax.random.key(seed), 24)
    image_tokens = scatter_about(seeds[0], (IMAGES, IMG_LEN, D), 1.0, 6.0, ((0, 32),))
    text_states = scatter_about(seeds[1], (ROWS, SLOTS, D), 1.0, 6.0, ((0, 8), (1, 4)))
    text_segments = jax.vmap(lambda own: jnp.searchsorted(jnp.cumsum(uneven_parts(own, CAPTIONS, SLOTS, CAP_MOST, 1)), jnp.arange(SLOTS), side="right"))(jax.random.split(seeds[2], ROWS)).reshape((ROWS, SLOTS)).astype(jnp.int32)
    image_segment = jax.vmap(lambda own: jax.random.permutation(own, CAPTIONS))(jax.random.split(seeds[3], ROWS)).reshape((ROWS, CAPTIONS)).astype(jnp.int32)
    out_grad = scatter_about(seeds[4], (IMAGES, IMG_LEN, D), 1.0, 6.0, ((0, 32),))
    norm1_gain = jnp.clip(1.0 + 0.1 * jax.random.normal(seeds[5], (D,), jnp.float32), 0.5, 1.5).astype(jnp.bfloat16)
    norm1_bias = scatter_about(seeds[6], (D,), 0.3, 1.75, ((0, 32),))
    self_query = scatter_about(seeds[7], (D, D), D ** -0.5, 0.1875, ((0, 32),))
    self_key = scatter_about(seeds[8], (D, D), D ** -0.5, 0.1875, ((0, 32),))
    self_value = scatter_about(seeds[9], (D, D), D ** -0.5, 0.1875, ((0, 32),))
    self_output = scatter_about(seeds[10], (D, D), (D // 8) ** -0.5, 0.5, ((0, 32),))
    norm2_gain = jnp.clip(1.0 + 0.1 * jax.random.normal(seeds[11], (D,), jnp.float32), 0.5, 1.5).astype(jnp.bfloat16)
    norm2_bias = scatter_about(seeds[12], (D,), 0.3, 1.75, ((0, 32),))
    cross_query = scatter_about(seeds[13], (D, D), D ** -0.5, 0.1875, ((0, 32),))
    cross_key = scatter_about(seeds[14], (D, D), D ** -0.5, 0.1875, ((0, 32),))
    cross_value = scatter_about(seeds[15], (D, D), D ** -0.5, 0.1875, ((0, 32),))
    cross_output = scatter_about(seeds[16], (D, D), (D // 4) ** -0.5, 0.375, ((0, 32),))
    norm3_gain = jnp.clip(1.0 + 0.1 * jax.random.normal(seeds[17], (D,), jnp.float32), 0.5, 1.5).astype(jnp.bfloat16)
    norm3_bias = scatter_about(seeds[18], (D,), 0.3, 1.75, ((0, 32),))
    mlp_in = scatter_about(seeds[19], (D, FF), D ** -0.5, 0.1875, ((0, 32),))
    mlp_in_bias = scatter_about(seeds[20], (FF,), 0.3, 1.75, ((0, 32),))
    mlp_out = scatter_about(seeds[21], (FF, D), FF ** -0.5, 0.09375, ((0, 32),))
    mlp_out_bias = scatter_about(seeds[22], (D,), 0.3, 1.75, ((0, 32),))
    return dict(image_tokens=image_tokens, text_states=text_states, text_segments=text_segments, image_segment=image_segment, out_grad=out_grad, norm1_gain=norm1_gain, norm1_bias=norm1_bias, self_query=self_query, self_key=self_key, self_value=self_value, self_output=self_output, norm2_gain=norm2_gain, norm2_bias=norm2_bias, cross_query=cross_query, cross_key=cross_key, cross_value=cross_value, cross_output=cross_output, norm3_gain=norm3_gain, norm3_bias=norm3_bias, mlp_in=mlp_in, mlp_in_bias=mlp_in_bias, mlp_out=mlp_out, mlp_out_bias=mlp_out_bias)


EPSILON = 1e-05
NEGATIVE = -1e+30
HIGHEST = lax.Precision.HIGHEST

@jax.custom_vjp
def low(v):
    return lax.optimization_barrier(v.astype(jnp.bfloat16)).astype(jnp.float32)

@jax.custom_vjp
def low_back(v):
    return v

def low_keep(v):
    return (low(v), None)

def low_pass(kept, grad):
    return (grad,)

def back_keep(v):
    return (v, None)

def back_low(kept, grad):
    return (low(grad),)
low.defvjp(low_keep, low_pass)
low_back.defvjp(back_keep, back_low)

def matmul(leading, trailing):
    return jnp.dot(leading, trailing, precision=HIGHEST, preferred_element_type=jnp.float32)

def layer_norm(values, norm_gain, norm_bias):
    center = lax.optimization_barrier(jnp.mean(values, axis=-1, keepdims=True))
    offset = values - center
    spread = lax.optimization_barrier(jnp.mean(offset * offset, axis=-1, keepdims=True))
    return offset * lax.rsqrt(spread + EPSILON) * norm_gain + norm_bias

def project(values, matrix):
    return low_back(low(matmul(values, matrix)))

def attend(queries, key_rows, value_rows, allowed):
    row_count = queries.shape[0]
    key_count = key_rows.shape[0]
    query_heads = queries.reshape(row_count, HEADS, HEAD_DIM)
    key_heads = key_rows.reshape(key_count, HEADS, HEAD_DIM)
    value_heads = value_rows.reshape(key_count, HEADS, HEAD_DIM)
    scores = jnp.einsum('qhe,khe->hqk', query_heads, key_heads, precision=HIGHEST)
    scores = low_back(scores * HEAD_DIM ** (-0.5))
    scores = jnp.where(allowed, scores, NEGATIVE)
    weights = low(jax.nn.softmax(scores, axis=-1))
    mixture = jnp.einsum('hqk,khe->qhe', weights, value_heads, precision=HIGHEST)
    return low_back(low(mixture.reshape(row_count, HEADS * HEAD_DIM)))

def forward(tokens, text_rows, segment_ids, own_segment, params):
    gain_one, bias_one, w_query, w_key, w_value, w_output, gain_two, bias_two, c_query, c_key, c_value, c_output, gain_three, bias_three, up_matrix, up_bias, down_matrix, down_bias = params
    row_count = tokens.shape[0]
    normed = low(layer_norm(tokens, gain_one, bias_one))
    queries = project(normed, w_query)
    key_rows = project(normed, w_key)
    value_rows = project(normed, w_value)
    row_pos = lax.broadcasted_iota(jnp.int32, (row_count, row_count), 0)
    column_pos = lax.broadcasted_iota(jnp.int32, (row_count, row_count), 1)
    causal = (row_pos >= column_pos)[None]
    mixed_self = attend(queries, key_rows, value_rows, causal)
    after_self = tokens + low_back(matmul(mixed_self, w_output))
    normed = low(layer_norm(after_self, gain_two, bias_two))
    cross_queries = project(normed, c_query)
    cross_keys = project(text_rows, c_key)
    cross_values = project(text_rows, c_value)
    matches = (segment_ids == own_segment)[None, None, :]
    mixed_cross = attend(cross_queries, cross_keys, cross_values, matches)
    after_cross = after_self + low_back(matmul(mixed_cross, c_output))
    normed = low(layer_norm(after_cross, gain_three, bias_three))
    hidden_pre = low_back(matmul(normed, up_matrix) + up_bias)
    hidden = low(jax.nn.gelu(hidden_pre, approximate=False))
    return after_cross + low_back(matmul(hidden, down_matrix) + down_bias)

def reference(image_tokens, text_states, text_segments, image_segment, out_grad, norm1_gain, norm1_bias, self_query, self_key, self_value, self_output, norm2_gain, norm2_bias, cross_query, cross_key, cross_value, cross_output, norm3_gain, norm3_bias, mlp_in, mlp_in_bias, mlp_out, mlp_out_bias):
    params = tuple((weight.astype(jnp.float32) for weight in (norm1_gain, norm1_bias, self_query, self_key, self_value, self_output, norm2_gain, norm2_bias, cross_query, cross_key, cross_value, cross_output, norm3_gain, norm3_bias, mlp_in, mlp_in_bias, mlp_out, mlp_out_bias)))

    def accumulate(running, image_index):
        weight_sums, text_sum = running
        row_index = image_index // CAPTIONS
        tokens = image_tokens[image_index].astype(jnp.float32)
        text_rows = text_states[row_index].astype(jnp.float32)
        segment_ids = text_segments[row_index]
        own_segment = image_segment[row_index, image_index % CAPTIONS]

        def single_image(tokens, text_rows, params):
            return forward(tokens, text_rows, segment_ids, own_segment, params)
        result, pullback = jax.vjp(single_image, tokens, text_rows, params)
        grad_tokens, grad_text, grad_params = pullback(out_grad[image_index].astype(jnp.float32))
        weight_sums = jax.tree.map(jnp.add, weight_sums, grad_params)
        text_sum = text_sum.at[row_index].add(grad_text)
        return ((weight_sums, text_sum), (result.astype(jnp.bfloat16), grad_tokens))
    initial = (tuple((jnp.zeros_like(weight) for weight in params)), jnp.zeros(text_states.shape, jnp.float32))
    finals, stacked = lax.scan(accumulate, initial, jnp.arange(IMAGES, dtype=jnp.int32))
    weight_sums, text_sum = finals
    outputs, grad_images = stacked
    return (outputs, grad_images, text_sum, weight_sums[0], weight_sums[1], weight_sums[2], weight_sums[3], weight_sums[4], weight_sums[5], weight_sums[6], weight_sums[7], weight_sums[8], weight_sums[9], weight_sums[10], weight_sums[11], weight_sums[12], weight_sums[13], weight_sums[14], weight_sums[15], weight_sums[16], weight_sums[17])
```

```python
import jax
import jax.numpy as jnp
from jax import lax
from jax.sharding import PartitionSpec as P

HEAD_DIM = 64


EPSILON = 1e-05
NEGATIVE = -1e30


def matmul(leading, trailing):
    return jnp.dot(leading, trailing, preferred_element_type=jnp.float32)


def matmul_nt(leading, trailing):
    return lax.dot_general(
        leading, trailing, (((1,), (1,)), ((), ())), preferred_element_type=jnp.float32
    )


def matmul_tn(leading, trailing):
    return lax.dot_general(
        leading, trailing, (((0,), (0,)), ((), ())), preferred_element_type=jnp.float32
    )


def layer_norm(values, norm_gain, norm_bias):
    center = jnp.mean(values, axis=-1, keepdims=True)
    offset = values - center
    spread = jnp.mean(offset * offset, axis=-1, keepdims=True)
    return offset * lax.rsqrt(spread + EPSILON) * norm_gain + norm_bias


def exact_gelu(values):
    return jax.nn.gelu(values, approximate=False)


AXES = ("wide", "narrow")


def axis_bits(axis):
    return lax.axis_size(axis).bit_length() - 1


def halving_order(kind):
    wide = [("wide", k) for k in range(1, axis_bits("wide"))]
    narrow = [("narrow", k) for k in range(axis_bits("narrow"))]
    core = [("wide", 0)]
    if kind == 0:
        return core + narrow + wide
    if kind == 1:
        return core + narrow[1:] + wide[:1] + narrow[:1] + wide[1:]
    return core + wide[:1] + narrow + wide[1:]


def swap_with(block, axis, bit):
    count = lax.axis_size(axis)
    return lax.ppermute(block, axis, [(i, i ^ (1 << bit)) for i in range(count)])


def scatter_sum(term, kind, sent=jnp.bfloat16):
    left = [("wide", k) for k in reversed(range(axis_bits("wide")))]
    left += [("narrow", k) for k in reversed(range(axis_bits("narrow")))]
    owners = 1 << len(left)
    tail = (term.shape[0] // owners,) + term.shape[1:]
    state = term
    for axis, bit in halving_order(kind):
        at = left.index((axis, bit))
        left.pop(at)
        state = state.reshape((1 << at, 2, 1 << (len(left) - at)) + tail)
        mine = (lax.axis_index(axis) >> bit) & 1
        away = lax.dynamic_index_in_dim(state, 1 - mine, 1, keepdims=False).astype(sent)
        kept = lax.dynamic_index_in_dim(state, mine, 1, keepdims=False)
        arrived = swap_with(away, axis, bit)
        state = kept.astype(jnp.float32) + arrived.astype(jnp.float32)
        if left:
            state = state.astype(sent)
    return state.reshape(tail)


def gather_rows(packed):
    whole = lax.all_gather(packed, AXES, axis=0, tiled=True)
    return whole.reshape((-1,) + packed.shape)


def pack_vectors(vectors):
    flat = jnp.concatenate(vectors)
    room = -flat.shape[0] % 1024
    return jnp.pad(flat, (0, room)).reshape(-1, 1024)


def take_vectors(rows, sizes):
    flat = rows.reshape(rows.shape[0], -1)
    out, at = [], 0
    for size in sizes:
        out.append(flat[:, at : at + size].reshape(-1).astype(jnp.float32))
        at += size
    return out


def text_partners():
    return range(1, lax.axis_size("narrow"))


def swap_narrow(block, offset):
    count = lax.axis_size("narrow")
    return lax.ppermute(block, "narrow", [(i, i ^ offset) for i in range(count)])


def head_slices(source, column, pair_width):
    return lax.dynamic_slice_in_dim(source, column, pair_width, 1).reshape(
        source.shape[0], 2, HEAD_DIM
    )


def attend_forward(queries, key_rows, value_rows, allowed):
    row_count = queries.shape[0]
    pair_width = 2 * HEAD_DIM
    groups = queries.shape[1] // pair_width
    scaling = HEAD_DIM ** (-0.5)

    def per_group(group_index, running):
        result, log_sums = running
        column = group_index * pair_width
        query_pair = head_slices(queries, column, pair_width)
        key_pair = head_slices(key_rows, column, pair_width)
        value_pair = head_slices(value_rows, column, pair_width)
        scores = (
            jnp.einsum("qhe,khe->hqk", query_pair, key_pair, preferred_element_type=jnp.float32)
            * scaling
        )
        scores = jnp.where(allowed, scores, NEGATIVE)
        row_max = jnp.max(scores, axis=2, keepdims=True)
        exp_scores = jnp.exp(scores - row_max)
        row_total = jnp.sum(exp_scores, axis=2, keepdims=True)
        weights = (exp_scores / row_total).astype(jnp.bfloat16)
        mixture = jnp.einsum(
            "hqk,khe->qhe", weights, value_pair, preferred_element_type=jnp.float32
        )
        result = lax.dynamic_update_slice_in_dim(
            result, mixture.reshape(row_count, pair_width).astype(jnp.bfloat16), column, 1
        )
        log_sums = lax.dynamic_update_slice_in_dim(
            log_sums, (row_max + jnp.log(row_total))[:, :, 0], 2 * group_index, 0
        )
        return (result, log_sums)

    initial = (
        jnp.zeros((row_count, queries.shape[1]), jnp.bfloat16),
        jnp.zeros((2 * groups, row_count), jnp.float32),
    )
    return lax.fori_loop(0, groups, per_group, initial)


def attend_backward(queries, key_rows, value_rows, allowed, log_sums, grad_mix):
    row_count = queries.shape[0]
    pair_width = 2 * HEAD_DIM
    groups = queries.shape[1] // pair_width
    scaling = HEAD_DIM ** (-0.5)

    def per_group(group_index, running):
        grad_queries, grad_keys, grad_values = running
        column = group_index * pair_width
        query_pair = head_slices(queries, column, pair_width)
        key_pair = head_slices(key_rows, column, pair_width)
        value_pair = head_slices(value_rows, column, pair_width)
        grad_pair = head_slices(grad_mix, column, pair_width)
        pair_sums = lax.dynamic_slice_in_dim(log_sums, 2 * group_index, 2, 0)
        scores = (
            jnp.einsum("qhe,khe->hqk", query_pair, key_pair, preferred_element_type=jnp.float32)
            * scaling
        )
        scores = jnp.where(allowed, scores, NEGATIVE)
        softmax_out = jnp.exp(scores - pair_sums[:, :, None])
        grad_value_pair = jnp.einsum(
            "hqk,qhe->khe",
            softmax_out.astype(jnp.bfloat16),
            grad_pair,
            preferred_element_type=jnp.float32,
        )
        grad_probs = jnp.einsum(
            "qhe,khe->hqk", grad_pair, value_pair, preferred_element_type=jnp.float32
        )
        inner_sum = jnp.sum(softmax_out * grad_probs, axis=2, keepdims=True)
        grad_scores = (softmax_out * (grad_probs - inner_sum)).astype(jnp.bfloat16)
        grad_query_pair = (
            jnp.einsum("hqk,khe->qhe", grad_scores, key_pair, preferred_element_type=jnp.float32)
            * scaling
        )
        grad_key_pair = (
            jnp.einsum("hqk,qhe->khe", grad_scores, query_pair, preferred_element_type=jnp.float32)
            * scaling
        )
        grad_queries = lax.dynamic_update_slice_in_dim(
            grad_queries,
            grad_query_pair.reshape(row_count, pair_width).astype(jnp.bfloat16),
            column,
            1,
        )
        grad_keys = lax.dynamic_update_slice_in_dim(
            grad_keys,
            grad_key_pair.reshape(key_rows.shape[0], pair_width).astype(jnp.bfloat16),
            column,
            1,
        )
        grad_values = lax.dynamic_update_slice_in_dim(
            grad_values,
            grad_value_pair.reshape(key_rows.shape[0], pair_width).astype(jnp.bfloat16),
            column,
            1,
        )
        return (grad_queries, grad_keys, grad_values)

    initial = (
        jnp.zeros(queries.shape, jnp.bfloat16),
        jnp.zeros(key_rows.shape, jnp.bfloat16),
        jnp.zeros(value_rows.shape, jnp.bfloat16),
    )
    return lax.fori_loop(0, groups, per_group, initial)


def on_device(
    image_tokens,
    text_states,
    text_segments,
    image_segment,
    out_grad,
    norm1_gain,
    norm1_bias,
    self_query,
    self_key,
    self_value,
    self_output,
    norm2_gain,
    norm2_bias,
    cross_query,
    cross_key,
    cross_value,
    cross_output,
    norm3_gain,
    norm3_bias,
    mlp_in,
    mlp_in_bias,
    mlp_out,
    mlp_out_bias,
):
    tokens = image_tokens[0].astype(jnp.float32)
    row_count = tokens.shape[0]
    vectors = (
        norm1_gain,
        norm1_bias,
        norm2_gain,
        norm2_bias,
        norm3_gain,
        norm3_bias,
        mlp_in_bias,
        mlp_out_bias,
    )
    sizes = [v.shape[0] for v in vectors]
    shard = self_query.shape[0]
    wide_parts = mlp_in.shape[1] // 1024
    first = gather_rows(
        jnp.concatenate([self_query, self_key, self_value, pack_vectors(vectors)], axis=0)
    )
    second = gather_rows(
        jnp.concatenate(
            [self_output, cross_query, cross_key, cross_value, cross_output]
            + [mlp_in[:, 1024 * k : 1024 * (k + 1)] for k in range(wide_parts)]
            + [mlp_out],
            axis=0,
        )
    )

    def matrix(source, index):
        return source[:, shard * index : shard * (index + 1)].reshape(-1, 1024)

    w_query, w_key, w_value = (matrix(first, k) for k in range(3))
    gain_one, bias_one, gain_two, bias_two, gain_three, bias_three, up_bias, down_bias = (
        take_vectors(first[:, 3 * shard :], sizes)
    )
    w_output, c_query, c_key, c_value, c_output = (matrix(second, k) for k in range(5))
    up_matrix = jnp.concatenate([matrix(second, 5 + k) for k in range(wide_parts)], axis=1)
    down_matrix = second[:, (5 + wide_parts) * shard :].reshape(-1, 1024)

    own_text = text_states[0]
    slots = own_text.shape[0]
    text_full = jnp.concatenate(
        [own_text] + [swap_narrow(own_text, k) for k in text_partners()], axis=0
    )
    narrow_at = lax.axis_index("narrow")
    segments = jnp.concatenate(
        [
            lax.dynamic_slice_in_dim(text_segments[0], (narrow_at ^ k) * slots, slots, 0)
            for k in range(lax.axis_size("narrow"))
        ]
    )
    matches = (segments == image_segment[0, 0])[None, None, :]

    normed_one = layer_norm(tokens, gain_one, bias_one).astype(jnp.bfloat16)
    queries = matmul(normed_one, w_query).astype(jnp.bfloat16)
    key_rows = matmul(normed_one, w_key).astype(jnp.bfloat16)
    value_rows = matmul(normed_one, w_value).astype(jnp.bfloat16)
    row_pos = lax.broadcasted_iota(jnp.int32, (row_count, row_count), 0)
    column_pos = lax.broadcasted_iota(jnp.int32, (row_count, row_count), 1)
    causal = (row_pos >= column_pos)[None]
    mixed_self, sums_self = attend_forward(queries, key_rows, value_rows, causal)
    after_self = tokens + matmul(mixed_self, w_output)
    normed_two = layer_norm(after_self, gain_two, bias_two).astype(jnp.bfloat16)
    cross_queries = matmul(normed_two, c_query).astype(jnp.bfloat16)
    cross_keys = matmul(text_full, c_key).astype(jnp.bfloat16)
    cross_values = matmul(text_full, c_value).astype(jnp.bfloat16)
    mixed_cross, sums_cross = attend_forward(cross_queries, cross_keys, cross_values, matches)
    after_cross = after_self + matmul(mixed_cross, c_output)
    normed_three = layer_norm(after_cross, gain_three, bias_three).astype(jnp.bfloat16)
    hidden_pre = matmul(normed_three, up_matrix) + up_bias
    hidden_act, gelu_pull = jax.vjp(exact_gelu, hidden_pre)
    hidden = hidden_act.astype(jnp.bfloat16)
    block_out = after_cross + matmul(hidden, down_matrix) + down_bias
    grad_out = out_grad[0]
    grad_tail = grad_out.astype(jnp.float32)
    grad_down = scatter_sum(matmul_tn(hidden, grad_out).astype(jnp.bfloat16), 0)
    grad_down_bias = jnp.sum(grad_tail, axis=0)
    grad_hidden = matmul_nt(grad_out, down_matrix)
    grad_pre = gelu_pull(grad_hidden)[0].astype(jnp.bfloat16)
    grad_up = scatter_sum(matmul_tn(normed_three, grad_pre).astype(jnp.bfloat16), 1)
    grad_up_bias = jnp.sum(grad_pre.astype(jnp.float32), axis=0)
    grad_normed = matmul_nt(grad_pre, up_matrix)
    unused_three, norm_pull = jax.vjp(layer_norm, after_cross, gain_three, bias_three)
    grad_middle, grad_gain_three, grad_bias_three = norm_pull(grad_normed)
    grad_after_cross = grad_tail + grad_middle
    grad_mix_out = grad_after_cross.astype(jnp.bfloat16)
    grad_cross_out = scatter_sum(matmul_tn(mixed_cross, grad_mix_out).astype(jnp.bfloat16), 2)
    grad_mixed = matmul_nt(grad_mix_out, c_output).astype(jnp.bfloat16)
    query_grad_two, key_grad_two, value_grad_two = attend_backward(
        cross_queries, cross_keys, cross_values, matches, sums_cross, grad_mixed
    )
    grad_cross_query = scatter_sum(matmul_tn(normed_two, query_grad_two).astype(jnp.bfloat16), 2)
    grad_normed = matmul_nt(query_grad_two, c_query)
    grad_cross_key = scatter_sum(matmul_tn(text_full, key_grad_two).astype(jnp.bfloat16), 0)
    grad_cross_value = scatter_sum(matmul_tn(text_full, value_grad_two).astype(jnp.bfloat16), 1)
    text_term = matmul_nt(key_grad_two, c_key) + matmul_nt(value_grad_two, c_value)
    text_grad = text_term[:slots]
    for k in text_partners():
        text_grad = text_grad + swap_narrow(text_term[k * slots : (k + 1) * slots], k)
    unused_two, norm_pull = jax.vjp(layer_norm, after_self, gain_two, bias_two)
    grad_middle, grad_gain_two, grad_bias_two = norm_pull(grad_normed)
    grad_after_self = grad_after_cross + grad_middle
    grad_self_mix = grad_after_self.astype(jnp.bfloat16)
    grad_self_out = scatter_sum(matmul_tn(mixed_self, grad_self_mix).astype(jnp.bfloat16), 2)
    grad_mixed = matmul_nt(grad_self_mix, w_output).astype(jnp.bfloat16)
    query_grad_one, key_grad_one, value_grad_one = attend_backward(
        queries, key_rows, value_rows, causal, sums_self, grad_mixed
    )
    grad_self_query = scatter_sum(matmul_tn(normed_one, query_grad_one).astype(jnp.bfloat16), 0)
    grad_self_key = scatter_sum(matmul_tn(normed_one, key_grad_one).astype(jnp.bfloat16), 1)
    grad_self_value = scatter_sum(matmul_tn(normed_one, value_grad_one).astype(jnp.bfloat16), 2)
    grad_normed = (
        matmul_nt(query_grad_one, w_query)
        + matmul_nt(key_grad_one, w_key)
        + matmul_nt(value_grad_one, w_value)
    )
    unused_one, norm_pull = jax.vjp(layer_norm, tokens, gain_one, bias_one)
    grad_middle, grad_gain_one, grad_bias_one = norm_pull(grad_normed)
    image_grad = grad_after_self + grad_middle
    vector_terms = (
        grad_gain_one,
        grad_bias_one,
        grad_gain_two,
        grad_bias_two,
        grad_gain_three,
        grad_bias_three,
        grad_up_bias,
        grad_down_bias,
    )
    owners = lax.axis_size("wide") * lax.axis_size("narrow")
    stacked = jnp.concatenate([v.reshape(owners, -1) for v in vector_terms], axis=1)
    width = stacked.shape[1]
    stacked = jnp.pad(stacked, ((0, 0), (0, -width % 1024))).reshape(owners, -1, 128)
    summed = scatter_sum(stacked, 0, jnp.float32).reshape(-1)
    vector_grads, at = [], 0
    for size in sizes:
        vector_grads.append(summed[at : at + size])
        at += size
    return (
        block_out.astype(jnp.bfloat16)[None],
        image_grad[None],
        text_grad[None],
        vector_grads[0],
        vector_grads[1],
        grad_self_query,
        grad_self_key,
        grad_self_value,
        grad_self_out,
        vector_grads[2],
        vector_grads[3],
        grad_cross_query,
        grad_cross_key,
        grad_cross_value,
        grad_cross_out,
        vector_grads[4],
        vector_grads[5],
        grad_up,
        vector_grads[6],
        grad_down,
        vector_grads[7],
    )


def solution(mesh):
    placed = (
        P(("wide", "narrow"), None, None),
        P("wide", "narrow", None),
        P("wide", None),
        P("wide", "narrow"),
        P(("wide", "narrow"), None, None),
        P(("wide", "narrow")),
        P(("wide", "narrow")),
        P(("wide", "narrow"), None),
        P(("wide", "narrow"), None),
        P(("wide", "narrow"), None),
        P(("wide", "narrow"), None),
        P(("wide", "narrow")),
        P(("wide", "narrow")),
        P(("wide", "narrow"), None),
        P(("wide", "narrow"), None),
        P(("wide", "narrow"), None),
        P(("wide", "narrow"), None),
        P(("wide", "narrow")),
        P(("wide", "narrow")),
        P(("wide", "narrow"), None),
        P(("wide", "narrow")),
        P(("wide", "narrow"), None),
        P(("wide", "narrow")),
    )
    return jax.shard_map(
        on_device,
        mesh=mesh,
        in_specs=placed,
        out_specs=(
            P(("wide", "narrow"), None, None),
            P(("wide", "narrow"), None, None),
            P("wide", "narrow", None),
            P(("wide", "narrow")),
            P(("wide", "narrow")),
            P(("wide", "narrow"), None),
            P(("wide", "narrow"), None),
            P(("wide", "narrow"), None),
            P(("wide", "narrow"), None),
            P(("wide", "narrow")),
            P(("wide", "narrow")),
            P(("wide", "narrow"), None),
            P(("wide", "narrow"), None),
            P(("wide", "narrow"), None),
            P(("wide", "narrow"), None),
            P(("wide", "narrow")),
            P(("wide", "narrow")),
            P(("wide", "narrow"), None),
            P(("wide", "narrow")),
            P(("wide", "narrow"), None),
            P(("wide", "narrow")),
        ),
        check_vma=False,
    )
```

```python
import functools
import math

import jax
import jax.numpy as jnp
from jax import lax
from jax.experimental import pallas as pl
from jax.experimental.pallas import tpu as pltpu
from jax.sharding import PartitionSpec as P

HEAD_DIM = 64
TILE = 256
BF16 = jnp.bfloat16
VMEM_LIMIT = 60 * 1024 * 1024

EPSILON = 1e-05
NEGATIVE = -1e30

AXES = ("wide", "narrow")


def axis_bits(axis):
    return lax.axis_size(axis).bit_length() - 1


def halving_order(kind):
    wide = [("wide", k) for k in range(1, axis_bits("wide"))]
    narrow = [("narrow", k) for k in range(axis_bits("narrow"))]
    core = [("wide", 0)]
    if kind == 0:
        return core + narrow + wide
    if kind == 1:
        return core + narrow[1:] + wide[:1] + narrow[:1] + wide[1:]
    return core + wide[:1] + narrow + wide[1:]


def gather_rows(packed):
    whole = lax.all_gather(packed, AXES, axis=0, tiled=True)
    return whole.reshape((-1,) + packed.shape)


def pack_vectors(vectors):
    flat = jnp.concatenate(vectors)
    room = -flat.shape[0] % (16 * 1024)
    return jnp.pad(flat, (0, room)).reshape(-1, 1024)


def take_vectors(rows, sizes):
    flat = rows.reshape(rows.shape[0], -1)
    out, at = [], 0
    for size in sizes:
        out.append(flat[:, at : at + size].reshape(1, -1).astype(jnp.float32))
        at += size
    return out


def text_partners():
    return range(1, lax.axis_size("narrow"))


def swap_narrow(block, offset):
    count = lax.axis_size("narrow")
    return lax.ppermute(block, "narrow", [(i, i ^ offset) for i in range(count)])


def nn(a, b):
    return lax.dot_general(a, b, (((1,), (0,)), ((), ())), preferred_element_type=jnp.float32)


def nt(a, b):
    return lax.dot_general(a, b, (((1,), (1,)), ((), ())), preferred_element_type=jnp.float32)


def tn(a, b):
    return lax.dot_general(a, b, (((0,), (0,)), ((), ())), preferred_element_type=jnp.float32)


def standardize(values):
    center = jnp.mean(values, axis=-1, keepdims=True)
    offset = values - center
    rate = lax.rsqrt(jnp.mean(offset * offset, axis=-1, keepdims=True) + EPSILON)
    return offset * rate, rate


def norm_back(standard, rate, gain, grad):
    scaled = grad * gain
    return rate * (
        scaled
        - jnp.mean(scaled, axis=-1, keepdims=True)
        - standard * jnp.mean(scaled * standard, axis=-1, keepdims=True)
    )


def column_sum(values):
    return jnp.sum(values, axis=0, keepdims=True)


def square(ref):
    return ref[...].reshape(-1, ref.shape[-1])


def head_lanes(block, head):
    lane = lax.broadcasted_iota(jnp.int32, block.shape, 1)
    inside = (lane >= HEAD_DIM) if head else (lane < HEAD_DIM)
    return jnp.where(inside, block, jnp.zeros_like(block))


def whole_block(shape):
    zeros = (0,) * len(shape)
    return pl.BlockSpec(shape, lambda *_: zeros, pipeline_mode=pl.Buffered(1))


def params(**extra):
    return pltpu.CompilerParams(vmem_limit_bytes=VMEM_LIMIT, **extra)


def project_kernel(x_ref, gain_ref, bias_ref, wq_ref, wk_ref, wv_ref, h_ref, q_ref, k_ref, v_ref):
    standard, _ = standardize(x_ref[...].astype(jnp.float32))
    normed = (standard * gain_ref[...] + bias_ref[...]).astype(BF16)
    h_ref[...] = normed
    q_ref[...] = nn(normed, square(wq_ref)).astype(BF16)
    k_ref[...] = nn(normed, square(wk_ref)).astype(BF16)
    v_ref[...] = nn(normed, square(wv_ref)).astype(BF16)


def project(tokens, gain, bias, weights):
    rows, width = tokens.shape
    tile = pl.BlockSpec((TILE, width), lambda i: (i, 0))
    arrays, specs = zip(*weights)
    return pl.pallas_call(
        project_kernel,
        grid=(rows // TILE,),
        in_specs=[tile, whole_block(gain.shape), whole_block(bias.shape), *specs],
        out_specs=[tile] * 4,
        out_shape=[jax.ShapeDtypeStruct(tokens.shape, BF16)] * 4,
        compiler_params=params(),
        cost_estimate=pl.CostEstimate(
            flops=6 * rows * width * width, bytes_accessed=16 * width * width, transcendentals=0
        ),
        name="self_project",
    )(tokens, gain, bias, *arrays)


def attend_kernel(q_ref, k_ref, v_ref, o_ref, sums_ref):
    rows, width = q_ref.shape
    flipped = v_ref[...].T
    for start in range(0, rows, TILE):
        span = start + TILE
        queries = q_ref[start:span, :] * (HEAD_DIM**-0.5)
        keys = k_ref[:span, :]
        mixed, sums = [], []
        for head in range(2):
            scores = nt(keys, head_lanes(queries, head))
            key_at = lax.broadcasted_iota(jnp.int32, (TILE, TILE), 0)
            query_at = lax.broadcasted_iota(jnp.int32, (TILE, TILE), 1)
            corner = jnp.where(key_at <= query_at, scores[start:], NEGATIVE)
            scores = jnp.concatenate([scores[:start], corner], axis=0) if start else corner
            top = jnp.max(scores, axis=0, keepdims=True)
            powers = jnp.exp(scores - top)
            total = jnp.sum(powers, axis=0, keepdims=True)
            part = nn(flipped[HEAD_DIM * head : HEAD_DIM * (head + 1), :span], powers.astype(BF16))
            mixed.append(part * (1.0 / total))
            sums.append(top + jnp.log(total))
        o_ref[start:span, :] = jnp.concatenate(mixed, axis=0).T.astype(BF16)
        sums_ref[0, :, start:span] = jnp.concatenate(sums, axis=0)


def attend(queries, keys, values):
    rows, width = queries.shape
    pairs = width // 128
    block = pl.BlockSpec((rows, 128), lambda p: (0, p))
    return pl.pallas_call(
        attend_kernel,
        grid=(pairs,),
        in_specs=[block] * 3,
        out_specs=[block, pl.BlockSpec((1, 2, rows), lambda p: (p, 0, 0))],
        out_shape=[
            jax.ShapeDtypeStruct(queries.shape, BF16),
            jax.ShapeDtypeStruct((pairs, 2, rows), jnp.float32),
        ],
        compiler_params=params(),
        cost_estimate=pl.CostEstimate(
            flops=24 * rows * rows * width,
            bytes_accessed=8 * rows * width,
            transcendentals=rows * rows * 16,
        ),
        name="self_attend",
    )(queries, keys, values)


def attend_back_kernel(q_ref, k_ref, v_ref, da_ref, sums_ref, dq_ref, dk_ref, dv_ref, dk_sum, dv_sum):
    rows, width = q_ref.shape
    flipped = k_ref[...].T
    for start in reversed(range(0, rows, TILE)):
        span = start + TILE
        queries = q_ref[start:span, :] * (HEAD_DIM**-0.5)
        grads = da_ref[start:span, :]
        keys = k_ref[:span, :]
        values = v_ref[:span, :]
        parts = []
        for head in range(2):
            own_queries = head_lanes(queries, head)
            own_grads = head_lanes(grads, head)
            scores = nt(keys, own_queries)
            key_at = lax.broadcasted_iota(jnp.int32, (TILE, TILE), 0)
            query_at = lax.broadcasted_iota(jnp.int32, (TILE, TILE), 1)
            corner = jnp.where(key_at <= query_at, scores[start:], NEGATIVE)
            scores = jnp.concatenate([scores[:start], corner], axis=0) if start else corner
            probs = jnp.exp(scores - sums_ref[0, head : head + 1, start:span])
            grad_probs = nt(values, own_grads)
            inner = jnp.sum(probs * grad_probs, axis=0, keepdims=True)
            grad_scores = (probs * (grad_probs - inner)).astype(BF16)
            value_term = nn(probs.astype(BF16), own_grads)
            key_term = nn(grad_scores, own_queries)
            if span == rows and head == 0:
                dv_sum[...] = value_term
                dk_sum[...] = key_term
            else:
                dv_sum[:span, :] += value_term
                dk_sum[:span, :] += key_term
            parts.append(nn(flipped[HEAD_DIM * head : HEAD_DIM * (head + 1), :span], grad_scores))
        dq = jnp.concatenate(parts, axis=0).T * (HEAD_DIM**-0.5)
        dq_ref[start:span, :] = dq.astype(BF16)
    dk_ref[...] = dk_sum[...].astype(BF16)
    dv_ref[...] = dv_sum[...].astype(BF16)


def attend_back(queries, keys, values, grads, sums, first, count):
    rows = queries.shape[0]
    block = pl.BlockSpec((rows, 128), lambda p: (0, p + first))
    out = pl.BlockSpec((rows, 128), lambda p: (0, p))
    return pl.pallas_call(
        attend_back_kernel,
        grid=(count,),
        in_specs=[block] * 4 + [pl.BlockSpec((1, 2, rows), lambda p: (p + first, 0, 0))],
        out_specs=[out] * 3,
        out_shape=[jax.ShapeDtypeStruct((rows, 128 * count), BF16)] * 3,
        scratch_shapes=[pltpu.VMEM((rows, 128), jnp.float32)] * 2,
        compiler_params=params(),
        cost_estimate=pl.CostEstimate(
            flops=48 * rows * rows * 128 * count,
            bytes_accessed=14 * rows * 128 * count,
            transcendentals=rows * rows * 2 * count,
        ),
        name="self_attend_back",
    )(queries, keys, values, grads, sums)


def gelu_both(values):
    phi = 0.5 + 0.5 * lax.erf(values * (0.5**0.5))
    density = jnp.exp(-0.5 * values * values) * ((2.0 * math.pi) ** -0.5)
    return values * phi, phi + values * density


def mlp_kernel(
    x_ref, h_ref, g_ref, gain_ref, up_ref, ub_ref, down_ref, db_ref,
    out_ref, dx_ref, dup_ref, dub_ref, ddown_ref, dgain_ref, dbias_ref, gsum_ref,
    out_sum, dh_sum, h_flip, act, grad_act,
):
    step, steps = pl.program_id(0), pl.num_programs(0)
    rows = h_ref.shape[0]

    @pl.when(step == 0)
    def _():
        h_flip[...] = h_ref[...].T
        out_sum[...] = x_ref[...] + db_ref[...]
        dh_sum[...] = jnp.zeros_like(dh_sum)

    up = square(up_ref)
    down = square(down_ref)
    bias_sum = jnp.zeros_like(dub_ref)
    for start in range(0, rows, TILE):
        at = slice(start, start + TILE)
        hidden, slope = gelu_both(nn(h_ref[at, :], up) + ub_ref[...])
        act[at, :] = hidden.astype(BF16)
        grad_pre = (nt(g_ref[at, :], down) * slope).astype(BF16)
        grad_act[at, :] = grad_pre
        bias_sum += column_sum(grad_pre.astype(jnp.float32))
        out_sum[at, :] += nn(act[at, :], down)
        dh_sum[at, :] += nt(grad_pre, up)
    dub_ref[...] = bias_sum
    dup_ref[...] = nn(h_flip[...], grad_act[...]).astype(BF16)
    ddown_ref[...] = tn(act[...], g_ref[...]).astype(BF16)

    @pl.when(step == steps - 1)
    def _():
        gain_sum = jnp.zeros_like(dgain_ref)
        grad_sum = jnp.zeros_like(dbias_ref)
        tail_sum = jnp.zeros_like(gsum_ref)
        for start in range(0, rows, TILE):
            at = slice(start, start + TILE)
            out_ref[at, :] = out_sum[at, :].astype(BF16)
            standard, rate = standardize(x_ref[at, :])
            grad = dh_sum[at, :]
            tail = g_ref[at, :].astype(jnp.float32)
            dx_ref[at, :] = tail + norm_back(standard, rate, gain_ref[...], grad)
            gain_sum += column_sum(grad * standard)
            grad_sum += column_sum(grad)
            tail_sum += column_sum(tail)
        dgain_ref[...] = gain_sum
        dbias_ref[...] = grad_sum
        gsum_ref[...] = tail_sum


def mlp(x, h, g, gain, up, up_bias, down, down_bias, chunk):
    rows, width = x.shape
    hidden = up_bias.shape[1]
    f32 = jnp.float32
    row = (1, width)
    return pl.pallas_call(
        mlp_kernel,
        grid=(hidden // chunk,),
        in_specs=[
            whole_block(x.shape), whole_block(h.shape), whole_block(g.shape), whole_block(row),
            up[1], pl.BlockSpec((1, chunk), lambda c: (0, c)), down[1], whole_block(row),
        ],
        out_specs=[
            whole_block(x.shape), whole_block(x.shape),
            pl.BlockSpec((width, chunk), lambda c: (0, c)),
            pl.BlockSpec((1, chunk), lambda c: (0, c)),
            pl.BlockSpec((chunk, width), lambda c: (c, 0)),
            whole_block(row), whole_block(row), whole_block(row),
        ],
        out_shape=[
            jax.ShapeDtypeStruct(x.shape, BF16), jax.ShapeDtypeStruct(x.shape, f32),
            jax.ShapeDtypeStruct((width, hidden), BF16),
            jax.ShapeDtypeStruct((1, hidden), f32),
            jax.ShapeDtypeStruct((hidden, width), BF16),
            jax.ShapeDtypeStruct(row, f32), jax.ShapeDtypeStruct(row, f32), jax.ShapeDtypeStruct(row, f32),
        ],
        scratch_shapes=[
            pltpu.VMEM(x.shape, f32), pltpu.VMEM(x.shape, f32), pltpu.VMEM((width, rows), BF16),
            pltpu.VMEM((rows, chunk), BF16), pltpu.VMEM((rows, chunk), BF16),
        ],
        compiler_params=params(),
        cost_estimate=pl.CostEstimate(
            flops=12 * rows * width * hidden,
            bytes_accessed=8 * width * hidden + 14 * rows * width,
            transcendentals=2 * rows * hidden,
        ),
        name="mlp_both_ways",
    )(x, h, g, gain, up[0], up_bias, down[0], down_bias)


def caption_probs(keys, own_queries, mask):
    scores = jnp.where(mask != 0, nt(keys, own_queries), NEGATIVE)
    powers = jnp.exp(scores - jnp.max(scores, axis=0, keepdims=True))
    return powers * (1.0 / jnp.sum(powers, axis=0, keepdims=True))


def middle_kernel(
    x_ref, a_ref, text_ref, mask_ref, gain2_ref, bias2_ref, gain3_ref, bias3_ref,
    wo_ref, cq_ref, ck_ref, cv_ref, co_ref,
    x1_ref, h2_ref, q2_ref, a2_ref, x2_ref, h3_ref, k2_ref, v2_ref,
):
    @pl.when(pl.program_id(0) == 0)
    def _():
        k2_ref[...] = nn(text_ref[...], square(ck_ref)).astype(BF16)
        v2_ref[...] = nn(text_ref[...], square(cv_ref)).astype(BF16)

    after_self = x_ref[...].astype(jnp.float32) + nn(a_ref[...], square(wo_ref))
    x1_ref[...] = after_self
    standard, _ = standardize(after_self)
    normed = (standard * gain2_ref[...] + bias2_ref[...]).astype(BF16)
    h2_ref[...] = normed
    q2_ref[...] = nn(normed, square(cq_ref)).astype(BF16)
    mask = mask_ref[...]
    for pair in range(q2_ref.shape[1] // 128):
        at = slice(128 * pair, 128 * (pair + 1))
        queries = q2_ref[:, at] * (HEAD_DIM**-0.5)
        keys = k2_ref[:, at]
        flipped = v2_ref[:, at].T
        mixed = []
        for head in range(2):
            probs = caption_probs(keys, head_lanes(queries, head), mask).astype(BF16)
            mixed.append(nn(flipped[HEAD_DIM * head : HEAD_DIM * (head + 1)], probs))
        a2_ref[:, at] = jnp.concatenate(mixed, axis=0).T.astype(BF16)
    after_cross = after_self + nn(a2_ref[...], square(co_ref))
    x2_ref[...] = after_cross
    standard, _ = standardize(after_cross)
    h3_ref[...] = (standard * gain3_ref[...] + bias3_ref[...]).astype(BF16)


def middle(tokens, mixed, text, mask, vectors, weights):
    rows, width = tokens.shape
    slots = text.shape[0]
    tile = pl.BlockSpec((TILE, width), lambda i: (i, 0))
    arrays, specs = zip(*weights)
    f32 = jnp.float32
    like = lambda dtype: jax.ShapeDtypeStruct(tokens.shape, dtype)
    return pl.pallas_call(
        middle_kernel,
        grid=(rows // TILE,),
        in_specs=[
            tile, tile, whole_block(text.shape), whole_block(mask.shape),
            *[whole_block(v.shape) for v in vectors], *specs,
        ],
        out_specs=[tile] * 6 + [whole_block(text.shape)] * 2,
        out_shape=[like(f32), like(BF16), like(BF16), like(BF16), like(f32), like(BF16)]
        + [jax.ShapeDtypeStruct(text.shape, BF16)] * 2,
        compiler_params=params(),
        cost_estimate=pl.CostEstimate(
            flops=6 * rows * width * width + 16 * rows * slots * width,
            bytes_accessed=28 * rows * width,
            transcendentals=16 * rows * slots,
        ),
        name="output_and_cross",
    )(tokens, mixed, text, mask, *vectors, *arrays)


def middle_back_kernel(
    dx2_ref, x1_ref, a1_ref, h2_ref, q2_ref, a2_ref, k2_ref, v2_ref, text_ref, mask_ref, gain2_ref,
    wo_ref, cq_ref, ck_ref, cv_ref, co_ref,
    dx1_ref, da1_ref, dwo_ref, dcq_ref, dck_ref, dcv_ref, dco_ref, dtext_ref, dgain_ref, dbias_ref,
    wo_sum, cq_sum, co_sum, dk_sum, dv_sum, dq2,
):
    step, steps = pl.program_id(0), pl.num_programs(0)

    @pl.when(step == 0)
    def _():
        for ref in (wo_sum, cq_sum, co_sum, dk_sum, dv_sum, dgain_ref, dbias_ref):
            ref[...] = jnp.zeros_like(ref)

    grad_out = dx2_ref[...].astype(BF16)
    co_sum[...] += tn(a2_ref[...], grad_out)
    grad_mixed = nt(grad_out, square(co_ref)).astype(BF16)
    mask = mask_ref[...]
    for pair in range(q2_ref.shape[1] // 128):
        at = slice(128 * pair, 128 * (pair + 1))
        queries = q2_ref[:, at] * (HEAD_DIM**-0.5)
        keys = k2_ref[:, at]
        flipped = keys.T
        values = v2_ref[:, at]
        grads = grad_mixed[:, at]
        parts = []
        for head in range(2):
            own_queries = head_lanes(queries, head)
            own_grads = head_lanes(grads, head)
            probs = caption_probs(keys, own_queries, mask)
            grad_probs = nt(values, own_grads)
            inner = jnp.sum(probs * grad_probs, axis=0, keepdims=True)
            grad_scores = (probs * (grad_probs - inner)).astype(BF16)
            dv_sum[:, at] += nn(probs.astype(BF16), own_grads)
            dk_sum[:, at] += nn(grad_scores, own_queries)
            parts.append(nn(flipped[HEAD_DIM * head : HEAD_DIM * (head + 1)], grad_scores))
        dq2[:, at] = (jnp.concatenate(parts, axis=0).T * (HEAD_DIM**-0.5)).astype(BF16)
    cq_sum[...] += tn(h2_ref[...], dq2[...])
    grad_normed = nt(dq2[...], square(cq_ref))
    standard, rate = standardize(x1_ref[...])
    grad_after = dx2_ref[...] + norm_back(standard, rate, gain2_ref[...], grad_normed)
    dgain_ref[...] += column_sum(grad_normed * standard)
    dbias_ref[...] += column_sum(grad_normed)
    dx1_ref[...] = grad_after
    grad_self = grad_after.astype(BF16)
    wo_sum[...] += tn(a1_ref[...], grad_self)
    da1_ref[...] = nt(grad_self, square(wo_ref)).astype(BF16)

    @pl.when(step == steps - 1)
    def _():
        dwo_ref[...] = wo_sum[...].astype(BF16)
        dcq_ref[...] = cq_sum[...].astype(BF16)
        dco_ref[...] = co_sum[...].astype(BF16)
        grad_keys = dk_sum[...].astype(BF16)
        grad_values = dv_sum[...].astype(BF16)
        dck_ref[...] = tn(text_ref[...], grad_keys).astype(BF16)
        dcv_ref[...] = tn(text_ref[...], grad_values).astype(BF16)
        dtext_ref[...] = nt(grad_keys, square(ck_ref)) + nt(grad_values, square(cv_ref))


def middle_back(dx2, x1, a1, h2, q2, a2, k2, v2, text, mask, gain, weights):
    rows, width = x1.shape
    slots = text.shape[0]
    tile = pl.BlockSpec((TILE, width), lambda i: (i, 0))
    arrays, specs = zip(*weights)
    f32 = jnp.float32
    matrix = (width, width)
    return pl.pallas_call(
        middle_back_kernel,
        grid=(rows // TILE,),
        in_specs=[tile] * 6
        + [whole_block(v.shape) for v in (k2, v2, text, mask, gain)]
        + list(specs),
        out_specs=[tile] * 2
        + [whole_block(matrix)] * 5
        + [whole_block(text.shape)]
        + [whole_block(gain.shape)] * 2,
        out_shape=[jax.ShapeDtypeStruct(x1.shape, f32), jax.ShapeDtypeStruct(x1.shape, BF16)]
        + [jax.ShapeDtypeStruct(matrix, BF16)] * 5
        + [jax.ShapeDtypeStruct(text.shape, f32)]
        + [jax.ShapeDtypeStruct(gain.shape, f32)] * 2,
        scratch_shapes=[pltpu.VMEM(matrix, f32)] * 3
        + [pltpu.VMEM(text.shape, f32)] * 2
        + [pltpu.VMEM((TILE, width), BF16)],
        compiler_params=params(),
        cost_estimate=pl.CostEstimate(
            flops=12 * rows * width * width + 8 * slots * width * width,
            bytes_accessed=40 * rows * width,
            transcendentals=16 * rows * slots,
        ),
        name="cross_back",
    )(dx2, x1, a1, h2, q2, a2, k2, v2, text, mask, gain, *arrays)


def weight_grads_kernel(h_ref, dq_ref, dk_ref, dv_ref, q_ref, k_ref, v_ref):
    normed = h_ref[...]
    q_ref[...] = tn(normed, dq_ref[...]).astype(BF16)
    k_ref[...] = tn(normed, dk_ref[...]).astype(BF16)
    v_ref[...] = tn(normed, dv_ref[...]).astype(BF16)


def weight_grads(normed, grads):
    rows, width = normed.shape
    columns = grads[0].shape[1]
    out = pl.BlockSpec((TILE, columns), lambda i: (i, 0))
    return pl.pallas_call(
        weight_grads_kernel,
        grid=(width // TILE,),
        in_specs=[pl.BlockSpec((rows, TILE), lambda i: (0, i))]
        + [whole_block(g.shape) for g in grads],
        out_specs=[out] * 3,
        out_shape=[jax.ShapeDtypeStruct((width, columns), BF16)] * 3,
        compiler_params=params(),
        cost_estimate=pl.CostEstimate(
            flops=6 * rows * width * columns, bytes_accessed=14 * rows * width, transcendentals=0
        ),
        name="self_weight_grads",
    )(normed, *grads)


def first_back_kernel(x_ref, dx1_ref, gain_ref, wq_ref, wk_ref, wv_ref, *rest):
    grads, (dx_ref, dgain_ref, dbias_ref) = rest[:-3], rest[-3:]

    @pl.when(pl.program_id(0) == 0)
    def _():
        dgain_ref[...] = jnp.zeros_like(dgain_ref)
        dbias_ref[...] = jnp.zeros_like(dbias_ref)

    grad_normed, at = None, 0
    for first in range(0, len(grads), 3):
        columns = grads[first].shape[1]
        for grad, weight in zip(grads[first : first + 3], (wq_ref, wk_ref, wv_ref)):
            term = nt(grad[...], square(weight)[:, at : at + columns])
            grad_normed = term if grad_normed is None else grad_normed + term
        at += columns
    standard, rate = standardize(x_ref[...].astype(jnp.float32))
    dx_ref[...] = dx1_ref[...] + norm_back(standard, rate, gain_ref[...], grad_normed)
    dgain_ref[...] += column_sum(grad_normed * standard)
    dbias_ref[...] += column_sum(grad_normed)


def first_back(tokens, dx1, gain, weights, grads):
    rows, width = tokens.shape
    tile = lambda columns: pl.BlockSpec((TILE, columns), lambda i: (i, 0))
    arrays, specs = zip(*weights)
    f32 = jnp.float32
    return pl.pallas_call(
        first_back_kernel,
        grid=(rows // TILE,),
        in_specs=[tile(width)] * 2
        + [whole_block(gain.shape)]
        + list(specs)
        + [tile(g.shape[1]) for g in grads],
        out_specs=[tile(width)] + [whole_block(gain.shape)] * 2,
        out_shape=[jax.ShapeDtypeStruct(tokens.shape, f32)]
        + [jax.ShapeDtypeStruct(gain.shape, f32)] * 2,
        compiler_params=params(),
        cost_estimate=pl.CostEstimate(
            flops=6 * rows * width * width, bytes_accessed=22 * rows * width, transcendentals=0
        ),
        name="self_norm_back",
    )(tokens, dx1, gain, *arrays, *grads)


def cube_dims():
    wide = [("wide", k) for k in reversed(range(axis_bits("wide")))]
    return wide + [("narrow", k) for k in reversed(range(axis_bits("narrow")))]


def my_bits(dims):
    return [(lax.axis_index(axis) >> bit) & 1 for axis, bit in dims]


def partner(axis, bit):
    return {axis: lax.axis_index(axis) ^ (1 << bit)}


def greet_partners(dims):
    barrier = pltpu.get_barrier_semaphore()
    for axis, bit in dims:
        pl.semaphore_signal(
            barrier, inc=1, device_id=partner(axis, bit), device_id_type=pl.DeviceIdType.MESH
        )
    pl.semaphore_wait(barrier, len(dims))


def skewed(plan, stages):
    slots = [(plan[p][2] + s, -s, p) for p in range(len(plan)) for s in range(stages)]
    return [(p, -minus) for _, minus, p in sorted(slots)]


def gather_kernel(dims, plan, src_ref, out_ref, send_sems, recv_sems, own_sem):
    mine = my_bits(dims)
    greet_partners(dims)
    own = pltpu.make_async_copy(src_ref, out_ref.at[tuple(mine)], own_sem)
    own.start()
    copies = {}
    for part, stage in skewed(plan, len(dims)):
        rows, order, _ = plan[part]
        if stage:
            copies[part, stage - 1].wait_recv()
        if stage == 1 and part == 0:
            own.wait()
        held = order[:stage]
        at = tuple(slice(None) if d in held else b for d, b in zip(dims, mine)) + (rows,)
        copy = pltpu.make_async_remote_copy(
            src_ref=out_ref.at[at] if stage else src_ref.at[rows],
            dst_ref=out_ref.at[at],
            send_sem=send_sems.at[part, stage],
            recv_sem=recv_sems.at[part, stage],
            device_id=partner(*order[stage]),
            device_id_type=pl.DeviceIdType.MESH,
        )
        copy.start()
        copies[part, stage] = copy
    for (part, stage), copy in copies.items():
        if stage == len(dims) - 1:
            copy.wait_recv()
        copy.wait_send()


SHARES = (2, 2, 1)


def split_rows(rows, shares, step=16):
    ends = [sum(shares[: k + 1]) for k in range(len(shares))]
    cuts = [0] + [(rows * e + ends[-1] * step // 2) // (ends[-1] * step) * step for e in ends]
    cuts[-1] = rows
    return [slice(a, b) for a, b in zip(cuts[:-1], cuts[1:])]


def gather_all(packed, collective_id, rounds):
    dims = cube_dims()
    rows, width = packed.shape
    shares = SHARES * rounds
    pieces = split_rows(rows, shares)
    plan = [(piece, halving_order(k % 3)[::-1], k // 3) for k, piece in enumerate(pieces)]
    out = pl.pallas_call(
        functools.partial(gather_kernel, dims, plan),
        in_specs=[pl.BlockSpec(memory_space=pl.ANY)],
        out_specs=pl.BlockSpec(memory_space=pl.ANY),
        out_shape=jax.ShapeDtypeStruct((2,) * len(dims) + packed.shape, packed.dtype),
        scratch_shapes=[
            pltpu.SemaphoreType.DMA((len(plan), len(dims))),
            pltpu.SemaphoreType.DMA((len(plan), len(dims))),
            pltpu.SemaphoreType.DMA,
        ],
        compiler_params=pltpu.CompilerParams(collective_id=collective_id, has_side_effects=True),
        name="gather_weights",
    )(packed)
    return out.reshape((-1,) + packed.shape)


def drop(items, index):
    return items[:index] + items[index + 1 :]


class Halving:
    def __init__(self, dims, orders, terms, kept, landed, outs, send_sems, recv_sems, kept_sems):
        self.dims, self.orders, self.terms = dims, orders, terms
        self.kept, self.landed, self.outs = kept, landed, outs
        self.send_sems, self.recv_sems, self.kept_sems = send_sems, recv_sems, kept_sems
        self.mine = dict(zip(dims, my_bits(dims)))

    def half(self, term, stage, other):
        order = self.orders[term]
        left = [d for d in self.dims if d not in order[:stage]]
        bit = self.mine[order[stage]]
        return tuple((1 - bit if other else bit) if d == order[stage] else slice(None) for d in left)

    def send(self, term, stage):
        source = self.terms[term] if stage == 0 else self.landed[term][stage - 1]
        return pltpu.make_async_remote_copy(
            src_ref=source.at[self.half(term, stage, True)],
            dst_ref=self.landed[term][stage],
            send_sem=self.send_sems.at[term, stage],
            recv_sem=self.recv_sems.at[term, stage],
            device_id=partner(*self.orders[term][stage]),
            device_id_type=pl.DeviceIdType.MESH,
        )

    def keep(self, term):
        source = self.terms[term].at[self.half(term, 0, False)]
        return pltpu.make_async_copy(source, self.kept[term], self.kept_sems.at[term])

    def start(self, stage, terms=None):
        for term in range(len(self.terms)) if terms is None else terms:
            self.send(term, stage).start()
            if stage == 0:
                self.keep(term).start()

    def finish(self, stage, terms=None):
        last = stage == len(self.dims) - 1
        for term in range(len(self.terms)) if terms is None else terms:
            self.send(term, stage).wait_recv()
            if stage == 0:
                self.keep(term).wait()
            landed = self.landed[term][stage]
            other = self.kept[term] if stage == 0 else self.landed[term][stage - 1]
            chosen = (slice(None),) * (len(self.dims) - 1) if stage == 0 else self.half(term, stage, False)
            depth = len(self.dims) - 1 - stage
            if last:
                total = landed[...].astype(jnp.float32) + other[chosen].astype(jnp.float32)
                self.outs[term][...] = total
                continue

            def add(block, carry, landed=landed, other=other, chosen=chosen, depth=depth):
                at = [(block >> k) & 1 for k in reversed(range(depth))]
                rest = iter(at)
                there = tuple(next(rest) if isinstance(c, slice) else c for c in chosen)
                total = landed[tuple(at)].astype(jnp.float32) + other[there].astype(jnp.float32)
                landed[tuple(at)] = total.astype(landed.dtype)
                return carry

            lax.fori_loop(0, 1 << depth, add, 0)

    def settle(self):
        for term in range(len(self.terms)):
            for stage in range(len(self.dims)):
                self.send(term, stage).wait_send()


def halving_scratch(dims, shapes, dtypes):
    count = len(dims)
    like = list(zip(shapes, dtypes))
    kept = [pltpu.VMEM((2,) * (count - 1) + s, d) for s, d in like]
    landed = [pltpu.VMEM((2,) * (count - 1 - k) + s, d) for s, d in like for k in range(count)]
    sems = [
        pltpu.SemaphoreType.DMA((len(shapes), count)),
        pltpu.SemaphoreType.DMA((len(shapes), count)),
        pltpu.SemaphoreType.DMA((len(shapes),)),
    ]
    return kept + landed + sems


def halving_of(dims, orders, terms, outs, scratch):
    count, stages = len(terms), len(dims)
    kept, rest = scratch[:count], scratch[count:]
    landed = [rest[stages * t : stages * (t + 1)] for t in range(count)]
    return Halving(dims, orders, terms, kept, landed, outs, *rest[stages * count :])


def scatter_kernel(dims, orders, *refs):
    count = len(orders)
    terms, outs, scratch = refs[:count], refs[count : 2 * count], refs[2 * count :]
    halving = halving_of(dims, orders, terms, outs, scratch)
    greet_partners(dims)
    for stage in range(len(dims)):
        halving.start(stage)
        halving.finish(stage)
    halving.settle()


def block_shape(term, dims):
    return (term.size // term.shape[-1] >> len(dims), term.shape[-1])


def scatter_all(terms, kinds, collective_id):
    dims = cube_dims()
    shapes = [block_shape(t, dims) for t in terms]
    cubes = [t.reshape((2,) * len(dims) + s) for t, s in zip(terms, shapes)]
    return pl.pallas_call(
        functools.partial(scatter_kernel, dims, [halving_order(k) for k in kinds]),
        in_specs=[pl.BlockSpec(memory_space=pl.ANY)] * len(cubes),
        out_specs=[pl.BlockSpec(memory_space=pltpu.VMEM)] * len(cubes),
        out_shape=[jax.ShapeDtypeStruct(s, jnp.float32) for s in shapes],
        scratch_shapes=halving_scratch(dims, shapes, [t.dtype for t in terms]),
        compiler_params=pltpu.CompilerParams(
            collective_id=collective_id, has_side_effects=True, vmem_limit_bytes=VMEM_LIMIT
        ),
        name="scatter_gradients",
    )(*cubes)


def on_device(
    image_tokens, text_states, text_segments, image_segment, out_grad,
    norm1_gain, norm1_bias, self_query, self_key, self_value, self_output,
    norm2_gain, norm2_bias, cross_query, cross_key, cross_value, cross_output,
    norm3_gain, norm3_bias, mlp_in, mlp_in_bias, mlp_out, mlp_out_bias,
):
    tokens = image_tokens[0]
    rows, width = tokens.shape
    hidden = mlp_in.shape[1]
    chunk = 512
    vectors = (
        norm1_gain, norm1_bias, norm2_gain, norm2_bias,
        norm3_gain, norm3_bias, mlp_in_bias, mlp_out_bias,
    )
    sizes = [v.shape[0] for v in vectors]
    shard = self_query.shape[0]
    owners = width // shard
    parts = hidden // width
    first = gather_all(
        jnp.concatenate([self_query, self_key, self_value, pack_vectors(vectors)], axis=0), 1, 2
    )
    second = gather_rows(
        jnp.concatenate(
            [mlp_out]
            + [mlp_in[:, width * k : width * (k + 1)] for k in range(parts)]
            + [self_output, cross_query, cross_key, cross_value, cross_output],
            axis=0,
        )
    )

    def matrix(source, index):
        if shard % 16 == 0:
            spec = pl.BlockSpec(
                (owners, shard, width), lambda *_: (0, index, 0), pipeline_mode=pl.Buffered(1)
            )
            return source, spec
        taken = source[:, shard * index : shard * (index + 1)].reshape(1, width, width)
        return taken, whole_block(taken.shape)

    weights_one = [matrix(first, k) for k in range(3)]
    gain_one, bias_one, gain_two, bias_two, gain_three, bias_three, up_bias, down_bias = (
        take_vectors(first[:, 3 * shard :], sizes)
    )
    weights_two = [matrix(second, 2 * parts + k) for k in range(5)]
    down_shard = mlp_out.shape[0]
    if shard % 16 == 0:
        per = width // chunk
        up = (
            second,
            pl.BlockSpec((owners, shard, chunk), lambda c: (0, parts + c // per, c % per)),
        )
        down = (
            second,
            pl.BlockSpec((chunk // down_shard, down_shard, width), lambda c: (c, 0, 0)),
        )
    else:
        taken = [
            second[:, shard * (parts + k) : shard * (parts + k + 1)].reshape(1, width, width)
            for k in range(parts)
        ]
        up = (
            jnp.concatenate(taken, axis=2),
            pl.BlockSpec((1, width, chunk), lambda c: (0, 0, c)),
        )
        down = (
            second[:, :down_shard].reshape(1, hidden, width),
            pl.BlockSpec((1, chunk, width), lambda c: (0, c, 0)),
        )

    own_text = text_states[0]
    slots = own_text.shape[0]
    text_full = jnp.concatenate(
        [own_text] + [swap_narrow(own_text, k) for k in text_partners()], axis=0
    )
    narrow_at = lax.axis_index("narrow")
    segments = jnp.concatenate(
        [
            lax.dynamic_slice_in_dim(text_segments[0], (narrow_at ^ k) * slots, slots, 0)
            for k in range(lax.axis_size("narrow"))
        ]
    )
    mask = (segments == image_segment[0, 0]).astype(jnp.int32).reshape(-1, 1)

    normed_one, queries, keys, values = project(tokens, gain_one, bias_one, weights_one)
    mixed_self, sums_self = attend(queries, keys, values)
    x1, h2, q2, a2, x2, h3, k2, v2 = middle(
        tokens, mixed_self, text_full, mask, (gain_two, bias_two, gain_three, bias_three), weights_two
    )
    (
        block_out, dx2, grad_up, grad_up_bias, grad_down,
        grad_gain_three, grad_bias_three, grad_down_bias,
    ) = mlp(x2, h3, out_grad[0], gain_three, up, up_bias, down, down_bias, chunk)
    (
        dx1, grad_mixed, grad_self_out, grad_cross_query, grad_cross_key, grad_cross_value,
        grad_cross_out, text_term, grad_gain_two, grad_bias_two,
    ) = middle_back(
        dx2, x1, mixed_self, h2, q2, a2, k2, v2, text_full, mask, gain_two, weights_two
    )
    text_grad = text_term[:slots]
    for k in text_partners():
        text_grad = text_grad + swap_narrow(text_term[k * slots : (k + 1) * slots], k)
    pairs = width // 128
    half = pairs // 2
    self_terms, self_grads = [], []
    for start in (0, half):
        terms = attend_back(queries, keys, values, grad_mixed, sums_self, start, half)
        self_terms.extend(terms)
        self_grads.extend(weight_grads(normed_one, terms))
    image_grad, grad_gain_one, grad_bias_one = first_back(
        tokens, dx1, gain_one, weights_one, self_terms
    )
    vector_terms = (
        grad_gain_one, grad_bias_one, grad_gain_two, grad_bias_two,
        grad_gain_three, grad_bias_three, grad_up_bias, grad_down_bias,
    )
    stacked = jnp.concatenate([v.reshape(owners, -1) for v in vector_terms], axis=1)
    stacked = jnp.pad(stacked, ((0, 0), (0, -stacked.shape[1] % 1024))).reshape(owners, -1, 128)
    (
        grad_down, grad_up, grad_cross_out, grad_cross_query, grad_self_out, grad_cross_key,
        grad_cross_value, *self_sums, summed,
    ) = scatter_all(
        [
            grad_down, grad_up, grad_cross_out, grad_cross_query, grad_self_out, grad_cross_key,
            grad_cross_value, *self_grads, stacked,
        ],
        [0, 1, 2, 2, 2, 0, 1, 2, 2, 0, 2, 2, 1, 0],
        2,
    )
    grad_self_query, grad_self_key, grad_self_value = (
        jnp.concatenate([self_sums[k], self_sums[k + 3]], axis=1) for k in range(3)
    )
    summed = summed.reshape(-1)
    vector_grads, at = [], 0
    for size in sizes:
        vector_grads.append(summed[at : at + size])
        at += size
    return (
        block_out[None], image_grad[None], text_grad[None],
        vector_grads[0], vector_grads[1],
        grad_self_query, grad_self_key, grad_self_value, grad_self_out,
        vector_grads[2], vector_grads[3],
        grad_cross_query, grad_cross_key, grad_cross_value, grad_cross_out,
        vector_grads[4], vector_grads[5],
        grad_up, vector_grads[6], grad_down, vector_grads[7],
    )


def solution(mesh):
    placed = (
        P(("wide", "narrow"), None, None),
        P("wide", "narrow", None),
        P("wide", None),
        P("wide", "narrow"),
        P(("wide", "narrow"), None, None),
        P(("wide", "narrow")),
        P(("wide", "narrow")),
        P(("wide", "narrow"), None),
        P(("wide", "narrow"), None),
        P(("wide", "narrow"), None),
        P(("wide", "narrow"), None),
        P(("wide", "narrow")),
        P(("wide", "narrow")),
        P(("wide", "narrow"), None),
        P(("wide", "narrow"), None),
        P(("wide", "narrow"), None),
        P(("wide", "narrow"), None),
        P(("wide", "narrow")),
        P(("wide", "narrow")),
        P(("wide", "narrow"), None),
        P(("wide", "narrow")),
        P(("wide", "narrow"), None),
        P(("wide", "narrow")),
    )
    return jax.shard_map(
        on_device,
        mesh=mesh,
        in_specs=placed,
        out_specs=(
            P(("wide", "narrow"), None, None),
            P(("wide", "narrow"), None, None),
            P("wide", "narrow", None),
            P(("wide", "narrow")),
            P(("wide", "narrow")),
            P(("wide", "narrow"), None),
            P(("wide", "narrow"), None),
            P(("wide", "narrow"), None),
            P(("wide", "narrow"), None),
            P(("wide", "narrow")),
            P(("wide", "narrow")),
            P(("wide", "narrow"), None),
            P(("wide", "narrow"), None),
            P(("wide", "narrow"), None),
            P(("wide", "narrow"), None),
            P(("wide", "narrow")),
            P(("wide", "narrow")),
            P(("wide", "narrow"), None),
            P(("wide", "narrow")),
            P(("wide", "narrow"), None),
            P(("wide", "narrow")),
        ),
        check_vma=False,
    )
```

```python
import functools
import math

import jax
import jax.numpy as jnp
from jax import lax
from jax.experimental import pallas as pl
from jax.experimental.pallas import tpu as pltpu
from jax.sharding import PartitionSpec as P

HEAD_DIM = 64
TILE = 256
BF16 = jnp.bfloat16
VMEM_LIMIT = 60 * 1024 * 1024
MLP_STEPS = 8

EPSILON = 1e-05
NEGATIVE = -1e30

AXES = ("wide", "narrow")


def axis_bits(axis):
    return lax.axis_size(axis).bit_length() - 1


def pack_vectors(vectors):
    flat = jnp.concatenate(vectors)
    room = -flat.shape[0] % (16 * 1024)
    return jnp.pad(flat, (0, room)).reshape(-1, 1024)


def take_vectors(rows, sizes):
    flat = rows.reshape(rows.shape[0], -1)
    out, at = [], 0
    for size in sizes:
        out.append(flat[:, at : at + size].reshape(1, -1).astype(jnp.float32))
        at += size
    return out


def nn(a, b):
    return lax.dot_general(a, b, (((1,), (0,)), ((), ())), preferred_element_type=jnp.float32)


def nt(a, b):
    return lax.dot_general(a, b, (((1,), (1,)), ((), ())), preferred_element_type=jnp.float32)


def tn(a, b):
    return lax.dot_general(a, b, (((0,), (0,)), ((), ())), preferred_element_type=jnp.float32)


def standardize(values):
    center = jnp.mean(values, axis=-1, keepdims=True)
    offset = values - center
    rate = lax.rsqrt(jnp.mean(offset * offset, axis=-1, keepdims=True) + EPSILON)
    return offset * rate, rate


def norm_back(standard, rate, gain, grad):
    scaled = grad * gain
    return rate * (
        scaled
        - jnp.mean(scaled, axis=-1, keepdims=True)
        - standard * jnp.mean(scaled * standard, axis=-1, keepdims=True)
    )


def column_sum(values):
    return jnp.sum(values, axis=0, keepdims=True)


def square(ref):
    return ref[...].reshape(-1, ref.shape[-1])


def head_lanes(block, head):
    lane = lax.broadcasted_iota(jnp.int32, block.shape, 1)
    inside = (lane >= HEAD_DIM) if head else (lane < HEAD_DIM)
    return jnp.where(inside, block, jnp.zeros_like(block))


def whole_block(shape):
    zeros = (0,) * len(shape)
    return pl.BlockSpec(shape, lambda *_: zeros, pipeline_mode=pl.Buffered(1))


def params(**extra):
    return pltpu.CompilerParams(vmem_limit_bytes=VMEM_LIMIT, **extra)


def attend_kernel(
    x_ref, gain_ref, bias_ref, wq_ref, wk_ref, wv_ref, h_ref, q_ref, k_ref, v_ref, o_ref, sums_ref
):
    rows = x_ref.shape[0]

    @pl.when(pl.program_id(0) == 0)
    def _():
        for start in range(0, rows, TILE):
            at = slice(start, start + TILE)
            standard, _ = standardize(x_ref[at, :].astype(jnp.float32))
            h_ref[at, :] = (standard * gain_ref[...] + bias_ref[...]).astype(BF16)

    weights = jnp.concatenate([square(w) for w in (wq_ref, wk_ref, wv_ref)], axis=1)
    mapped = nn(h_ref[...], weights).astype(BF16)
    q_ref[...] = mapped[:, :128]
    k_ref[...] = mapped[:, 128:256]
    v_ref[...] = mapped[:, 256:]
    flipped = v_ref[...].T
    for start in range(0, rows, TILE):
        span = start + TILE
        queries = q_ref[start:span, :] * (HEAD_DIM**-0.5)
        keys = k_ref[:span, :]
        mixed, sums = [], []
        for head in range(2):
            scores = nt(keys, head_lanes(queries, head))
            key_at = lax.broadcasted_iota(jnp.int32, (TILE, TILE), 0)
            query_at = lax.broadcasted_iota(jnp.int32, (TILE, TILE), 1)
            corner = jnp.where(key_at <= query_at, scores[start:], NEGATIVE)
            scores = jnp.concatenate([scores[:start], corner], axis=0) if start else corner
            top = jnp.max(scores, axis=0, keepdims=True)
            powers = jnp.exp(scores - top)
            total = jnp.sum(powers, axis=0, keepdims=True)
            part = nn(flipped[HEAD_DIM * head : HEAD_DIM * (head + 1), :span], powers.astype(BF16))
            mixed.append(part * (1.0 / total))
            sums.append(top + jnp.log(total))
        o_ref[start:span, :] = jnp.concatenate(mixed, axis=0).T.astype(BF16)
        sums_ref[0, :, start:span] = jnp.concatenate(sums, axis=0)


def attend(tokens, gain, bias, weights, work, schedule, collective_id):
    rows, width = tokens.shape
    pairs = width // 128
    block = pl.BlockSpec((rows, 128), lambda p: (0, p))
    arrays, specs = zip(*weights)
    like = jax.ShapeDtypeStruct(tokens.shape, BF16)
    results = pl.pallas_call(
        beside(attend_kernel, work, (6, 6, 0), schedule, pairs),
        grid=(pairs,),
        in_specs=[whole_block(tokens.shape), whole_block(gain.shape), whole_block(bias.shape)]
        + list(specs)
        + work.in_specs,
        out_specs=[whole_block(tokens.shape)]
        + [block] * 4
        + [pl.BlockSpec((1, 2, rows), lambda p: (p, 0, 0))]
        + work.out_specs,
        out_shape=[like] * 5
        + [jax.ShapeDtypeStruct((pairs, 2, rows), jnp.float32)]
        + work.out_shape,
        scratch_shapes=work.scratch,
        compiler_params=params(collective_id=collective_id, has_side_effects=True),
        name="self_attend",
    )(tokens, gain, bias, *arrays, *work.arrays)
    return results[:6], work.results(results[6:])


def attend_back_kernel(
    q_ref, k_ref, v_ref, da_ref, sums_ref, h_ref,
    dq_ref, dk_ref, dv_ref, dwq_ref, dwk_ref, dwv_ref, dk_sum, dv_sum, h_flip,
):
    rows, width = q_ref.shape

    @pl.when(pl.program_id(0) == 0)
    def _():
        h_flip[...] = h_ref[...].T

    flipped = k_ref[...].T
    for start in reversed(range(0, rows, TILE)):
        span = start + TILE
        queries = q_ref[start:span, :] * (HEAD_DIM**-0.5)
        grads = da_ref[start:span, :]
        keys = k_ref[:span, :]
        values = v_ref[:span, :]
        parts = []
        for head in range(2):
            own_queries = head_lanes(queries, head)
            own_grads = head_lanes(grads, head)
            scores = nt(keys, own_queries)
            key_at = lax.broadcasted_iota(jnp.int32, (TILE, TILE), 0)
            query_at = lax.broadcasted_iota(jnp.int32, (TILE, TILE), 1)
            corner = jnp.where(key_at <= query_at, scores[start:], NEGATIVE)
            scores = jnp.concatenate([scores[:start], corner], axis=0) if start else corner
            probs = jnp.exp(scores - sums_ref[0, head : head + 1, start:span])
            grad_probs = nt(values, own_grads)
            inner = jnp.sum(probs * grad_probs, axis=0, keepdims=True)
            grad_scores = (probs * (grad_probs - inner)).astype(BF16)
            value_term = nn(probs.astype(BF16), own_grads)
            key_term = nn(grad_scores, own_queries)
            if span == rows and head == 0:
                dv_sum[...] = value_term
                dk_sum[...] = key_term
            else:
                dv_sum[:span, :] += value_term
                dk_sum[:span, :] += key_term
            parts.append(nn(flipped[HEAD_DIM * head : HEAD_DIM * (head + 1), :span], grad_scores))
        dq = jnp.concatenate(parts, axis=0).T * (HEAD_DIM**-0.5)
        dq_ref[start:span, :] = dq.astype(BF16)
    dk_ref[...] = dk_sum[...].astype(BF16)
    dv_ref[...] = dv_sum[...].astype(BF16)
    grads = jnp.concatenate([dq_ref[...], dk_ref[...], dv_ref[...]], axis=1)
    weights = nn(h_flip[...], grads).astype(BF16)
    dwq_ref[...] = weights[:, :128]
    dwk_ref[...] = weights[:, 128:256]
    dwv_ref[...] = weights[:, 256:]


def attend_back(queries, keys, values, grads, sums, normed, work, schedule, collective_id):
    rows, width = queries.shape
    steps = width // 128
    block = pl.BlockSpec((rows, 128), lambda p: (0, p))
    results = pl.pallas_call(
        beside(attend_back_kernel, work, (6, 6, 3), schedule, steps),
        grid=(steps,),
        in_specs=[block] * 4
        + [pl.BlockSpec((1, 2, rows), lambda p: (p, 0, 0)), whole_block(normed.shape)]
        + work.in_specs,
        out_specs=[block] * 6 + work.out_specs,
        out_shape=[jax.ShapeDtypeStruct(queries.shape, BF16)] * 3
        + [jax.ShapeDtypeStruct((width, width), BF16)] * 3
        + work.out_shape,
        scratch_shapes=[pltpu.VMEM((rows, 128), jnp.float32)] * 2
        + [pltpu.VMEM((width, rows), BF16)]
        + work.scratch,
        compiler_params=params(collective_id=collective_id, has_side_effects=True),
        name="self_attend_back",
    )(queries, keys, values, grads, sums, normed, *work.arrays)
    return results[:6], work.results(results[6:])


def gelu_both(values):
    phi = 0.5 + 0.5 * lax.erf(values * (0.5**0.5))
    density = jnp.exp(-0.5 * values * values) * ((2.0 * math.pi) ** -0.5)
    return values * phi, phi + values * density


def mlp_kernel(
    near, far, work, x_ref, h_ref, g_ref, gain_ref, up_ref, ub_ref, down_ref, db_ref,
    out_ref, dx_ref, dub_ref, dgain_ref, dbias_ref, gsum_ref, ddown_ref, *refs,
):
    far_refs, refs = refs[:far], refs[far:]
    sums, refs = refs[: len(work.out_specs)], refs[len(work.out_specs) :]
    out_sum, dh_sum, h_flip, act, grad_act = refs[:5]
    near_refs, refs = refs[5 : 5 + near], refs[5 + near :]
    step, steps = pl.program_id(0), pl.num_programs(0)
    rows = h_ref.shape[0]
    parts = near + far
    per = MLP_STEPS // parts
    moving = work.bind(near_refs, sums, refs) if near else None

    @pl.when(step == 0)
    def _():
        if near:
            greet_partners()
        h_flip[...] = h_ref[...].T
        out_sum[...] = x_ref[...] + db_ref[...]
        dh_sum[...] = jnp.zeros_like(dh_sum)

    left = []
    for part in range(near):
        terms = [k for k, t in enumerate(work.terms) if t[0] == part]
        for stage in range(-1, moving.stages):
            place = per * (part + 1) + stage + 1
            if place >= MLP_STEPS:
                left.append((stage, terms))
                continue

            @pl.when(step == place)
            def _(stage=stage, terms=terms):
                moving.step(stage, terms)

    up = square(up_ref)
    down = square(down_ref)
    bias_sum = jnp.zeros_like(dub_ref)
    for start in range(0, rows, TILE):
        at = slice(start, start + TILE)
        hidden, slope = gelu_both(nn(h_ref[at, :], up) + ub_ref[...])
        act[at, :] = hidden.astype(BF16)
        grad_pre = (nt(g_ref[at, :], down) * slope).astype(BF16)
        grad_act[at, :] = grad_pre
        bias_sum += column_sum(grad_pre.astype(jnp.float32))
        out_sum[at, :] += nn(act[at, :], down)
        dh_sum[at, :] += nt(grad_pre, up)
    dub_ref[...] = bias_sum
    grad_up = nn(h_flip[...], grad_act[...]).astype(BF16)
    chunk = grad_up.shape[1]
    for part, ref in enumerate(far_refs):

        @pl.when(step // per == near + part)
        def _(ref=ref):
            ref[...] = grad_up

    for place in range(near * per):

        @pl.when(step == place)
        def _(place=place):
            ref = near_refs[place // per]
            first = chunk * (place % per)
            ref[..., first : first + chunk] = grad_up.reshape(ref.shape[:-1] + (chunk,))

    ddown_ref[...] = tn(act[...], g_ref[...]).astype(BF16)

    @pl.when(step == steps - 1)
    def _():
        gain_sum = jnp.zeros_like(dgain_ref)
        grad_sum = jnp.zeros_like(dbias_ref)
        tail_sum = jnp.zeros_like(gsum_ref)
        for start in range(0, rows, TILE):
            at = slice(start, start + TILE)
            out_ref[at, :] = out_sum[at, :].astype(BF16)
            standard, rate = standardize(x_ref[at, :])
            grad = dh_sum[at, :]
            tail = g_ref[at, :].astype(jnp.float32)
            dx_ref[at, :] = tail + norm_back(standard, rate, gain_ref[...], grad)
            gain_sum += column_sum(grad * standard)
            grad_sum += column_sum(grad)
            tail_sum += column_sum(tail)
        dgain_ref[...] = gain_sum
        dbias_ref[...] = grad_sum
        gsum_ref[...] = tail_sum
        for stage, terms in left:
            moving.step(stage, terms)
        if near:
            moving.settle()


def mlp(x, h, g, gain, up, up_bias, down, down_bias, near, runs, orders, collective_id):
    rows, width = x.shape
    hidden = up_bias.shape[1]
    chunk = hidden // MLP_STEPS
    f32 = jnp.float32
    row = (1, width)
    parts = hidden // width
    per = width // chunk
    lead = (2,) * len(cube_dims())
    block = lead + (width >> len(lead), width)
    source = jax.ShapeDtypeStruct(block, BF16)
    work = Scatter([(source, runs, orders)] * near, near=True)
    far = parts - near
    results = pl.pallas_call(
        functools.partial(mlp_kernel, near, far, work),
        grid=(MLP_STEPS,),
        in_specs=[
            whole_block(x.shape), whole_block(h.shape), whole_block(g.shape), whole_block(row),
            up[1], pl.BlockSpec((1, chunk), lambda c: (0, c)), down[1], whole_block(row),
        ],
        out_specs=[
            whole_block(x.shape), whole_block(x.shape),
            pl.BlockSpec((1, chunk), lambda c: (0, c)),
            whole_block(row), whole_block(row), whole_block(row),
            pl.BlockSpec((chunk, width), lambda c: (c, 0)),
        ]
        + [
            pl.BlockSpec((width, chunk), lambda c, k=k: (0, jnp.clip(c - per * k, 0, per - 1)))
            for k in range(near, parts)
        ]
        + work.out_specs,
        out_shape=[
            jax.ShapeDtypeStruct(x.shape, BF16), jax.ShapeDtypeStruct(x.shape, f32),
            jax.ShapeDtypeStruct((1, hidden), f32),
            jax.ShapeDtypeStruct(row, f32), jax.ShapeDtypeStruct(row, f32), jax.ShapeDtypeStruct(row, f32),
            jax.ShapeDtypeStruct((hidden, width), BF16),
        ]
        + [jax.ShapeDtypeStruct((width, width), BF16)] * far
        + work.out_shape,
        scratch_shapes=[
            pltpu.VMEM(x.shape, f32), pltpu.VMEM(x.shape, f32), pltpu.VMEM((width, rows), BF16),
            pltpu.VMEM((rows, chunk), BF16), pltpu.VMEM((rows, chunk), BF16),
        ]
        + [pltpu.VMEM(block, BF16)] * near
        + (work.scratch if near else []),
        compiler_params=params(collective_id=collective_id, has_side_effects=True) if near else params(),
        name="mlp_both_ways",
    )(x, h, g, gain, up[0], up_bias, down[0], down_bias)
    sums = work.results(results[7 + far :]) if near else []
    return *results[:7], results[7 : 7 + far], sums


def caption_probs(keys, own_queries, mask):
    scores = jnp.where(mask != 0, nt(keys, own_queries), NEGATIVE)
    powers = jnp.exp(scores - jnp.max(scores, axis=0, keepdims=True))
    return powers * (1.0 / jnp.sum(powers, axis=0, keepdims=True))


def middle_kernel(
    x_ref, a_ref, text_ref, mask_ref, gain2_ref, bias2_ref, gain3_ref, bias3_ref,
    wo_ref, cq_ref, ck_ref, cv_ref, co_ref,
    x1_ref, h2_ref, q2_ref, a2_ref, x2_ref, h3_ref, k2_ref, v2_ref,
):
    @pl.when(pl.program_id(0) == 0)
    def _():
        k2_ref[...] = nn(text_ref[...], square(ck_ref)).astype(BF16)
        v2_ref[...] = nn(text_ref[...], square(cv_ref)).astype(BF16)

    after_self = x_ref[...].astype(jnp.float32) + nn(a_ref[...], square(wo_ref))
    x1_ref[...] = after_self
    standard, _ = standardize(after_self)
    normed = (standard * gain2_ref[...] + bias2_ref[...]).astype(BF16)
    h2_ref[...] = normed
    q2_ref[...] = nn(normed, square(cq_ref)).astype(BF16)
    mask = mask_ref[...]
    for pair in range(q2_ref.shape[1] // 128):
        at = slice(128 * pair, 128 * (pair + 1))
        queries = q2_ref[:, at] * (HEAD_DIM**-0.5)
        keys = k2_ref[:, at]
        flipped = v2_ref[:, at].T
        mixed = []
        for head in range(2):
            probs = caption_probs(keys, head_lanes(queries, head), mask).astype(BF16)
            mixed.append(nn(flipped[HEAD_DIM * head : HEAD_DIM * (head + 1)], probs))
        a2_ref[:, at] = jnp.concatenate(mixed, axis=0).T.astype(BF16)
    after_cross = after_self + nn(a2_ref[...], square(co_ref))
    x2_ref[...] = after_cross
    standard, _ = standardize(after_cross)
    h3_ref[...] = (standard * gain3_ref[...] + bias3_ref[...]).astype(BF16)


def middle(tokens, mixed, text, mask, vectors, weights, work, schedule, collective_id):
    rows, width = tokens.shape
    slots = text.shape[0]
    tile = pl.BlockSpec((TILE, width), lambda i: (i, 0))
    arrays, specs = zip(*weights)
    f32 = jnp.float32
    like = lambda dtype: jax.ShapeDtypeStruct(tokens.shape, dtype)
    results = pl.pallas_call(
        beside(middle_kernel, work, (13, 8, 0), schedule, rows // TILE),
        grid=(rows // TILE,),
        in_specs=[
            tile, tile, whole_block(text.shape), whole_block(mask.shape),
            *[whole_block(v.shape) for v in vectors], *specs, *work.in_specs,
        ],
        out_specs=[tile] * 6 + [whole_block(text.shape)] * 2 + work.out_specs,
        out_shape=[like(f32), like(BF16), like(BF16), like(BF16), like(f32), like(BF16)]
        + [jax.ShapeDtypeStruct(text.shape, BF16)] * 2
        + work.out_shape,
        scratch_shapes=work.scratch,
        compiler_params=params(collective_id=collective_id, has_side_effects=True),
        name="output_and_cross",
    )(tokens, mixed, text, mask, *vectors, *arrays, *work.arrays)
    return results[:8], work.results(results[8:])


def middle_back_kernel(
    dx2_ref, x1_ref, a1_ref, h2_ref, q2_ref, a2_ref, k2_ref, v2_ref, text_ref, mask_ref, gain2_ref,
    wo_ref, cq_ref, ck_ref, cv_ref, co_ref,
    dx1_ref, da1_ref, dwo_ref, dcq_ref, dck_ref, dcv_ref, dco_ref, dtext_ref, dgain_ref, dbias_ref,
    wo_sum, cq_sum, co_sum, dk_sum, dv_sum, dq2,
):
    step, steps = pl.program_id(0), pl.num_programs(0)

    @pl.when(step == 0)
    def _():
        for ref in (wo_sum, cq_sum, co_sum, dk_sum, dv_sum, dgain_ref, dbias_ref):
            ref[...] = jnp.zeros_like(ref)

    grad_out = dx2_ref[...].astype(BF16)
    co_sum[...] += tn(a2_ref[...], grad_out)
    grad_mixed = nt(grad_out, square(co_ref)).astype(BF16)
    mask = mask_ref[...]
    for pair in range(q2_ref.shape[1] // 128):
        at = slice(128 * pair, 128 * (pair + 1))
        queries = q2_ref[:, at] * (HEAD_DIM**-0.5)
        keys = k2_ref[:, at]
        flipped = keys.T
        values = v2_ref[:, at]
        grads = grad_mixed[:, at]
        parts = []
        for head in range(2):
            own_queries = head_lanes(queries, head)
            own_grads = head_lanes(grads, head)
            probs = caption_probs(keys, own_queries, mask)
            grad_probs = nt(values, own_grads)
            inner = jnp.sum(probs * grad_probs, axis=0, keepdims=True)
            grad_scores = (probs * (grad_probs - inner)).astype(BF16)
            dv_sum[:, at] += nn(probs.astype(BF16), own_grads)
            dk_sum[:, at] += nn(grad_scores, own_queries)
            parts.append(nn(flipped[HEAD_DIM * head : HEAD_DIM * (head + 1)], grad_scores))
        dq2[:, at] = (jnp.concatenate(parts, axis=0).T * (HEAD_DIM**-0.5)).astype(BF16)
    cq_sum[...] += tn(h2_ref[...], dq2[...])
    grad_normed = nt(dq2[...], square(cq_ref))
    standard, rate = standardize(x1_ref[...])
    grad_after = dx2_ref[...] + norm_back(standard, rate, gain2_ref[...], grad_normed)
    dgain_ref[...] += column_sum(grad_normed * standard)
    dbias_ref[...] += column_sum(grad_normed)
    dx1_ref[...] = grad_after
    grad_self = grad_after.astype(BF16)
    wo_sum[...] += tn(a1_ref[...], grad_self)
    da1_ref[...] = nt(grad_self, square(wo_ref)).astype(BF16)

    @pl.when(step == steps - 1)
    def _():
        dwo_ref[...] = wo_sum[...].astype(BF16)
        dcq_ref[...] = cq_sum[...].astype(BF16)
        dco_ref[...] = co_sum[...].astype(BF16)
        grad_keys = dk_sum[...].astype(BF16)
        grad_values = dv_sum[...].astype(BF16)
        dck_ref[...] = tn(text_ref[...], grad_keys).astype(BF16)
        dcv_ref[...] = tn(text_ref[...], grad_values).astype(BF16)
        dtext_ref[...] = nt(grad_keys, square(ck_ref)) + nt(grad_values, square(cv_ref))


def middle_back(
    dx2, x1, a1, h2, q2, a2, k2, v2, text, mask, gain, weights, work, schedule, collective_id
):
    rows, width = x1.shape
    slots = text.shape[0]
    tile = pl.BlockSpec((TILE, width), lambda i: (i, 0))
    arrays, specs = zip(*weights)
    f32 = jnp.float32
    matrix = (width, width)
    results = pl.pallas_call(
        beside(middle_back_kernel, work, (16, 10, 6), schedule, rows // TILE),
        grid=(rows // TILE,),
        in_specs=[tile] * 6
        + [whole_block(v.shape) for v in (k2, v2, text, mask, gain)]
        + list(specs)
        + work.in_specs,
        out_specs=[tile] * 2
        + [whole_block(matrix)] * 5
        + [whole_block(text.shape)]
        + [whole_block(gain.shape)] * 2
        + work.out_specs,
        out_shape=[jax.ShapeDtypeStruct(x1.shape, f32), jax.ShapeDtypeStruct(x1.shape, BF16)]
        + [jax.ShapeDtypeStruct(matrix, BF16)] * 5
        + [jax.ShapeDtypeStruct(text.shape, f32)]
        + [jax.ShapeDtypeStruct(gain.shape, f32)] * 2
        + work.out_shape,
        scratch_shapes=[pltpu.VMEM(matrix, f32)] * 3
        + [pltpu.VMEM(text.shape, f32)] * 2
        + [pltpu.VMEM((TILE, width), BF16)]
        + work.scratch,
        compiler_params=params(collective_id=collective_id, has_side_effects=True),
        name="cross_back",
    )(dx2, x1, a1, h2, q2, a2, k2, v2, text, mask, gain, *arrays, *work.arrays)
    return results[:10], work.results(results[10:])


def first_back_kernel(
    work, schedule, steps, x_ref, dx1_ref, gain_ref, vectors_ref, wq_ref, wk_ref, wv_ref, dq_ref, dk_ref, dv_ref,
    *refs,
):
    n, m = len(work.in_specs), len(work.out_specs)
    sources, (dx_ref, vector_sum_ref), sums = refs[:n], refs[n : n + 2], refs[n + 2 : n + 2 + m]
    stages = len(cube_dims())
    rest = refs[n + 2 + m :]
    doubling = Doubling(rest[0], rest[1 : stages + 1], *rest[stages + 1 : stages + 3])
    halving = work.bind(sources, sums, rest[stages + 3 :])
    step = pl.program_id(0)
    vectors = doubling.buffers[0]

    @pl.when(step == 0)
    def _():
        greet_partners()
        halving.step(-1)
        vectors[...] = vectors_ref[...]

    for stage, place in enumerate(schedule):

        @pl.when(step == place)
        def _(stage=stage):
            halving.step(stage)

    grad_normed = (
        nt(dq_ref[...], square(wq_ref)) + nt(dk_ref[...], square(wk_ref)) + nt(dv_ref[...], square(wv_ref))
    )
    standard, rate = standardize(x_ref[...].astype(jnp.float32))
    dx_ref[...] = dx1_ref[...] + norm_back(standard, rate, gain_ref[...], grad_normed)
    vectors[0:1, :] += column_sum(grad_normed * standard)
    vectors[1:2, :] += column_sum(grad_normed)

    @pl.when(step == steps - 1)
    def _():
        doubling.step(-1)
        for stage in range(max(stages, halving.stages)):
            if stage < stages:
                doubling.step(stage)
            if len(schedule) + stage < halving.stages:
                halving.step(len(schedule) + stage)
        vector_sum_ref[...] = doubling.buffers[-1][...]
        doubling.settle()
        halving.settle()


def first_back(tokens, dx1, gain, vectors, weights, grads, work, schedule, collective_id):
    rows, width = tokens.shape
    steps = rows // TILE
    tile = pl.BlockSpec((TILE, width), lambda i: (i, 0))
    arrays, specs = zip(*weights)
    f32 = jnp.float32
    results = pl.pallas_call(
        functools.partial(first_back_kernel, work, schedule, steps),
        grid=(steps,),
        in_specs=[tile] * 2
        + [whole_block(gain.shape), whole_block(vectors.shape)]
        + list(specs)
        + [tile] * 3
        + work.in_specs,
        out_specs=[tile, whole_block(vectors.shape)] + work.out_specs,
        out_shape=[
            jax.ShapeDtypeStruct(tokens.shape, f32),
            jax.ShapeDtypeStruct(vectors.shape, f32),
        ]
        + work.out_shape,
        scratch_shapes=doubling_scratch(vectors.shape) + work.scratch,
        compiler_params=params(collective_id=collective_id, has_side_effects=True),
        name="self_norm_back",
    )(tokens, dx1, gain, vectors, *arrays, *grads, *work.arrays)
    return results[:2], work.results(results[2:])


def cube_dims(axes=AXES):
    return [(axis, k) for axis in axes for k in reversed(range(axis_bits(axis)))]


def bits_of(dims):
    return [(lax.axis_index(axis) >> bit) & 1 for axis, bit in dims]


def partner(axis, bit):
    return {axis: lax.axis_index(axis) ^ (1 << bit)}


def halving_orders():
    x, y, near, far = ("narrow", 0), ("narrow", 1), ("wide", 1), ("wide", 2)
    core = ("wide", 0)
    six = (
        (far, x, y, near),
        (near, y, x, far),
        (y, far, x, near),
        (x, near, y, far),
        (x, y, far, near),
        (y, x, near, far),
    )
    rest = [d for d in cube_dims() if d not in (core, x, y, near, far)]
    return [[core, *order, *rest] for order in six]


def greet_partners():
    dims = cube_dims()
    barrier = pltpu.get_barrier_semaphore()
    for axis, bit in dims:
        pl.semaphore_signal(
            barrier, inc=1, device_id=partner(axis, bit), device_id_type=pl.DeviceIdType.MESH
        )
    pl.semaphore_wait(barrier, len(dims))


def row_pieces(rows, count, step=16):
    if rows % step:
        return [(0, rows)]
    cuts = [rows * k // count // step * step for k in range(count)] + [rows]
    return [(a, b - a) for a, b in zip(cuts[:-1], cuts[1:]) if b > a]


class Gathering:
    def __init__(self, pieces, dims, sources, outs, scratch):
        self.pieces, self.dims, self.sources, self.outs = pieces, dims, sources, outs
        self.send_sems, self.recv_sems, self.own_sems = scratch
        self.stages = max(len(order) for _, _, _, order in pieces)
        self.base = [sum(len(p[3]) for p in pieces[:k]) for k in range(len(pieces))]

    def own(self, which):
        there = self.outs[which].at[tuple(bits_of(self.dims[which]))]
        return pltpu.make_async_copy(self.sources[which], there, self.own_sems.at[which])

    def send(self, piece, stage):
        which, start, size, order = self.pieces[piece]
        rows = slice(start, start + size)
        held = order[:stage]
        dims = self.dims[which]
        at = tuple(slice(None) if d in held else b for d, b in zip(dims, bits_of(dims))) + (rows,)
        there = self.outs[which].at[at]
        sem = self.base[piece] + stage
        return pltpu.make_async_remote_copy(
            src_ref=there if stage else self.sources[which].at[rows],
            dst_ref=there,
            send_sem=self.send_sems.at[sem],
            recv_sem=self.recv_sems.at[sem],
            device_id=partner(*order[stage]),
            device_id_type=pl.DeviceIdType.MESH,
        )

    def step(self, stage):
        if stage < 0:
            for which in range(len(self.sources)):
                self.own(which).start()
        if stage == 0:
            for which in range(len(self.sources)):
                self.own(which).wait()
        for piece, (_, _, _, order) in enumerate(self.pieces):
            if 0 <= stage < len(order):
                self.send(piece, stage).wait_recv()
            if stage + 1 < len(order):
                self.send(piece, stage + 1).start()

    def settle(self):
        for piece, (_, _, _, order) in enumerate(self.pieces):
            for stage in range(len(order)):
                self.send(piece, stage).wait_send()


class Gather:
    def __init__(self, groups):
        self.arrays = [array for array, _, _ in groups]
        self.pieces, self.dims = [], []
        for which, (array, runs, orders) in enumerate(groups):
            self.dims.append([d for d in cube_dims() if d in orders[0]])
            for k, (start, size) in enumerate(runs):
                self.pieces.append((which, start, size, orders[k % len(orders)]))
        copies = sum(len(order) for _, _, _, order in self.pieces)
        self.in_specs = [pl.BlockSpec(memory_space=pl.ANY)] * len(groups)
        self.out_specs = self.in_specs
        self.out_shape = [
            jax.ShapeDtypeStruct((2,) * len(d) + a.shape, a.dtype)
            for a, d in zip(self.arrays, self.dims)
        ]
        self.scratch = [pltpu.SemaphoreType.DMA((copies,))] * 2
        self.scratch += [pltpu.SemaphoreType.DMA((len(groups),))]

    def bind(self, sources, outs, scratch):
        return Gathering(self.pieces, self.dims, sources, outs, scratch)

    def results(self, outs):
        return [out.reshape((-1,) + a.shape) for out, a in zip(outs, self.arrays)]


class Halving:
    def __init__(self, terms, sources, outs, scratch, near=False):
        count = len(terms)
        self.terms, self.sources, self.outs, self.near = terms, sources, outs, near
        self.kept, rest = ([], scratch) if near else (scratch[:count], scratch[count:])
        self.landed, self.base = [], []
        for _, _, _, order in terms:
            self.base.append(sum(len(t[3]) for t in terms[: len(self.base)]))
            self.landed.append(rest[: len(order)])
            rest = rest[len(order) :]
        self.send_sems, self.recv_sems = rest[:2]
        self.kept_sems = None if near else rest[2]
        self.stages = max(len(order) for _, _, _, order in terms)

    def half(self, term, stage, other):
        _, start, size, order = self.terms[term]
        left = [d for d in cube_dims() if d in order[stage:]]
        bit = bits_of([order[stage]])[0]
        at = [(1 - bit if other else bit) if d == order[stage] else slice(None) for d in left]
        if stage == 0:
            at.append(slice(start, start + size))
        return tuple(at)

    def before(self, term, stage):
        return self.sources[self.terms[term][0]] if stage == 0 else self.landed[term][stage - 1]

    def send(self, term, stage):
        order = self.terms[term][3]
        sem = self.base[term] + stage
        return pltpu.make_async_remote_copy(
            src_ref=self.before(term, stage).at[self.half(term, stage, True)],
            dst_ref=self.landed[term][stage],
            send_sem=self.send_sems.at[sem],
            recv_sem=self.recv_sems.at[sem],
            device_id=partner(*order[stage]),
            device_id_type=pl.DeviceIdType.MESH,
        )

    def keep(self, term):
        source = self.before(term, 0).at[self.half(term, 0, False)]
        return pltpu.make_async_copy(source, self.kept[term], self.kept_sems.at[term])

    def start(self, term, stage):
        self.send(term, stage).start()
        if stage == 0 and not self.near:
            self.keep(term).start()

    def finish(self, term, stage):
        self.send(term, stage).wait_recv()
        if stage == 0 and not self.near:
            self.keep(term).wait()
        landed = self.landed[term][stage]
        depth = len(self.terms[term][3]) - 1 - stage
        if stage == 0 and not self.near:
            other, chosen = self.kept[term], (slice(None),) * depth
        else:
            other, chosen = self.before(term, stage), self.half(term, stage, False)
        if depth == 0:
            total = landed[...].astype(jnp.float32) + other[chosen].astype(jnp.float32)
            self.outs[term][...] = total
            return

        def add(block, carry):
            at = [(block >> k) & 1 for k in reversed(range(depth))]
            rest = iter(at)
            there = [next(rest, c) if isinstance(c, slice) else c for c in chosen]
            total = landed[tuple(at)].astype(jnp.float32) + other[tuple(there)].astype(jnp.float32)
            landed[tuple(at)] = total.astype(landed.dtype)
            return carry

        lax.fori_loop(0, 1 << depth, add, 0)

    def step(self, stage, terms=None):
        for term in range(len(self.terms)) if terms is None else terms:
            stages = len(self.terms[term][3])
            if 0 <= stage < stages:
                self.finish(term, stage)
            if stage + 1 < stages:
                self.start(term, stage + 1)

    def settle(self):
        for term, (_, _, _, order) in enumerate(self.terms):
            for stage in range(len(order)):
                self.send(term, stage).wait_send()


class Scatter:
    def __init__(self, groups, near=False):
        self.near = near
        self.terms, self.arrays = [], []
        shapes, dtypes = [], []
        for which, (array, runs, orders) in enumerate(groups):
            lead = 1 << len(orders[0])
            columns = array.shape[-1]
            block = (array.size // columns // lead, columns)
            self.arrays.append(array if near else array.reshape((2,) * len(orders[0]) + block))
            for start, size in runs:
                order = orders[len(self.terms) % len(orders)]
                self.terms.append((which, start, size, order))
                shapes.append((size, columns))
                dtypes.append(array.dtype)
        like = [(s, d, len(t[3])) for s, d, t in zip(shapes, dtypes, self.terms)]
        kept = [pltpu.VMEM((2,) * (n - 1) + s, d) for s, d, n in like]
        landed = [pltpu.VMEM((2,) * (n - 1 - k) + s, d) for s, d, n in like for k in range(n)]
        copies = sum(n for _, _, n in like)
        self.in_specs = [] if near else [pl.BlockSpec(memory_space=pl.ANY)] * len(groups)
        self.out_specs = [whole_block(s) for s in shapes]
        self.out_shape = [jax.ShapeDtypeStruct(s, jnp.float32) for s in shapes]
        self.scratch = ([] if near else kept) + landed + [pltpu.SemaphoreType.DMA((copies,))] * 2
        if not near:
            self.scratch += [pltpu.SemaphoreType.DMA((len(self.terms),))]

    def bind(self, sources, outs, scratch):
        return Halving(self.terms, sources, outs, scratch, self.near)

    def results(self, outs):
        found = {}
        for (which, _, _, _), out in zip(self.terms, outs):
            found.setdefault(which, []).append(out)
        return [jnp.concatenate(found[k], axis=0) for k in sorted(found)]


def beside(kernel, work, counts, schedule, steps):
    n_in, n_out, n_scratch = counts

    def run(*refs):
        cuts = [0, n_in, len(work.in_specs), n_out, len(work.out_specs), n_scratch]
        at = [sum(cuts[: k + 1]) for k in range(len(cuts))]
        ins, sources, outs, sums, own = (refs[a:b] for a, b in zip(at[:-1], at[1:]))
        moving = work.bind(sources, sums, refs[at[-1] :])
        step = pl.program_id(0)
        for place in sorted({0, *schedule}):

            @pl.when(step == place)
            def _(place=place):
                if place == 0:
                    greet_partners()
                    moving.step(-1)
                for stage, when in enumerate(schedule):
                    if when == place:
                        moving.step(stage)

        kernel(*ins, *outs, *own)

        @pl.when(step == steps - 1)
        def _():
            for stage in range(len(schedule), moving.stages):
                moving.step(stage)
            moving.settle()

    return run


def alone_kernel(work, *refs):
    n, m = len(work.in_specs), len(work.out_specs)
    moving = work.bind(refs[:n], refs[n : n + m], refs[n + m :])
    greet_partners()
    for stage in range(-1, moving.stages):
        moving.step(stage)
    moving.settle()


def alone(work, collective_id):
    outs = pl.pallas_call(
        functools.partial(alone_kernel, work),
        in_specs=work.in_specs,
        out_specs=work.out_specs,
        out_shape=work.out_shape,
        scratch_shapes=work.scratch,
        compiler_params=params(collective_id=collective_id, has_side_effects=True),
        name="gather_weights",
    )(*work.arrays)
    return work.results(outs)


class Doubling:
    def __init__(self, source, landed, send_sems, recv_sems):
        self.buffers = [source, *landed]
        self.send_sems, self.recv_sems = send_sems, recv_sems

    def swap(self, stage):
        return pltpu.make_async_remote_copy(
            src_ref=self.buffers[stage],
            dst_ref=self.buffers[stage + 1],
            send_sem=self.send_sems.at[stage],
            recv_sem=self.recv_sems.at[stage],
            device_id=partner(*cube_dims()[stage]),
            device_id_type=pl.DeviceIdType.MESH,
        )

    def step(self, stage):
        if stage >= 0:
            self.swap(stage).wait_recv()
            self.buffers[stage + 1][...] += self.buffers[stage][...]
        if stage + 2 < len(self.buffers):
            self.swap(stage + 1).start()

    def settle(self):
        for stage in range(len(self.buffers) - 1):
            self.swap(stage).wait_send()


def doubling_scratch(shape):
    stages = len(cube_dims())
    return [pltpu.VMEM(shape, jnp.float32)] * (stages + 1) + [pltpu.SemaphoreType.DMA((stages,))] * 2


def on_device(
    image_tokens, text_states, text_segments, image_segment, out_grad,
    norm1_gain, norm1_bias, self_query, self_key, self_value, self_output,
    norm2_gain, norm2_bias, cross_query, cross_key, cross_value, cross_output,
    norm3_gain, norm3_bias, mlp_in, mlp_in_bias, mlp_out, mlp_out_bias,
):
    tokens = image_tokens[0]
    rows, width = tokens.shape
    hidden = mlp_in.shape[1]
    chunk = hidden // MLP_STEPS
    vectors = (
        norm1_gain, norm1_bias, norm2_gain, norm2_bias,
        norm3_gain, norm3_bias, mlp_in_bias, mlp_out_bias,
    )
    sizes = [v.shape[0] for v in vectors]
    shard = self_query.shape[0]
    owners = width // shard
    parts = hidden // width
    matrices = (
        self_query, self_key, self_value,
        self_output, cross_query, cross_key, cross_value, cross_output,
    )
    orders = halving_orders()
    spread = [order[::-1] for order in orders]
    down_shard = mlp_out.shape[0]
    first_pack = jnp.concatenate([*matrices[:3], pack_vectors(vectors)], axis=0)
    cross_pack = jnp.concatenate([mlp_out, *matrices[3:]], axis=0)
    up_pack = jnp.concatenate(
        [mlp_in[:, width * k : width * (k + 1)] for k in range(parts)], axis=0
    )
    first, text_full = alone(
        Gather(
            [
                (first_pack, row_pieces(first_pack.shape[0], 6), spread),
                (text_states[0], [(0, text_states.shape[1])], [cube_dims(("narrow",))]),
            ]
        ),
        1,
    )
    text_full = text_full.reshape(-1, width)

    def matrix(source, index):
        if shard % 16 == 0:
            spec = pl.BlockSpec(
                (owners, shard, width), lambda *_: (0, index, 0), pipeline_mode=pl.Buffered(1)
            )
            return source, spec
        taken = source[:, shard * index : shard * (index + 1)].reshape(1, width, width)
        return taken, whole_block(taken.shape)

    def columns(source, index):
        if shard % 16 == 0:
            return source, pl.BlockSpec((owners, shard, 128), lambda p: (0, index, p))
        taken = source[:, shard * index : shard * (index + 1)].reshape(1, width, width)
        return taken, pl.BlockSpec((1, width, 128), lambda p: (0, 0, p))

    weights_one = [matrix(first, k) for k in range(3)]
    gain_one, bias_one, gain_two, bias_two, gain_three, bias_three, up_bias, down_bias = (
        take_vectors(first[:, 3 * shard :], sizes)
    )
    mask = (text_segments[0] == image_segment[0, 0]).astype(jnp.int32).reshape(-1, 1)

    (normed_one, queries, keys, values, mixed_self, sums_self), (second,) = attend(
        tokens, gain_one, bias_one, [columns(first, k) for k in range(3)],
        Gather([(cross_pack, row_pieces(cross_pack.shape[0], 6), spread)]),
        (1, 2, 3, 5), 2,
    )
    places = down_shard // shard
    weights_two = [matrix(second, places + k) for k in range(5)]
    (x1, h2, q2, a2, x2, h3, k2, v2), (third,) = middle(
        tokens, mixed_self, text_full, mask, (gain_two, bias_two, gain_three, bias_three), weights_two,
        Gather([(up_pack, row_pieces(up_pack.shape[0], 6), spread)]),
        (1, 2), 3,
    )
    if shard % 16 == 0:
        per = width // chunk
        up = (third, pl.BlockSpec((owners, shard, chunk), lambda c: (0, c // per, c % per)))
        down = (
            second,
            pl.BlockSpec((chunk // down_shard, down_shard, width), lambda c: (c, 0, 0)),
        )
    else:
        taken = [
            third[:, shard * k : shard * (k + 1)].reshape(1, width, width) for k in range(parts)
        ]
        up = (
            jnp.concatenate(taken, axis=2),
            pl.BlockSpec((1, width, chunk), lambda c: (0, 0, c)),
        )
        down = (
            second[:, :down_shard].reshape(1, hidden, width),
            pl.BlockSpec((1, chunk, width), lambda c: (0, c, 0)),
        )
    halves = row_pieces(shard, 2)
    near = 2 if shard % 16 == 0 else 0
    (
        block_out, dx2, grad_up_bias, grad_gain_three, grad_bias_three, grad_down_bias,
        grad_down, grad_up, near_sums,
    ) = mlp(
        x2, h3, out_grad[0], gain_three, up, up_bias, down, down_bias, near, halves, orders, 4
    )
    down_runs = row_pieces(down_shard, 8)
    cut = 6 if len(down_runs) == 8 else 1
    (
        dx1, grad_mixed, grad_self_out, grad_cross_query, grad_cross_key, grad_cross_value,
        grad_cross_out, text_term, grad_gain_two, grad_bias_two,
    ), (down_first,) = middle_back(
        dx2, x1, mixed_self, h2, q2, a2, k2, v2, text_full, mask, gain_two, weights_two,
        Scatter([(grad_down, down_runs[:cut], orders)]), (1,), 5,
    )
    groups = [(g, halves, orders) for g in grad_up]
    groups += [(grad_down, down_runs[cut:], orders)] if down_runs[cut:] else []
    groups += [
        (g, halves, orders)
        for g in (grad_self_out, grad_cross_query, grad_cross_key, grad_cross_value, grad_cross_out)
    ]
    groups.append((text_term, [(0, text_states.shape[1])], [cube_dims(("narrow",))]))
    (grad_queries, grad_keys, grad_values, *self_weights), sums = attend_back(
        queries, keys, values, grad_mixed, sums_self, normed_one, Scatter(groups), (1, 5), 6
    )
    grad_up = jnp.concatenate([*near_sums, *sums[: parts - near]], axis=1)
    grad_down = jnp.concatenate([down_first, *sums[parts - near : -6]], axis=0)
    (
        grad_self_out, grad_cross_query, grad_cross_key, grad_cross_value, grad_cross_out, text_grad,
    ) = sums[-6:]
    self_terms = (grad_queries, grad_keys, grad_values)
    others = jnp.concatenate(
        [
            jnp.zeros((2, width), jnp.float32),
            grad_gain_two, grad_bias_two, grad_gain_three, grad_bias_three, grad_down_bias,
            grad_up_bias.reshape(-1, width),
        ],
        axis=0,
    )
    others = jnp.pad(others, ((0, -others.shape[0] % 8), (0, 0)))
    (image_grad, vector_sums), (grad_self_query, grad_self_key, grad_self_value) = first_back(
        tokens, dx1, gain_one, others, weights_one, self_terms,
        Scatter([(g, halves, orders) for g in self_weights]), (1,), 7,
    )
    place = lax.axis_index(AXES)
    flat = vector_sums.reshape(-1)
    rows_of = (0, 1, 2, 3, 4, 5, 7, 6)
    vector_grads = [
        lax.dynamic_slice_in_dim(flat, row * width + place * size, size)
        for row, size in zip(rows_of, sizes)
    ]
    return (
        block_out[None], image_grad[None], text_grad[None],
        vector_grads[0], vector_grads[1],
        grad_self_query, grad_self_key, grad_self_value, grad_self_out,
        vector_grads[2], vector_grads[3],
        grad_cross_query, grad_cross_key, grad_cross_value, grad_cross_out,
        vector_grads[4], vector_grads[5],
        grad_up, vector_grads[6], grad_down, vector_grads[7],
    )


def solution(mesh):
    placed = (
        P(("wide", "narrow"), None, None),
        P("wide", "narrow", None),
        P("wide", None),
        P("wide", "narrow"),
        P(("wide", "narrow"), None, None),
        P(("wide", "narrow")),
        P(("wide", "narrow")),
        P(("wide", "narrow"), None),
        P(("wide", "narrow"), None),
        P(("wide", "narrow"), None),
        P(("wide", "narrow"), None),
        P(("wide", "narrow")),
        P(("wide", "narrow")),
        P(("wide", "narrow"), None),
        P(("wide", "narrow"), None),
        P(("wide", "narrow"), None),
        P(("wide", "narrow"), None),
        P(("wide", "narrow")),
        P(("wide", "narrow")),
        P(("wide", "narrow"), None),
        P(("wide", "narrow")),
        P(("wide", "narrow"), None),
        P(("wide", "narrow")),
    )
    return jax.shard_map(
        on_device,
        mesh=mesh,
        in_specs=placed,
        out_specs=(
            P(("wide", "narrow"), None, None),
            P(("wide", "narrow"), None, None),
            P("wide", "narrow", None),
            P(("wide", "narrow")),
            P(("wide", "narrow")),
            P(("wide", "narrow"), None),
            P(("wide", "narrow"), None),
            P(("wide", "narrow"), None),
            P(("wide", "narrow"), None),
            P(("wide", "narrow")),
            P(("wide", "narrow")),
            P(("wide", "narrow"), None),
            P(("wide", "narrow"), None),
            P(("wide", "narrow"), None),
            P(("wide", "narrow"), None),
            P(("wide", "narrow")),
            P(("wide", "narrow")),
            P(("wide", "narrow"), None),
            P(("wide", "narrow")),
            P(("wide", "narrow"), None),
            P(("wide", "narrow")),
        ),
        check_vma=False,
    )
```

```python
import functools
import math

import jax
import jax.numpy as jnp
from jax import lax
from jax.experimental import pallas as pl
from jax.experimental.pallas import tpu as pltpu
from jax.sharding import PartitionSpec as P

HEAD_DIM = 64
TILE = 256
BF16 = jnp.bfloat16
VMEM_LIMIT = 60 * 1024 * 1024
MLP_STEPS = 8

EPSILON = 1e-05
NEGATIVE = -1e30

AXES = ("wide", "narrow")


def axis_bits(axis):
    return lax.axis_size(axis).bit_length() - 1


def pack_vectors(vectors):
    room = 1024
    placed = [
        jnp.pad(v.astype(jnp.float32), (128 * k, room - 128 * k - v.shape[0]))
        for k, v in enumerate(vectors)
    ]
    return sum(placed).reshape(-1, 128)


def nn(a, b):
    return lax.dot_general(a, b, (((1,), (0,)), ((), ())), preferred_element_type=jnp.float32)


def nt(a, b):
    return lax.dot_general(a, b, (((1,), (1,)), ((), ())), preferred_element_type=jnp.float32)


def tn(a, b):
    return lax.dot_general(a, b, (((0,), (0,)), ((), ())), preferred_element_type=jnp.float32)


def standardize(values):
    center = jnp.mean(values, axis=-1, keepdims=True)
    offset = values - center
    rate = lax.rsqrt(jnp.mean(offset * offset, axis=-1, keepdims=True) + EPSILON)
    return offset * rate, rate


def norm_back(standard, rate, gain, grad):
    scaled = grad * gain
    return rate * (
        scaled
        - jnp.mean(scaled, axis=-1, keepdims=True)
        - standard * jnp.mean(scaled * standard, axis=-1, keepdims=True)
    )


def column_sum(values):
    return jnp.sum(values, axis=0, keepdims=True)


def head_lanes(block, head):
    lane = lax.broadcasted_iota(jnp.int32, block.shape, 1)
    inside = (lane >= HEAD_DIM) if head else (lane < HEAD_DIM)
    return jnp.where(inside, block, jnp.zeros_like(block))


def whole_block(shape):
    zeros = (0,) * len(shape)
    return pl.BlockSpec(shape, lambda *_: zeros, pipeline_mode=pl.Buffered(1))


def params(**extra):
    return pltpu.CompilerParams(vmem_limit_bytes=VMEM_LIMIT, **extra)


def attend_kernel(
    x_ref, vectors_ref, wq_ref, wk_ref, wv_ref, h_ref, q_ref, k_ref, v_ref, o_ref, sums_ref,
    hook,
):
    rows = x_ref.shape[0]

    @pl.when(pl.program_id(0) == 0)
    def _():
        for start in range(0, rows, TILE):
            at = slice(start, start + TILE)
            standard, _ = standardize(x_ref[at, :].astype(jnp.float32))
            h_ref[at, :] = (standard * vectors_ref[0:1, :] + vectors_ref[1:2, :]).astype(BF16)

    weights = jnp.concatenate([w[...] for w in (wq_ref, wk_ref, wv_ref)], axis=1)
    mapped = nn(h_ref[...], weights).astype(BF16)
    q_ref[...] = mapped[:, :128]
    k_ref[...] = mapped[:, 128:256]
    v_ref[...] = mapped[:, 256:]
    flipped = v_ref[...].T
    for start in range(0, rows, TILE):
        span = start + TILE
        queries = q_ref[start:span, :] * (HEAD_DIM**-0.5)
        keys = k_ref[:span, :]
        mixed, sums = [], []
        for head in range(2):
            scores = nt(keys, head_lanes(queries, head))
            key_at = lax.broadcasted_iota(jnp.int32, (TILE, TILE), 0)
            query_at = lax.broadcasted_iota(jnp.int32, (TILE, TILE), 1)
            corner = jnp.where(key_at <= query_at, scores[start:], NEGATIVE)
            scores = jnp.concatenate([scores[:start], corner], axis=0) if start else corner
            top = jnp.max(scores, axis=0, keepdims=True)
            powers = jnp.exp(scores - top)
            total = jnp.sum(powers, axis=0, keepdims=True)
            part = nn(flipped[HEAD_DIM * head : HEAD_DIM * (head + 1), :span], powers.astype(BF16))
            mixed.append(part * (1.0 / total))
            sums.append(top + jnp.log(total))
        o_ref[start:span, :] = jnp.concatenate(mixed, axis=0).T.astype(BF16)
        sums_ref[0, :, start:span] = jnp.concatenate(sums, axis=0)


def attend(tokens, vectors, weights, work, schedule, collective_id):
    rows, width = tokens.shape
    pairs = width // 128
    block = pl.BlockSpec((rows, 128), lambda p: (0, p))
    like = jax.ShapeDtypeStruct(tokens.shape, BF16)
    results = pl.pallas_call(
        beside(attend_kernel, work, (5, 6, 0), schedule, pairs),
        grid=(pairs,),
        in_specs=[whole_block(tokens.shape), whole_block(vectors.shape)]
        + [pl.BlockSpec((width, 128), lambda p: (0, p))] * 3
        + work.in_specs,
        out_specs=[whole_block(tokens.shape)]
        + [block] * 4
        + [pl.BlockSpec((1, 2, rows), lambda p: (p, 0, 0))]
        + work.out_specs,
        out_shape=[like] * 5
        + [jax.ShapeDtypeStruct((pairs, 2, rows), jnp.float32)]
        + work.out_shape,
        scratch_shapes=work.scratch,
        compiler_params=params(collective_id=collective_id, has_side_effects=True),
        name="self_attend",
    )(tokens, vectors, *weights, *work.arrays)
    return results[:6], work.results(results[6:])


def attend_back_kernel(
    q_ref, k_ref, v_ref, da_ref, sums_ref, h_ref, dk2_ref, dv2_ref, text_ref, ck_ref, cv_ref,
    dq_ref, dk_ref, dv_ref, dwq_ref, dwk_ref, dwv_ref, dck_ref, dcv_ref, dtext_ref,
    dk_sum, dv_sum, h_flip, hook,
):
    rows, width = q_ref.shape

    @pl.when(pl.program_id(0) == 0)
    def _():
        h_flip[...] = h_ref[...].T
        dck_ref[...] = tn(text_ref[...], dk2_ref[...]).astype(BF16)
        dcv_ref[...] = tn(text_ref[...], dv2_ref[...]).astype(BF16)
        dtext_ref[...] = nt(dk2_ref[...], ck_ref[...]) + nt(dv2_ref[...], cv_ref[...])

    flipped = k_ref[...].T
    for start in reversed(range(0, rows, TILE)):
        if start == TILE:
            hook(1)
        span = start + TILE
        queries = q_ref[start:span, :] * (HEAD_DIM**-0.5)
        grads = da_ref[start:span, :]
        keys = k_ref[:span, :]
        values = v_ref[:span, :]
        parts = []
        for head in range(2):
            own_queries = head_lanes(queries, head)
            own_grads = head_lanes(grads, head)
            scores = nt(keys, own_queries)
            key_at = lax.broadcasted_iota(jnp.int32, (TILE, TILE), 0)
            query_at = lax.broadcasted_iota(jnp.int32, (TILE, TILE), 1)
            corner = jnp.where(key_at <= query_at, scores[start:], NEGATIVE)
            scores = jnp.concatenate([scores[:start], corner], axis=0) if start else corner
            probs = jnp.exp(scores - sums_ref[0, head : head + 1, start:span])
            grad_probs = nt(values, own_grads)
            inner = jnp.sum(probs * grad_probs, axis=0, keepdims=True)
            grad_scores = (probs * (grad_probs - inner)).astype(BF16)
            value_term = nn(probs.astype(BF16), own_grads)
            key_term = nn(grad_scores, own_queries)
            if span == rows and head == 0:
                dv_sum[...] = value_term
                dk_sum[...] = key_term
            else:
                dv_sum[:span, :] += value_term
                dk_sum[:span, :] += key_term
            parts.append(nn(flipped[HEAD_DIM * head : HEAD_DIM * (head + 1), :span], grad_scores))
        dq = jnp.concatenate(parts, axis=0).T * (HEAD_DIM**-0.5)
        dq_ref[start:span, :] = dq.astype(BF16)
    dk_ref[...] = dk_sum[...].astype(BF16)
    dv_ref[...] = dv_sum[...].astype(BF16)
    grads = jnp.concatenate([dq_ref[...], dk_ref[...], dv_ref[...]], axis=1)
    weights = nn(h_flip[...], grads).astype(BF16)
    dwq_ref[...] = weights[:, :128]
    dwk_ref[...] = weights[:, 128:256]
    dwv_ref[...] = weights[:, 256:]


def attend_back(queries, keys, values, grads, sums, normed, cross, work, schedule, collective_id):
    rows, width = queries.shape
    steps = width // 128
    block = pl.BlockSpec((rows, 128), lambda p: (0, p))
    results = pl.pallas_call(
        beside(attend_back_kernel, work, (11, 9, 3), schedule, steps),
        grid=(steps,),
        in_specs=[block] * 4
        + [pl.BlockSpec((1, 2, rows), lambda p: (p, 0, 0)), whole_block(normed.shape)]
        + [whole_block(c.shape) for c in cross]
        + work.in_specs,
        out_specs=[block] * 6
        + [whole_block((width, width))] * 2
        + [whole_block(cross[2].shape)]
        + work.out_specs,
        out_shape=[jax.ShapeDtypeStruct(queries.shape, BF16)] * 3
        + [jax.ShapeDtypeStruct((width, width), BF16)] * 5
        + [jax.ShapeDtypeStruct(cross[2].shape, jnp.float32)]
        + work.out_shape,
        scratch_shapes=[pltpu.VMEM((rows, 128), jnp.float32)] * 2
        + [pltpu.VMEM((width, rows), BF16)]
        + work.scratch,
        compiler_params=params(collective_id=collective_id, has_side_effects=True),
        name="self_attend_back",
    )(queries, keys, values, grads, sums, normed, *cross, *work.arrays)
    return results[:9], work.results(results[9:])


def gelu_both(values):
    phi = 0.5 + 0.5 * lax.erf(values * (0.5**0.5))
    density = jnp.exp(-0.5 * values * values) * ((2.0 * math.pi) ** -0.5)
    return values * phi, phi + values * density


def mlp_kernel(
    near, far, pace, work, x_ref, h_ref, g_ref, vectors_ref, up_ref, ub_ref, down_ref,
    out_ref, dx_ref, dub_ref, dgain_ref, dbias_ref, gsum_ref, ddown_ref, *refs,
):
    far_refs, refs = refs[:far], refs[far:]
    sums, refs = refs[:near], refs[near:]
    out_sum, dh_sum, h_flip, act, grad_act = refs[:5]
    near_refs, refs = refs[5 : 5 + near], refs[5 + near :]
    step, steps = pl.program_id(0), pl.num_programs(0)
    rows = h_ref.shape[0]
    parts = near + far
    per = MLP_STEPS // parts
    moving = work.bind(near_refs, sums, refs) if near else None

    @pl.when(step == 0)
    def _():
        if near:
            greet_partners()
        h_flip[...] = h_ref[...].T
        out_sum[...] = x_ref[...] + vectors_ref[7:8, :]
        dh_sum[...] = jnp.zeros_like(dh_sum)

    left, due = [], {}
    for part in range(near):
        pieces = [k for k, p in enumerate(work.pieces) if p[0][0] == part]
        for at in range(-1, work.ticks):
            place = 2 * per * (part + 1) + pace[at + 1]
            if place < 2 * MLP_STEPS:
                due.setdefault(place, []).append((at, pieces))
            else:
                left.append((at, pieces))

    def move(half):
        for place in due:
            if place % 2 == half:

                @pl.when(step == place // 2)
                def _(place=place):
                    for at, pieces in due[place]:
                        tick(moving, at, pieces)

    move(0)
    up = up_ref[...]
    down = down_ref[...]
    bias_sum = jnp.zeros_like(dub_ref)
    for start in range(0, rows, TILE):
        at = slice(start, start + TILE)
        hidden, slope = gelu_both(nn(h_ref[at, :], up) + ub_ref[...])
        act[at, :] = hidden.astype(BF16)
        grad_pre = (nt(g_ref[at, :], down) * slope).astype(BF16)
        grad_act[at, :] = grad_pre
        bias_sum += column_sum(grad_pre.astype(jnp.float32))
        out_sum[at, :] += nn(act[at, :], down)
        dh_sum[at, :] += nt(grad_pre, up)
    dub_ref[...] = bias_sum
    move(1)
    grad_up = nn(h_flip[...], grad_act[...]).astype(BF16)
    chunk = grad_up.shape[1]
    for part, ref in enumerate(far_refs):

        @pl.when(step // per == near + part)
        def _(ref=ref):
            ref[...] = grad_up

    for place in range(near * per):

        @pl.when(step == place)
        def _(place=place):
            ref = near_refs[place // per]
            first = chunk * (place % per)
            ref[..., first : first + chunk] = grad_up.reshape(ref.shape[:-1] + (chunk,))

    ddown_ref[...] = tn(act[...], g_ref[...]).astype(BF16)

    @pl.when(step == steps - 1)
    def _():
        gain_sum = jnp.zeros_like(dgain_ref)
        grad_sum = jnp.zeros_like(dbias_ref)
        tail_sum = jnp.zeros_like(gsum_ref)
        for start in range(0, rows, TILE):
            at = slice(start, start + TILE)
            out_ref[at, :] = out_sum[at, :].astype(BF16)
            standard, rate = standardize(x_ref[at, :])
            grad = dh_sum[at, :]
            tail = g_ref[at, :].astype(jnp.float32)
            dx_ref[at, :] = tail + norm_back(standard, rate, vectors_ref[4:5, :], grad)
            gain_sum += column_sum(grad * standard)
            grad_sum += column_sum(grad)
            tail_sum += column_sum(tail)
        dgain_ref[...] = gain_sum
        dbias_ref[...] = grad_sum
        gsum_ref[...] = tail_sum
        for at, pieces in left:
            tick(moving, at, pieces)
        if near:
            settle(moving)


def mlp(x, h, g, vectors, up, up_bias, down, near, pace, orders, collective_id):
    rows, width = x.shape
    hidden = up_bias.shape[1]
    chunk = hidden // MLP_STEPS
    f32 = jnp.float32
    row = (1, width)
    parts = hidden // width
    per = width // chunk
    lead = (2,) * len(cube_dims())
    block = lead + (width >> len(lead), width)
    source = jax.ShapeDtypeStruct(block, BF16)
    work = Scatter([(source, orders, 1)] * near, near=True) if near else None
    far = parts - near
    pace = [*pace, *range(pace[-1] + 1, pace[-1] + 1 + len(cube_dims()))]
    results = pl.pallas_call(
        functools.partial(mlp_kernel, near, far, pace, work),
        grid=(MLP_STEPS,),
        in_specs=[
            whole_block(x.shape), whole_block(h.shape), whole_block(g.shape), whole_block(vectors.shape),
            pl.BlockSpec((width, chunk), lambda c: (0, c)),
            pl.BlockSpec((1, chunk), lambda c: (0, c)),
            pl.BlockSpec((chunk, width), lambda c: (c, 0)),
        ],
        out_specs=[
            whole_block(x.shape), whole_block(x.shape),
            pl.BlockSpec((1, chunk), lambda c: (0, c)),
            whole_block(row), whole_block(row), whole_block(row),
            pl.BlockSpec((chunk, width), lambda c: (c, 0)),
        ]
        + [
            pl.BlockSpec((width, chunk), lambda c, k=k: (0, jnp.clip(c - per * k, 0, per - 1)))
            for k in range(near, parts)
        ]
        + (work.out_specs if near else []),
        out_shape=[
            jax.ShapeDtypeStruct(x.shape, BF16), jax.ShapeDtypeStruct(x.shape, f32),
            jax.ShapeDtypeStruct((1, hidden), f32),
            jax.ShapeDtypeStruct(row, f32), jax.ShapeDtypeStruct(row, f32), jax.ShapeDtypeStruct(row, f32),
            jax.ShapeDtypeStruct((hidden, width), BF16),
        ]
        + [jax.ShapeDtypeStruct((width, width), BF16)] * far
        + (work.out_shape if near else []),
        scratch_shapes=[
            pltpu.VMEM(x.shape, f32), pltpu.VMEM(x.shape, f32), pltpu.VMEM((width, rows), BF16),
            pltpu.VMEM((rows, chunk), BF16), pltpu.VMEM((rows, chunk), BF16),
        ]
        + [pltpu.VMEM(block, BF16)] * near
        + (work.scratch if near else []),
        compiler_params=params(collective_id=collective_id, has_side_effects=True) if near else params(),
        name="mlp_both_ways",
    )(x, h, g, vectors, up, up_bias, down)
    sums = work.results(results[7 + far :]) if near else []
    return *results[:7], results[7 : 7 + far], sums


def stack_heads(pair):
    return jnp.concatenate([head_lanes(pair, 0), head_lanes(pair, 1)], axis=0)


def by_head(stacked):
    return stacked.reshape(2, stacked.shape[0] // 2, stacked.shape[1])


def caption_probs(keys, queries, mask):
    scores = by_head(jnp.where(mask != 0, nt(keys, queries), NEGATIVE))
    powers = jnp.exp(scores - jnp.max(scores, axis=1, keepdims=True))
    return powers * (1.0 / jnp.sum(powers, axis=1, keepdims=True))


def middle_kernel(
    x_ref, a_ref, text_ref, mask_ref, vectors_ref,
    wo_ref, cq_ref, ck_ref, cv_ref, co_ref,
    x1_ref, h2_ref, q2_ref, a2_ref, x2_ref, h3_ref, k2_ref, v2_ref, keys, values_flip,
    hook,
):
    @pl.when(pl.program_id(0) == 0)
    def _():
        k2_ref[...] = nn(text_ref[...], ck_ref[...]).astype(BF16)
        v2_ref[...] = nn(text_ref[...], cv_ref[...]).astype(BF16)
        for pair in range(keys.shape[0]):
            at = slice(128 * pair, 128 * (pair + 1))
            keys[pair] = stack_heads(k2_ref[:, at])
            values_flip[pair] = stack_heads(v2_ref[:, at]).T

    after_self = x_ref[...].astype(jnp.float32) + nn(a_ref[...], wo_ref[...])
    x1_ref[...] = after_self
    standard, _ = standardize(after_self)
    normed = (standard * vectors_ref[2:3, :] + vectors_ref[3:4, :]).astype(BF16)
    h2_ref[...] = normed
    q2_ref[...] = nn(normed, cq_ref[...]).astype(BF16)
    mask = mask_ref[...]
    for pair in range(q2_ref.shape[1] // 128):
        at = slice(128 * pair, 128 * (pair + 1))
        queries = q2_ref[:, at] * (HEAD_DIM**-0.5)
        probs = caption_probs(keys[pair], queries, mask).astype(BF16)
        mixed = nn(values_flip[pair], probs.reshape(-1, probs.shape[2]))
        a2_ref[:, at] = mixed.T.astype(BF16)
    hook(1)
    after_cross = after_self + nn(a2_ref[...], co_ref[...])
    x2_ref[...] = after_cross
    standard, _ = standardize(after_cross)
    h3_ref[...] = (standard * vectors_ref[4:5, :] + vectors_ref[5:6, :]).astype(BF16)


def middle(tokens, mixed, text, mask, vectors, weights, work, schedule, collective_id):
    rows, width = tokens.shape
    slots = text.shape[0]
    tile = pl.BlockSpec((TILE, width), lambda i: (i, 0))
    f32 = jnp.float32
    like = lambda dtype: jax.ShapeDtypeStruct(tokens.shape, dtype)
    results = pl.pallas_call(
        beside(middle_kernel, work, (10, 8, 2), schedule, rows // TILE),
        grid=(rows // TILE,),
        in_specs=[
            tile, tile, whole_block(text.shape), whole_block(mask.shape),
            whole_block(vectors.shape), *[whole_block(w.shape) for w in weights], *work.in_specs,
        ],
        out_specs=[tile] * 6 + [whole_block(text.shape)] * 2 + work.out_specs,
        out_shape=[like(f32), like(BF16), like(BF16), like(BF16), like(f32), like(BF16)]
        + [jax.ShapeDtypeStruct(text.shape, BF16)] * 2
        + work.out_shape,
        scratch_shapes=[
            pltpu.VMEM((width // 128, 2 * slots, 128), BF16),
            pltpu.VMEM((width // 128, 128, 2 * slots), BF16),
        ]
        + work.scratch,
        compiler_params=params(collective_id=collective_id, has_side_effects=True),
        name="output_and_cross",
    )(tokens, mixed, text, mask, vectors, *weights, *work.arrays)
    return results[:8], work.results(results[8:])


def middle_back_kernel(
    dx2_ref, x1_ref, a1_ref, h2_ref, q2_ref, a2_ref, k2_ref, v2_ref, mask_ref, vectors_ref,
    wo_ref, cq_ref, co_ref,
    dx1_ref, da1_ref, dwo_ref, dcq_ref, dco_ref, dk2_ref, dv2_ref, dgain_ref, dbias_ref,
    wo_sum, cq_sum, co_sum, dk_sum, dv_sum, dq2, keys, keys_flip, values,
    hook,
):
    step, steps = pl.program_id(0), pl.num_programs(0)
    pairs = keys.shape[0]
    slots = k2_ref.shape[0]

    @pl.when(step == 0)
    def _():
        for ref in (wo_sum, cq_sum, co_sum, dk_sum, dv_sum, dgain_ref, dbias_ref):
            ref[...] = jnp.zeros_like(ref)
        for pair in range(pairs):
            at = slice(128 * pair, 128 * (pair + 1))
            keys[pair] = stack_heads(k2_ref[:, at])
            keys_flip[pair] = keys[pair].T
            values[pair] = stack_heads(v2_ref[:, at])

    grad_out = dx2_ref[...].astype(BF16)
    co_sum[...] += tn(a2_ref[...], grad_out)
    grad_mixed = nt(grad_out, co_ref[...]).astype(BF16)
    mask = mask_ref[...]
    for pair in range(pairs):
        at = slice(128 * pair, 128 * (pair + 1))
        queries = q2_ref[:, at] * (HEAD_DIM**-0.5)
        grads = grad_mixed[:, at]
        probs = caption_probs(keys[pair], queries, mask)
        grad_probs = by_head(nt(values[pair], grads))
        inner = jnp.sum(probs * grad_probs, axis=1, keepdims=True)
        grad_scores = (probs * (grad_probs - inner)).astype(BF16).reshape(2 * slots, -1)
        dv_sum[pair] += nn(probs.astype(BF16).reshape(2 * slots, -1), grads)
        dk_sum[pair] += nn(grad_scores, queries)
        dq2[:, at] = (nn(keys_flip[pair], grad_scores).T * (HEAD_DIM**-0.5)).astype(BF16)
    hook(1)
    cq_sum[...] += tn(h2_ref[...], dq2[...])
    grad_normed = nt(dq2[...], cq_ref[...])
    standard, rate = standardize(x1_ref[...])
    grad_after = dx2_ref[...] + norm_back(standard, rate, vectors_ref[2:3, :], grad_normed)
    dgain_ref[...] += column_sum(grad_normed * standard)
    dbias_ref[...] += column_sum(grad_normed)
    dx1_ref[...] = grad_after
    grad_self = grad_after.astype(BF16)
    wo_sum[...] += tn(a1_ref[...], grad_self)
    da1_ref[...] = nt(grad_self, wo_ref[...]).astype(BF16)

    @pl.when(step == steps - 1)
    def _():
        dwo_ref[...] = wo_sum[...].astype(BF16)
        dcq_ref[...] = cq_sum[...].astype(BF16)
        dco_ref[...] = co_sum[...].astype(BF16)
        for pair in range(pairs):
            at = slice(128 * pair, 128 * (pair + 1))
            for total, ref in ((dk_sum, dk2_ref), (dv_sum, dv2_ref)):
                upper, lower = total[pair, :slots], total[pair, slots:]
                ref[:, at] = (head_lanes(upper, 0) + head_lanes(lower, 1)).astype(BF16)


def middle_back(
    dx2, x1, a1, h2, q2, a2, k2, v2, mask, vectors, weights, work, schedule, collective_id
):
    rows, width = x1.shape
    slots = k2.shape[0]
    pairs = width // 128
    tile = pl.BlockSpec((TILE, width), lambda i: (i, 0))
    f32 = jnp.float32
    matrix = (width, width)
    results = pl.pallas_call(
        beside(middle_back_kernel, work, (13, 9, 9), schedule, rows // TILE),
        grid=(rows // TILE,),
        in_specs=[tile] * 6
        + [whole_block(v.shape) for v in (k2, v2, mask, vectors, *weights)]
        + work.in_specs,
        out_specs=[tile] * 2
        + [whole_block(matrix)] * 3
        + [whole_block(k2.shape)] * 2
        + [whole_block((1, width))] * 2
        + work.out_specs,
        out_shape=[jax.ShapeDtypeStruct(x1.shape, f32), jax.ShapeDtypeStruct(x1.shape, BF16)]
        + [jax.ShapeDtypeStruct(matrix, BF16)] * 3
        + [jax.ShapeDtypeStruct(k2.shape, BF16)] * 2
        + [jax.ShapeDtypeStruct((1, width), f32)] * 2
        + work.out_shape,
        scratch_shapes=[pltpu.VMEM(matrix, f32)] * 3
        + [pltpu.VMEM((pairs, 2 * slots, 128), f32)] * 2
        + [
            pltpu.VMEM((TILE, width), BF16),
            pltpu.VMEM((pairs, 2 * slots, 128), BF16),
            pltpu.VMEM((pairs, 128, 2 * slots), BF16),
            pltpu.VMEM((pairs, 2 * slots, 128), BF16),
        ]
        + work.scratch,
        compiler_params=params(collective_id=collective_id, has_side_effects=True),
        name="cross_back",
    )(dx2, x1, a1, h2, q2, a2, k2, v2, mask, vectors, *weights, *work.arrays)
    return results[:9], work.results(results[9:])


def first_back_kernel(
    work, schedule, steps, x_ref, dx1_ref, given_ref, vectors_ref, wq_ref, wk_ref, wv_ref, dq_ref, dk_ref, dv_ref,
    *refs,
):
    n, m = len(work.in_specs), len(work.out_specs)
    sources, (dx_ref, vector_sum_ref), sums = refs[:n], refs[n : n + 2], refs[n + 2 : n + 2 + m]
    stages = len(cube_dims())
    rest = refs[n + 2 + m :]
    doubling = Doubling(rest[0], rest[1 : stages + 1], *rest[stages + 1 : stages + 3])
    halving = work.bind(sources, sums, rest[stages + 3 :])
    step = pl.program_id(0)
    vectors = doubling.buffers[0]

    @pl.when(step == 0)
    def _():
        greet_partners()
        tick(halving, -1)
        vectors[...] = vectors_ref[...]

    for at, place in enumerate(schedule):

        @pl.when(step == place)
        def _(at=at):
            tick(halving, at)

    grad_normed = (
        nt(dq_ref[...], wq_ref[...]) + nt(dk_ref[...], wk_ref[...]) + nt(dv_ref[...], wv_ref[...])
    )
    standard, rate = standardize(x_ref[...].astype(jnp.float32))
    dx_ref[...] = dx1_ref[...] + norm_back(standard, rate, given_ref[0:1, :], grad_normed)
    vectors[0:1, :] += column_sum(grad_normed * standard)
    vectors[1:2, :] += column_sum(grad_normed)

    @pl.when(step == steps - 1)
    def _():
        doubling.step(-1)
        for at in range(max(stages, work.ticks)):
            if at < stages:
                doubling.step(at)
            if len(schedule) + at < work.ticks:
                tick(halving, len(schedule) + at)
        vector_sum_ref[...] = doubling.buffers[-1][...]
        doubling.settle()
        settle(halving)


def first_back(tokens, dx1, given, vectors, weights, grads, work, schedule, collective_id):
    rows, width = tokens.shape
    steps = rows // TILE
    tile = pl.BlockSpec((TILE, width), lambda i: (i, 0))
    f32 = jnp.float32
    results = pl.pallas_call(
        functools.partial(first_back_kernel, work, schedule, steps),
        grid=(steps,),
        in_specs=[tile] * 2
        + [whole_block(given.shape), whole_block(vectors.shape)]
        + [whole_block(w.shape) for w in weights]
        + [tile] * 3
        + work.in_specs,
        out_specs=[tile, whole_block(vectors.shape)] + work.out_specs,
        out_shape=[
            jax.ShapeDtypeStruct(tokens.shape, f32),
            jax.ShapeDtypeStruct(vectors.shape, f32),
        ]
        + work.out_shape,
        scratch_shapes=doubling_scratch(vectors.shape) + work.scratch,
        compiler_params=params(collective_id=collective_id, has_side_effects=True),
        name="self_norm_back",
    )(tokens, dx1, given, vectors, *weights, *grads, *work.arrays)
    return results[:2], work.results(results[2:])


def hand_over_kernel(groups, *refs):
    ins, outs = refs[: sum(groups)], refs[sum(groups) :]
    at = 0
    for count, out in zip(groups, outs):
        width = out.shape[1] // count
        for part in range(count):
            out[:, width * part : width * (part + 1)] = ins[at + part][...]
        at += count


def hand_over(groups):
    arrays = [a for group in groups for a in group]
    return pl.pallas_call(
        functools.partial(hand_over_kernel, [len(group) for group in groups]),
        in_specs=[pl.BlockSpec(memory_space=pltpu.VMEM)] * len(arrays),
        out_specs=[pl.BlockSpec(memory_space=pltpu.VMEM)] * len(groups),
        out_shape=[
            jax.ShapeDtypeStruct((g[0].shape[0], sum(a.shape[1] for a in g)), g[0].dtype) for g in groups
        ],
        compiler_params=params(),
        name="hand_over",
    )(*arrays)


def cube_dims(axes=AXES):
    return [(axis, k) for axis in axes for k in reversed(range(axis_bits(axis)))]


def bits_of(dims):
    return [(lax.axis_index(axis) >> bit) & 1 for axis, bit in dims]


def partner(axis, bit):
    return {axis: lax.axis_index(axis) ^ (1 << bit)}


def halving_orders():
    x, y, near, far = ("narrow", 0), ("narrow", 1), ("wide", 1), ("wide", 2)
    core = ("wide", 0)
    six = (
        (far, x, y, near),
        (near, y, x, far),
        (y, far, x, near),
        (x, near, y, far),
        (x, y, far, near),
        (y, x, near, far),
    )
    rest = [d for d in cube_dims() if d not in (core, x, y, near, far)]
    return [[core, *order, *rest] for order in six]


def greet_partners():
    dims = cube_dims()
    barrier = pltpu.get_barrier_semaphore()
    for axis, bit in dims:
        pl.semaphore_signal(
            barrier, inc=1, device_id=partner(axis, bit), device_id_type=pl.DeviceIdType.MESH
        )
    pl.semaphore_wait(barrier, len(dims))


def runs_of(rows, step=16):
    step = step if rows % step == 0 else rows
    return [(start, step) for start in range(0, rows, step)]


def columns_of(columns, parts=6):
    if columns <= 1024:
        return [(0, columns)]
    cuts = [columns * k // parts // 128 * 128 for k in range(parts)] + [columns]
    return [(a, b - a) for a, b in zip(cuts[:-1], cuts[1:])]


def cut_up(groups):
    pieces = []
    for which, ((rows, columns), orders, rounds) in enumerate(groups):
        for start, size in runs_of(rows):
            for first, width in columns_of(columns):
                k = len(pieces)
                box = (which, slice(start, start + size), slice(first, first + width))
                pieces.append((box, orders[k % len(orders)], k // 6 % rounds))
    return pieces


def tick(mover, at, pieces=None):
    for piece in range(len(mover.pieces)) if pieces is None else pieces:
        _, order, late = mover.pieces[piece]
        stage = at - late
        if 0 <= stage < len(order):
            mover.finish(piece, stage)
        if -1 <= stage < len(order) - 1:
            mover.start(piece, stage + 1)


def settle(mover):
    for piece, (_, order, _) in enumerate(mover.pieces):
        for stage in range(len(order)):
            mover.send(piece, stage).wait_send()


def ticks_of(pieces):
    return max(len(order) + late for _, order, late in pieces)


def places_of(pieces):
    ends = [sum(len(p[1]) for p in pieces[:k]) for k in range(len(pieces) + 1)]
    return ends[:-1], ends[-1]


class Gathering:
    def __init__(self, pieces, dims, sources, outs, scratch):
        self.pieces, self.dims, self.sources, self.outs = pieces, dims, sources, outs
        self.send_sems, self.recv_sems, self.own_sems = scratch
        self.base, _ = places_of(pieces)
        self.ready = set()

    def own(self, piece):
        (which, *box), _, _ = self.pieces[piece]
        there = self.outs[which].at[(*bits_of(self.dims[which]), *box)]
        return pltpu.make_async_copy(self.sources[which].at[tuple(box)], there, self.own_sems.at[piece])

    def send(self, piece, stage):
        (which, *box), order, _ = self.pieces[piece]
        held = order[:stage]
        dims = self.dims[which]
        at = [slice(None) if d in held else b for d, b in zip(dims, bits_of(dims))]
        there = self.outs[which].at[(*at, *box)]
        sem = self.base[piece] + stage
        return pltpu.make_async_remote_copy(
            src_ref=there if stage else self.sources[which].at[tuple(box)],
            dst_ref=there,
            send_sem=self.send_sems.at[sem],
            recv_sem=self.recv_sems.at[sem],
            device_id=partner(*order[stage]),
            device_id_type=pl.DeviceIdType.MESH,
        )

    def start(self, piece, stage):
        if stage == 0:
            self.own(piece).start()
        if stage == 1:
            self.own(piece).wait()
        self.send(piece, stage).start()

    def finish(self, piece, stage):
        self.send(piece, stage).wait_recv()


class Gather:
    def __init__(self, groups):
        self.arrays = [array for array, _, _ in groups]
        self.pieces = cut_up([(array.shape, orders, rounds) for array, orders, rounds in groups])
        self.dims = [[d for d in cube_dims() if d in orders[0]] for _, orders, _ in groups]
        self.ticks = ticks_of(self.pieces)
        _, copies = places_of(self.pieces)
        self.in_specs = [pl.BlockSpec(memory_space=pl.ANY)] * len(groups)
        self.out_specs = self.in_specs
        self.out_shape = [
            jax.ShapeDtypeStruct((2,) * len(d) + a.shape, a.dtype)
            for a, d in zip(self.arrays, self.dims)
        ]
        self.scratch = [pltpu.SemaphoreType.DMA((copies,))] * 2
        self.scratch += [pltpu.SemaphoreType.DMA((len(self.pieces),))]

    def bind(self, sources, outs, scratch):
        return Gathering(self.pieces, self.dims, sources, outs, scratch)

    def results(self, outs):
        return [out.reshape(-1, a.shape[-1]) for out, a in zip(outs, self.arrays)]


class Halving:
    def __init__(self, pieces, firsts, sources, outs, scratch, near=False):
        count = len(pieces)
        self.firsts = firsts
        self.pieces, self.sources, self.outs, self.near = pieces, sources, outs, near
        self.kept, rest = ([], scratch) if near else (scratch[:count], scratch[count:])
        self.base, _ = places_of(pieces)
        self.landed = []
        for _, order, _ in pieces:
            self.landed.append(rest[: len(order)])
            rest = rest[len(order) :]
        self.send_sems, self.recv_sems = rest[:2]
        self.kept_sems = None if near else rest[2]

    def half(self, piece, stage, other):
        (which, rows, columns), order, _ = self.pieces[piece]
        left = [d for d in cube_dims() if d in order[stage:]]
        bit = bits_of([order[stage]])[0]
        at = [(1 - bit if other else bit) if d == order[stage] else slice(None) for d in left]
        if stage == 0:
            first = self.firsts[which]
            at += [slice(first + rows.start, first + rows.stop), columns]
        return tuple(at)

    def before(self, piece, stage):
        return self.sources[self.pieces[piece][0][0]] if stage == 0 else self.landed[piece][stage - 1]

    def send(self, piece, stage):
        sem = self.base[piece] + stage
        return pltpu.make_async_remote_copy(
            src_ref=self.before(piece, stage).at[self.half(piece, stage, True)],
            dst_ref=self.landed[piece][stage],
            send_sem=self.send_sems.at[sem],
            recv_sem=self.recv_sems.at[sem],
            device_id=partner(*self.pieces[piece][1][stage]),
            device_id_type=pl.DeviceIdType.MESH,
        )

    def keep(self, piece):
        source = self.before(piece, 0).at[self.half(piece, 0, False)]
        return pltpu.make_async_copy(source, self.kept[piece], self.kept_sems.at[piece])

    def start(self, piece, stage):
        self.send(piece, stage).start()
        if stage == 0 and not self.near:
            self.keep(piece).start()

    def finish(self, piece, stage):
        (which, rows, columns), order, _ = self.pieces[piece]
        self.send(piece, stage).wait_recv()
        if stage == 0 and not self.near:
            self.keep(piece).wait()
        landed = self.landed[piece][stage]
        depth = len(order) - 1 - stage
        if stage == 0 and not self.near:
            other, chosen = self.kept[piece], (slice(None),) * depth
        else:
            other, chosen = self.before(piece, stage), self.half(piece, stage, False)
        if depth == 0:
            total = landed[...].astype(jnp.float32) + other[chosen].astype(jnp.float32)
            self.outs[which][rows, columns] = total
            return

        def add(block, carry):
            at = [(block >> k) & 1 for k in reversed(range(depth))]
            rest = iter(at)
            there = [next(rest, c) if isinstance(c, slice) else c for c in chosen]
            landed[tuple(at)] = landed[tuple(at)] + other[tuple(there)]
            return carry

        lax.fori_loop(0, 1 << depth, add, 0, unroll=min(4, 1 << depth))


class Scatter:
    def __init__(self, groups, near=False):
        self.near = near
        self.arrays, self.firsts, shapes, cuts = [], [], [], []
        for array, orders, rounds, *span in groups:
            columns = array.shape[-1]
            block = (array.size // columns >> len(orders[0]), columns)
            self.arrays.append(array if near else array.reshape((2,) * len(orders[0]) + block))
            first, last = span or (0, block[0])
            self.firsts.append(first)
            shapes.append((last - first, columns))
            cuts.append(((last - first, columns), orders, rounds))
        self.pieces = cut_up(cuts)
        self.ticks = ticks_of(self.pieces)
        like = [
            ((rows.stop - rows.start, columns.stop - columns.start), self.arrays[which].dtype, len(order))
            for (which, rows, columns), order, _ in self.pieces
        ]
        kept = [pltpu.VMEM((2,) * (n - 1) + s, d) for s, d, n in like]
        landed = [pltpu.VMEM((2,) * (n - 1 - k) + s, d) for s, d, n in like for k in range(n)]
        _, copies = places_of(self.pieces)
        self.in_specs = [] if near else [pl.BlockSpec(memory_space=pl.ANY)] * len(groups)
        self.out_specs = [whole_block(s) for s in shapes]
        self.out_shape = [jax.ShapeDtypeStruct(s, jnp.float32) for s in shapes]
        self.scratch = ([] if near else kept) + landed + [pltpu.SemaphoreType.DMA((copies,))] * 2
        if not near:
            self.scratch += [pltpu.SemaphoreType.DMA((len(self.pieces),))]

    def bind(self, sources, outs, scratch):
        return Halving(self.pieces, self.firsts, sources, outs, scratch, self.near)

    def results(self, outs):
        return list(outs)


def beside(kernel, work, counts, schedule, steps):
    n_in, n_out, n_scratch = counts

    def run(*refs):
        cuts = [0, n_in, len(work.in_specs), n_out, len(work.out_specs), n_scratch]
        at = [sum(cuts[: k + 1]) for k in range(len(cuts))]
        ins, sources, outs, sums, own = (refs[a:b] for a, b in zip(at[:-1], at[1:]))
        moving = work.bind(sources, sums, refs[at[-1] :])
        step = pl.program_id(0)

        def hook(place):
            for when in sorted({when for when, where in schedule if where == place}):

                @pl.when(step == when)
                def _(when=when):
                    for at, slot in enumerate(schedule):
                        if slot == (when, place):
                            tick(moving, at)

        @pl.when(step == 0)
        def _():
            greet_partners()
            tick(moving, -1)

        hook(0)
        kernel(*ins, *outs, *own, hook=hook)

        @pl.when(step == steps - 1)
        def _():
            for at in range(len(schedule), work.ticks):
                tick(moving, at)
            settle(moving)

    return run


def alone_kernel(work, *refs):
    n, m = len(work.in_specs), len(work.out_specs)
    moving = work.bind(refs[:n], refs[n : n + m], refs[n + m :])
    greet_partners()
    for at in range(-1, work.ticks):
        tick(moving, at)
    settle(moving)


def alone(work, collective_id):
    outs = pl.pallas_call(
        functools.partial(alone_kernel, work),
        in_specs=work.in_specs,
        out_specs=work.out_specs,
        out_shape=work.out_shape,
        scratch_shapes=work.scratch,
        compiler_params=params(collective_id=collective_id, has_side_effects=True),
        name="gather_weights",
    )(*work.arrays)
    return work.results(outs)


class Doubling:
    def __init__(self, source, landed, send_sems, recv_sems):
        self.buffers = [source, *landed]
        self.send_sems, self.recv_sems = send_sems, recv_sems

    def swap(self, stage):
        return pltpu.make_async_remote_copy(
            src_ref=self.buffers[stage],
            dst_ref=self.buffers[stage + 1],
            send_sem=self.send_sems.at[stage],
            recv_sem=self.recv_sems.at[stage],
            device_id=partner(*cube_dims()[stage]),
            device_id_type=pl.DeviceIdType.MESH,
        )

    def step(self, stage):
        if stage >= 0:
            self.swap(stage).wait_recv()
            self.buffers[stage + 1][...] += self.buffers[stage][...]
        if stage + 2 < len(self.buffers):
            self.swap(stage + 1).start()

    def settle(self):
        for stage in range(len(self.buffers) - 1):
            self.swap(stage).wait_send()


def doubling_scratch(shape):
    stages = len(cube_dims())
    return [pltpu.VMEM(shape, jnp.float32)] * (stages + 1) + [pltpu.SemaphoreType.DMA((stages,))] * 2


def on_device(
    image_tokens, text_states, text_segments, image_segment, out_grad,
    norm1_gain, norm1_bias, self_query, self_key, self_value, self_output,
    norm2_gain, norm2_bias, cross_query, cross_key, cross_value, cross_output,
    norm3_gain, norm3_bias, mlp_in, mlp_in_bias, mlp_out, mlp_out_bias,
):
    tokens = image_tokens[0]
    rows, width = tokens.shape
    hidden = mlp_in.shape[1]
    vectors = (
        norm1_gain, norm1_bias, norm2_gain, norm2_bias,
        norm3_gain, norm3_bias, mlp_in_bias, mlp_out_bias,
    )
    sizes = [v.shape[0] for v in vectors]
    shard = self_query.shape[0]
    owners = width // shard
    parts = hidden // width
    orders = halving_orders()
    spread = [order[::-1] for order in orders]
    w_query, w_key, w_value, shared, text_full = alone(
        Gather(
            [(w, spread, 1) for w in (self_query, self_key, self_value, pack_vectors(vectors))]
            + [(text_states[0], [cube_dims(("narrow",))], 1)]
        ),
        1,
    )
    shared = shared.reshape(owners, -1, 128)
    given = shared[:, :, :shard].transpose(1, 0, 2).reshape(-1, width)
    up_bias = shared[:, 6, : sizes[6]].reshape(1, -1)
    mask = (text_segments[0] == image_segment[0, 0]).astype(jnp.int32)
    mask = jnp.concatenate([mask, mask]).reshape(-1, 1)

    (normed_one, queries, keys, values, mixed_self, sums_self), (down, *weights_two) = attend(
        tokens, given, (w_query, w_key, w_value),
        Gather(
            [
                (w, spread, 2)
                for w in (mlp_out, self_output, cross_query, cross_key, cross_value, cross_output)
            ]
        ),
        ((1, 0), (2, 0), (3, 0), (5, 0)), 2,
    )
    (x1, h2, q2, a2, x2, h3, k2, v2), ups = middle(
        tokens, mixed_self, text_full, mask, given, weights_two,
        Gather([(mlp_in, spread, 1)]), ((0, 1), (1, 1), (2, 1)), 3,
    )
    (
        block_out, dx2, grad_up_bias, grad_gain_three, grad_bias_three, grad_down_bias,
        grad_down, grad_up, near_sums,
    ) = mlp(x2, h3, out_grad[0], given, ups[0], up_bias, down, 2, (0, 1, 3, 5, 6, 7), orders[4:], 4)
    w_output, c_query, c_key, c_value, c_output = weights_two
    (
        dx1, grad_mixed, grad_self_out, grad_cross_query, grad_cross_out, grad_k2, grad_v2,
        grad_gain_two, grad_bias_two,
    ), (grad_down,) = middle_back(
        dx2, x1, mixed_self, h2, q2, a2, k2, v2, mask, given, (w_output, c_query, c_output),
        Scatter([(grad_down, orders, 1)]), ((0, 1), (2, 1), (3, 1)), 5,
    )
    (
        grad_queries, grad_keys, grad_values, *late, text_term,
    ), (*far_sums, grad_self_out, grad_cross_query, grad_cross_out) = attend_back(
        queries, keys, values, grad_mixed, sums_self, normed_one,
        (grad_k2, grad_v2, text_full, c_key, c_value),
        Scatter(
            [(g, orders, 1) for g in (*grad_up, grad_self_out, grad_cross_query, grad_cross_out)]
        ),
        ((1, 0), (4, 0), (6, 0), (7, 0)), 6,
    )
    self_terms = (grad_queries, grad_keys, grad_values)
    others = jnp.concatenate(
        [
            jnp.zeros((2, width), jnp.float32),
            grad_gain_two, grad_bias_two, grad_gain_three, grad_bias_three, grad_down_bias,
            grad_up_bias.reshape(-1, width),
        ],
        axis=0,
    )
    others = jnp.pad(others, ((0, -others.shape[0] % 8), (0, 0)))
    (image_grad, vector_sums), (
        grad_self_query, grad_self_key, grad_self_value, grad_cross_key, grad_cross_value, text_grad,
    ) = first_back(
        tokens, dx1, given, others, (w_query, w_key, w_value), self_terms,
        Scatter(
            [(g, orders, 1) for g in late] + [(text_term, [cube_dims(("narrow",))], 1)]
        ),
        (1,), 7,
    )
    (
        grad_self_query, grad_self_key, grad_self_value, grad_self_out,
        grad_cross_query, grad_cross_key, grad_cross_value, grad_cross_out,
        grad_up, grad_down, text_grad,
    ) = hand_over(
        [
            (g,)
            for g in (
                grad_self_query, grad_self_key, grad_self_value, grad_self_out,
                grad_cross_query, grad_cross_key, grad_cross_value, grad_cross_out,
            )
        ]
        + [(*near_sums, *far_sums), (grad_down,), (text_grad,)]
    )
    place = lax.axis_index(AXES)
    flat = vector_sums.reshape(-1)
    rows_of = (0, 1, 2, 3, 4, 5, 7, 6)
    vector_grads = [
        lax.dynamic_slice_in_dim(flat, row * width + place * size, size)
        for row, size in zip(rows_of, sizes)
    ]
    return (
        block_out[None], image_grad[None], text_grad[None],
        vector_grads[0], vector_grads[1],
        grad_self_query, grad_self_key, grad_self_value, grad_self_out,
        vector_grads[2], vector_grads[3],
        grad_cross_query, grad_cross_key, grad_cross_value, grad_cross_out,
        vector_grads[4], vector_grads[5],
        grad_up, vector_grads[6], grad_down, vector_grads[7],
    )


def solution(mesh):
    placed = (
        P(("wide", "narrow"), None, None),
        P("wide", "narrow", None),
        P("wide", None),
        P("wide", "narrow"),
        P(("wide", "narrow"), None, None),
        P(("wide", "narrow")),
        P(("wide", "narrow")),
        P(("wide", "narrow"), None),
        P(("wide", "narrow"), None),
        P(("wide", "narrow"), None),
        P(("wide", "narrow"), None),
        P(("wide", "narrow")),
        P(("wide", "narrow")),
        P(("wide", "narrow"), None),
        P(("wide", "narrow"), None),
        P(("wide", "narrow"), None),
        P(("wide", "narrow"), None),
        P(("wide", "narrow")),
        P(("wide", "narrow")),
        P(("wide", "narrow"), None),
        P(("wide", "narrow")),
        P(("wide", "narrow"), None),
        P(("wide", "narrow")),
    )
    return jax.shard_map(
        on_device,
        mesh=mesh,
        in_specs=placed,
        out_specs=(
            P(("wide", "narrow"), None, None),
            P(("wide", "narrow"), None, None),
            P("wide", "narrow", None),
            P(("wide", "narrow")),
            P(("wide", "narrow")),
            P(("wide", "narrow"), None),
            P(("wide", "narrow"), None),
            P(("wide", "narrow"), None),
            P(("wide", "narrow"), None),
            P(("wide", "narrow")),
            P(("wide", "narrow")),
            P(("wide", "narrow"), None),
            P(("wide", "narrow"), None),
            P(("wide", "narrow"), None),
            P(("wide", "narrow"), None),
            P(("wide", "narrow")),
            P(("wide", "narrow")),
            P(("wide", "narrow"), None),
            P(("wide", "narrow")),
            P(("wide", "narrow"), None),
            P(("wide", "narrow")),
        ),
        check_vma=False,
    )
```

```python
import functools
import math

import jax
import jax.numpy as jnp
from jax import lax
from jax.experimental import pallas as pl
from jax.experimental.pallas import tpu as pltpu
from jax.sharding import PartitionSpec as P

HEAD_DIM = 64
TILE = 256
BF16 = jnp.bfloat16
VMEM_LIMIT = 60 * 1024 * 1024
MLP_STEPS = 8
MLP_TILE = 512
VECTOR_ROWS = 16

EPSILON = 1e-05
NEGATIVE = -1e30

AXES = ("wide", "narrow")


def axis_bits(axis):
    return lax.axis_size(axis).bit_length() - 1


def pack_vectors(vectors):
    room = 1024
    placed = [
        jnp.pad(v.astype(jnp.float32), (128 * k, room - 128 * k - v.shape[0]))
        for k, v in enumerate(vectors)
    ]
    return sum(placed).reshape(-1, 128)


def nn(a, b):
    return lax.dot_general(a, b, (((1,), (0,)), ((), ())), preferred_element_type=jnp.float32)


def nt(a, b):
    return lax.dot_general(a, b, (((1,), (1,)), ((), ())), preferred_element_type=jnp.float32)


def tn(a, b):
    return lax.dot_general(a, b, (((0,), (0,)), ((), ())), preferred_element_type=jnp.float32)


def standardize(values):
    center = jnp.mean(values, axis=-1, keepdims=True)
    offset = values - center
    rate = lax.rsqrt(jnp.mean(offset * offset, axis=-1, keepdims=True) + EPSILON)
    return offset * rate, rate


def norm_back(standard, rate, gain, grad):
    scaled = grad * gain
    return rate * (
        scaled
        - jnp.mean(scaled, axis=-1, keepdims=True)
        - standard * jnp.mean(scaled * standard, axis=-1, keepdims=True)
    )


def column_sum(values):
    return jnp.sum(values, axis=0, keepdims=True)


def head_lanes(block, head):
    lane = lax.broadcasted_iota(jnp.int32, block.shape, 1)
    inside = (lane >= HEAD_DIM) if head else (lane < HEAD_DIM)
    return jnp.where(inside, block, jnp.zeros_like(block))


def whole_block(shape):
    zeros = (0,) * len(shape)
    return pl.BlockSpec(shape, lambda *_: zeros, pipeline_mode=pl.Buffered(1))


def params(**extra):
    return pltpu.CompilerParams(vmem_limit_bytes=VMEM_LIMIT, **extra)


def attend_kernel(
    x_ref, vectors_ref, wq_ref, wk_ref, wv_ref, h_ref, q_ref, k_ref, v_ref, o_ref, sums_ref,
    hook,
):
    rows = x_ref.shape[0]

    @pl.when(pl.program_id(0) == 0)
    def _():
        for start in range(0, rows, TILE):
            at = slice(start, start + TILE)
            standard, _ = standardize(x_ref[at, :].astype(jnp.float32))
            h_ref[at, :] = (standard * vectors_ref[0:1, :] + vectors_ref[1:2, :]).astype(BF16)

    weights = jnp.concatenate([w[...] for w in (wq_ref, wk_ref, wv_ref)], axis=1)
    mapped = nn(h_ref[...], weights).astype(BF16)
    q_ref[...] = mapped[:, :128]
    k_ref[...] = mapped[:, 128:256]
    v_ref[...] = mapped[:, 256:]
    flipped = v_ref[...].T
    for start in range(0, rows, TILE):
        span = start + TILE
        queries = q_ref[start:span, :] * (HEAD_DIM**-0.5)
        keys = k_ref[:span, :]
        mixed, sums = [], []
        for head in range(2):
            scores = nt(keys, head_lanes(queries, head))
            key_at = lax.broadcasted_iota(jnp.int32, (TILE, TILE), 0)
            query_at = lax.broadcasted_iota(jnp.int32, (TILE, TILE), 1)
            corner = jnp.where(key_at <= query_at, scores[start:], NEGATIVE)
            scores = jnp.concatenate([scores[:start], corner], axis=0) if start else corner
            top = jnp.max(scores, axis=0, keepdims=True)
            powers = jnp.exp(scores - top)
            total = jnp.sum(powers, axis=0, keepdims=True)
            part = nn(flipped[HEAD_DIM * head : HEAD_DIM * (head + 1), :span], powers.astype(BF16))
            mixed.append(part * (1.0 / total))
            sums.append(top + jnp.log(total))
        o_ref[start:span, :] = jnp.concatenate(mixed, axis=0).T.astype(BF16)
        sums_ref[0, :, start:span] = jnp.concatenate(sums, axis=0)


def attend(tokens, vectors, weights, work, schedule, collective_id):
    rows, width = tokens.shape
    pairs = width // 128
    block = pl.BlockSpec((rows, 128), lambda p: (0, p))
    like = jax.ShapeDtypeStruct(tokens.shape, BF16)
    results = pl.pallas_call(
        beside(attend_kernel, work, (5, 6, 0), schedule, pairs),
        grid=(pairs,),
        in_specs=[whole_block(tokens.shape), whole_block(vectors.shape)]
        + [pl.BlockSpec((width, 128), lambda p: (0, p))] * 3
        + work.in_specs,
        out_specs=[whole_block(tokens.shape)]
        + [block] * 4
        + [pl.BlockSpec((1, 2, rows), lambda p: (p, 0, 0))]
        + work.out_specs,
        out_shape=[like] * 5
        + [jax.ShapeDtypeStruct((pairs, 2, rows), jnp.float32)]
        + work.out_shape,
        scratch_shapes=work.scratch,
        compiler_params=params(collective_id=collective_id, has_side_effects=True),
        name="self_attend",
    )(tokens, vectors, *weights, *work.arrays)
    return results[:6], work.results(results[6:])


def attend_back_kernel(
    q_ref, k_ref, v_ref, da_ref, sums_ref, h_ref, dk2_ref, dv2_ref, text_ref, ck_ref, cv_ref,
    dq_ref, dk_ref, dv_ref, dwq_ref, dwk_ref, dwv_ref, dck_ref, dcv_ref, dtext_ref,
    dk_sum, dv_sum, h_flip, hook,
):
    rows, width = q_ref.shape

    @pl.when(pl.program_id(0) == 0)
    def _():
        h_flip[...] = h_ref[...].T
        dck_ref[...] = tn(text_ref[...], dk2_ref[...]).astype(BF16)
        dcv_ref[...] = tn(text_ref[...], dv2_ref[...]).astype(BF16)
        dtext_ref[...] = nt(dk2_ref[...], ck_ref[...]) + nt(dv2_ref[...], cv_ref[...])

    flipped = k_ref[...].T
    for start in reversed(range(0, rows, TILE)):
        if start == TILE:
            hook(1)
        span = start + TILE
        queries = q_ref[start:span, :] * (HEAD_DIM**-0.5)
        grads = da_ref[start:span, :]
        keys = k_ref[:span, :]
        values = v_ref[:span, :]
        parts = []
        for head in range(2):
            own_queries = head_lanes(queries, head)
            own_grads = head_lanes(grads, head)
            scores = nt(keys, own_queries)
            key_at = lax.broadcasted_iota(jnp.int32, (TILE, TILE), 0)
            query_at = lax.broadcasted_iota(jnp.int32, (TILE, TILE), 1)
            corner = jnp.where(key_at <= query_at, scores[start:], NEGATIVE)
            scores = jnp.concatenate([scores[:start], corner], axis=0) if start else corner
            probs = jnp.exp(scores - sums_ref[0, head : head + 1, start:span])
            grad_probs = nt(values, own_grads)
            inner = jnp.sum(probs * grad_probs, axis=0, keepdims=True)
            grad_scores = (probs * (grad_probs - inner)).astype(BF16)
            value_term = nn(probs.astype(BF16), own_grads)
            key_term = nn(grad_scores, own_queries)
            if span == rows and head == 0:
                dv_sum[...] = value_term
                dk_sum[...] = key_term
            else:
                dv_sum[:span, :] += value_term
                dk_sum[:span, :] += key_term
            parts.append(nn(flipped[HEAD_DIM * head : HEAD_DIM * (head + 1), :span], grad_scores))
        dq = jnp.concatenate(parts, axis=0).T * (HEAD_DIM**-0.5)
        dq_ref[start:span, :] = dq.astype(BF16)
    dk_ref[...] = dk_sum[...].astype(BF16)
    dv_ref[...] = dv_sum[...].astype(BF16)
    grads = jnp.concatenate([dq_ref[...], dk_ref[...], dv_ref[...]], axis=1)
    weights = nn(h_flip[...], grads).astype(BF16)
    dwq_ref[...] = weights[:, :128]
    dwk_ref[...] = weights[:, 128:256]
    dwv_ref[...] = weights[:, 256:]


def attend_back(queries, keys, values, grads, sums, normed, cross, work, schedule, collective_id):
    rows, width = queries.shape
    steps = width // 128
    block = pl.BlockSpec((rows, 128), lambda p: (0, p))
    results = pl.pallas_call(
        beside(attend_back_kernel, work, (11, 9, 3), schedule, steps),
        grid=(steps,),
        in_specs=[block] * 4
        + [pl.BlockSpec((1, 2, rows), lambda p: (p, 0, 0)), whole_block(normed.shape)]
        + [whole_block(c.shape) for c in cross]
        + work.in_specs,
        out_specs=[block] * 6
        + [whole_block((width, width))] * 2
        + [whole_block(cross[2].shape)]
        + work.out_specs,
        out_shape=[jax.ShapeDtypeStruct(queries.shape, BF16)] * 3
        + [jax.ShapeDtypeStruct((width, width), BF16)] * 5
        + [jax.ShapeDtypeStruct(cross[2].shape, jnp.float32)]
        + work.out_shape,
        scratch_shapes=[pltpu.VMEM((rows, 128), jnp.float32)] * 2
        + [pltpu.VMEM((width, rows), BF16)]
        + work.scratch,
        compiler_params=params(collective_id=collective_id, has_side_effects=True),
        name="self_attend_back",
    )(queries, keys, values, grads, sums, normed, *cross, *work.arrays)
    return results[:9], work.results(results[9:])


def gelu_both(values):
    phi = 0.5 + 0.5 * lax.erf(values * (0.5**0.5))
    density = jnp.exp(-0.5 * values * values) * ((2.0 * math.pi) ** -0.5)
    return values * phi, phi + values * density


def mlp_kernel(
    near, far, paces, coming, work, x_ref, h_ref, g_ref, vectors_ref, ub_ref, down_ref, *refs
):
    parts = near + far
    late = len(coming.arrays)
    per = MLP_STEPS // parts
    early_refs, refs = refs[: parts - late], refs[parts - late :]
    shard_refs, refs = refs[:late], refs[late:]
    dx_ref, dub_ref, dgain_ref, dbias_ref, gsum_ref, ddown_ref, act = refs[:7]
    far_refs, refs = refs[7 : 7 + far], refs[7 + far :]
    sums, refs = refs[:near], refs[near:]
    dh_sum, h_flip, up, grad_act = refs[:4]
    near_refs, refs = refs[4 : 4 + near], refs[4 + near :]
    late_refs, refs = refs[:late], refs[late:]
    step, steps = pl.program_id(0), pl.num_programs(0)
    rows = h_ref.shape[0]
    chunk = up.shape[1]
    moving = work.bind(near_refs, sums, refs[: len(work.scratch)])
    arriving = coming.bind(shard_refs, late_refs, refs[len(work.scratch) :])

    @pl.when(step == 0)
    def _():
        greet_partners()
        tick(arriving, -1)
        h_flip[...] = h_ref[...].T
        dh_sum[...] = jnp.zeros_like(dh_sum)

    left, due = [], {}
    for at in range(coming.ticks):
        due.setdefault(paces[0][at], []).append((arriving, at, None))
    for part in range(near):
        pieces = [k for k, p in enumerate(work.pieces) if p[0][0] == part]
        for at in range(-1, work.ticks):
            place = 2 * per * (part + 1) + paces[1][at + 1]
            if place < 2 * MLP_STEPS:
                due.setdefault(place, []).append((moving, at, pieces))
            else:
                left.append((moving, at, pieces))

    def move(half):
        for place in due:
            if place % 2 == half:

                @pl.when(step == place // 2)
                def _(place=place):
                    for mover, at, pieces in due[place]:
                        tick(mover, at, pieces)

    move(0)
    for place in range(MLP_STEPS):

        @pl.when(step == place)
        def _(place=place):
            part, first = place // per, chunk * (place % per)
            if part < parts - late:
                up[...] = early_refs[part][...]
            else:
                ref = late_refs[part - parts + late]
                up[...] = ref[..., first : first + chunk].reshape(up.shape)

    down = down_ref[...]
    bias_sum = jnp.zeros_like(dub_ref)
    for start in range(0, rows, MLP_TILE):
        at = slice(start, start + MLP_TILE)
        hidden, slope = gelu_both(nn(h_ref[at, :], up[...]) + ub_ref[...])
        act[at, :] = hidden.astype(BF16)
        grad_pre = (nt(g_ref[at, :], down) * slope).astype(BF16)
        grad_act[at, :] = grad_pre
        bias_sum += column_sum(grad_pre.astype(jnp.float32))
        dh_sum[at, :] += nt(grad_pre, up[...])
    dub_ref[...] = bias_sum
    move(1)
    grad_up = nn(h_flip[...], grad_act[...]).astype(BF16)
    for part, ref in enumerate(far_refs):

        @pl.when(step // per == near + part)
        def _(ref=ref):
            ref[...] = grad_up

    for place in range(near * per):

        @pl.when(step == place)
        def _(place=place):
            ref = near_refs[place // per]
            first = chunk * (place % per)
            ref[..., first : first + chunk] = grad_up.reshape(ref.shape[:-1] + (chunk,))

    ddown_ref[...] = tn(act[...], g_ref[...]).astype(BF16)

    @pl.when(step == steps - 1)
    def _():
        gain_sum = jnp.zeros_like(dgain_ref)
        grad_sum = jnp.zeros_like(dbias_ref)
        tail_sum = jnp.zeros_like(gsum_ref)
        for start in range(0, rows, TILE):
            at = slice(start, start + TILE)
            standard, rate = standardize(x_ref[at, :])
            grad = dh_sum[at, :]
            tail = g_ref[at, :].astype(jnp.float32)
            dx_ref[at, :] = tail + norm_back(standard, rate, vectors_ref[4:5, :], grad)
            gain_sum += column_sum(grad * standard)
            grad_sum += column_sum(grad)
            tail_sum += column_sum(tail)
        dgain_ref[...] = gain_sum
        dbias_ref[...] = grad_sum
        gsum_ref[...] = tail_sum
        for mover, at, pieces in left:
            tick(mover, at, pieces)
        settle(moving)
        settle(arriving)


def mlp(x, h, g, vectors, early, coming, up_bias, down, near, paces, orders, collective_id):
    rows, width = x.shape
    hidden = up_bias.shape[1]
    chunk = hidden // MLP_STEPS
    f32 = jnp.float32
    row = (1, width)
    parts = hidden // width
    per = width // chunk
    lead = (2,) * len(cube_dims())
    block = lead + (width >> len(lead), width)
    source = jax.ShapeDtypeStruct(block, BF16)
    work = Scatter([(source, orders, (1, 16))] * near, near=True)
    far = parts - near
    more = range(1, 1 + len(cube_dims()))
    paces = [[*pace, *(pace[-1] + k for k in more)] for pace in paces]

    def part_of(k):
        return pl.BlockSpec((width, chunk), lambda c: (0, jnp.clip(c - per * k, 0, per - 1)))

    results = pl.pallas_call(
        functools.partial(mlp_kernel, near, far, paces, coming, work),
        grid=(MLP_STEPS,),
        in_specs=[
            whole_block(x.shape), whole_block(h.shape), whole_block(g.shape), whole_block(vectors.shape),
            pl.BlockSpec((1, chunk), lambda c: (0, c)),
            pl.BlockSpec((chunk, width), lambda c: (c, 0)),
        ]
        + [part_of(k) for k in range(len(early))]
        + coming.in_specs,
        out_specs=[
            whole_block(x.shape),
            pl.BlockSpec((1, chunk), lambda c: (0, c)),
            whole_block(row), whole_block(row), whole_block(row),
            pl.BlockSpec((chunk, width), lambda c: (c, 0)),
            pl.BlockSpec((rows, chunk), lambda c: (0, c)),
        ]
        + [part_of(k) for k in range(near, parts)]
        + work.out_specs,
        out_shape=[
            jax.ShapeDtypeStruct(x.shape, f32),
            jax.ShapeDtypeStruct((1, hidden), f32),
            jax.ShapeDtypeStruct(row, f32), jax.ShapeDtypeStruct(row, f32), jax.ShapeDtypeStruct(row, f32),
            jax.ShapeDtypeStruct((hidden, width), BF16),
            jax.ShapeDtypeStruct((rows, hidden), BF16),
        ]
        + [jax.ShapeDtypeStruct((width, width), BF16)] * far
        + work.out_shape,
        scratch_shapes=[
            pltpu.VMEM(x.shape, f32), pltpu.VMEM((width, rows), BF16),
            pltpu.VMEM((width, chunk), BF16), pltpu.VMEM((rows, chunk), BF16),
        ]
        + [pltpu.VMEM(block, BF16)] * near
        + [pltpu.VMEM(b, BF16) for b in coming.blocks]
        + work.scratch
        + coming.scratch,
        compiler_params=params(collective_id=collective_id, has_side_effects=True),
        name="mlp_both_ways",
    )(x, h, g, vectors, up_bias, down, *early, *coming.arrays)
    return *results[:7], results[7 : 7 + far], work.results(results[7 + far :])


def load_all(sources, buffers, sems):
    copies = [
        pltpu.make_async_copy(source, buffer, sems.at[k])
        for k, (source, buffer) in enumerate(zip(sources, buffers))
    ]
    for copy in copies:
        copy.start()
    for copy in copies:
        copy.wait()


def room_for(arrays):
    return [pltpu.VMEM(a.shape, a.dtype) for a in arrays] + [pltpu.SemaphoreType.DMA((len(arrays),))]


def stack_heads(pair):
    return jnp.concatenate([head_lanes(pair, 0), head_lanes(pair, 1)], axis=0)


def by_head(stacked):
    return stacked.reshape(2, stacked.shape[0] // 2, stacked.shape[1])


def caption_probs(keys, queries, mask):
    scores = by_head(jnp.where(mask != 0, nt(keys, queries), NEGATIVE))
    powers = jnp.exp(scores - jnp.max(scores, axis=1, keepdims=True))
    return powers * (1.0 / jnp.sum(powers, axis=1, keepdims=True))


def middle_kernel(
    x_ref, a_ref, text_ref, mask_ref, vectors_ref,
    wo_hbm, cq_hbm, ck_hbm, cv_hbm, co_hbm,
    x1_ref, h2_ref, q2_ref, a2_ref, x2_ref, h3_ref, k2_ref, v2_ref, keys, values_flip,
    wo_ref, cq_ref, ck_ref, cv_ref, co_ref, weight_sems,
    hook,
):
    @pl.when(pl.program_id(0) == 0)
    def _():
        load_all(
            (wo_hbm, cq_hbm, ck_hbm, cv_hbm, co_hbm),
            (wo_ref, cq_ref, ck_ref, cv_ref, co_ref),
            weight_sems,
        )
        k2_ref[...] = nn(text_ref[...], ck_ref[...]).astype(BF16)
        v2_ref[...] = nn(text_ref[...], cv_ref[...]).astype(BF16)
        for pair in range(keys.shape[0]):
            at = slice(128 * pair, 128 * (pair + 1))
            keys[pair] = stack_heads(k2_ref[:, at])
            values_flip[pair] = stack_heads(v2_ref[:, at]).T

    after_self = x_ref[...].astype(jnp.float32) + nn(a_ref[...], wo_ref[...])
    x1_ref[...] = after_self
    standard, _ = standardize(after_self)
    normed = (standard * vectors_ref[2:3, :] + vectors_ref[3:4, :]).astype(BF16)
    h2_ref[...] = normed
    q2_ref[...] = nn(normed, cq_ref[...]).astype(BF16)
    mask = mask_ref[...]
    for pair in range(q2_ref.shape[1] // 128):
        at = slice(128 * pair, 128 * (pair + 1))
        queries = q2_ref[:, at] * (HEAD_DIM**-0.5)
        probs = caption_probs(keys[pair], queries, mask).astype(BF16)
        mixed = nn(values_flip[pair], probs.reshape(-1, probs.shape[2]))
        a2_ref[:, at] = mixed.T.astype(BF16)
    hook(1)
    after_cross = after_self + nn(a2_ref[...], co_ref[...])
    x2_ref[...] = after_cross
    standard, _ = standardize(after_cross)
    h3_ref[...] = (standard * vectors_ref[4:5, :] + vectors_ref[5:6, :]).astype(BF16)


def middle(tokens, mixed, text, mask, vectors, weights, work, schedule, collective_id):
    rows, width = tokens.shape
    slots = text.shape[0]
    tile = pl.BlockSpec((TILE, width), lambda i: (i, 0))
    f32 = jnp.float32
    like = lambda dtype: jax.ShapeDtypeStruct(tokens.shape, dtype)
    results = pl.pallas_call(
        beside(middle_kernel, work, (10, 8, 8), schedule, rows // TILE),
        grid=(rows // TILE,),
        in_specs=[
            tile, tile, whole_block(text.shape), whole_block(mask.shape),
            whole_block(vectors.shape), *[pl.BlockSpec(memory_space=pl.ANY)] * 5, *work.in_specs,
        ],
        out_specs=[tile] * 6 + [whole_block(text.shape)] * 2 + work.out_specs,
        out_shape=[like(f32), like(BF16), like(BF16), like(BF16), like(f32), like(BF16)]
        + [jax.ShapeDtypeStruct(text.shape, BF16)] * 2
        + work.out_shape,
        scratch_shapes=[
            pltpu.VMEM((width // 128, 2 * slots, 128), BF16),
            pltpu.VMEM((width // 128, 128, 2 * slots), BF16),
        ]
        + room_for(weights)
        + work.scratch,
        compiler_params=params(collective_id=collective_id, has_side_effects=True),
        name="output_and_cross",
    )(tokens, mixed, text, mask, vectors, *weights, *work.arrays)
    return results[:8], work.results(results[8:])


def middle_back_kernel(
    dx2_ref, x1_ref, a1_ref, h2_ref, q2_ref, a2_ref, k2_ref, v2_ref, mask_ref, vectors_ref,
    wo_ref, cq_ref, co_ref,
    dx1_ref, da1_ref, dwo_ref, dcq_ref, dco_ref, dk2_ref, dv2_ref, dgain_ref, dbias_ref,
    wo_sum, cq_sum, co_sum, dk_sum, dv_sum, dq2, keys, keys_flip, values,
    hook,
):
    step, steps = pl.program_id(0), pl.num_programs(0)
    pairs = keys.shape[0]
    slots = k2_ref.shape[0]

    @pl.when(step == 0)
    def _():
        for ref in (wo_sum, cq_sum, co_sum, dk_sum, dv_sum, dgain_ref, dbias_ref):
            ref[...] = jnp.zeros_like(ref)
        for pair in range(pairs):
            at = slice(128 * pair, 128 * (pair + 1))
            keys[pair] = stack_heads(k2_ref[:, at])
            keys_flip[pair] = keys[pair].T
            values[pair] = stack_heads(v2_ref[:, at])

    grad_out = dx2_ref[...].astype(BF16)
    co_sum[...] += tn(a2_ref[...], grad_out)
    grad_mixed = nt(grad_out, co_ref[...]).astype(BF16)
    mask = mask_ref[...]
    for pair in range(pairs):
        at = slice(128 * pair, 128 * (pair + 1))
        queries = q2_ref[:, at] * (HEAD_DIM**-0.5)
        grads = grad_mixed[:, at]
        probs = caption_probs(keys[pair], queries, mask)
        grad_probs = by_head(nt(values[pair], grads))
        inner = jnp.sum(probs * grad_probs, axis=1, keepdims=True)
        grad_scores = (probs * (grad_probs - inner)).astype(BF16).reshape(2 * slots, -1)
        dv_sum[pair] += nn(probs.astype(BF16).reshape(2 * slots, -1), grads)
        dk_sum[pair] += nn(grad_scores, queries)
        dq2[:, at] = (nn(keys_flip[pair], grad_scores).T * (HEAD_DIM**-0.5)).astype(BF16)
    hook(1)
    cq_sum[...] += tn(h2_ref[...], dq2[...])
    grad_normed = nt(dq2[...], cq_ref[...])
    standard, rate = standardize(x1_ref[...])
    grad_after = dx2_ref[...] + norm_back(standard, rate, vectors_ref[2:3, :], grad_normed)
    dgain_ref[...] += column_sum(grad_normed * standard)
    dbias_ref[...] += column_sum(grad_normed)
    dx1_ref[...] = grad_after
    grad_self = grad_after.astype(BF16)
    wo_sum[...] += tn(a1_ref[...], grad_self)
    da1_ref[...] = nt(grad_self, wo_ref[...]).astype(BF16)

    @pl.when(step == steps - 1)
    def _():
        dwo_ref[...] = wo_sum[...].astype(BF16)
        dcq_ref[...] = cq_sum[...].astype(BF16)
        dco_ref[...] = co_sum[...].astype(BF16)
        for pair in range(pairs):
            at = slice(128 * pair, 128 * (pair + 1))
            for total, ref in ((dk_sum, dk2_ref), (dv_sum, dv2_ref)):
                upper, lower = total[pair, :slots], total[pair, slots:]
                ref[:, at] = (head_lanes(upper, 0) + head_lanes(lower, 1)).astype(BF16)


def middle_back(
    dx2, x1, a1, h2, q2, a2, k2, v2, mask, vectors, weights, work, schedule, collective_id
):
    rows, width = x1.shape
    slots = k2.shape[0]
    pairs = width // 128
    tile = pl.BlockSpec((TILE, width), lambda i: (i, 0))
    f32 = jnp.float32
    matrix = (width, width)
    results = pl.pallas_call(
        beside(middle_back_kernel, work, (13, 9, 9), schedule, rows // TILE),
        grid=(rows // TILE,),
        in_specs=[tile] * 6
        + [whole_block(v.shape) for v in (k2, v2, mask, vectors, *weights)]
        + work.in_specs,
        out_specs=[tile] * 2
        + [whole_block(matrix)] * 3
        + [whole_block(k2.shape)] * 2
        + [whole_block((1, width))] * 2
        + work.out_specs,
        out_shape=[jax.ShapeDtypeStruct(x1.shape, f32), jax.ShapeDtypeStruct(x1.shape, BF16)]
        + [jax.ShapeDtypeStruct(matrix, BF16)] * 3
        + [jax.ShapeDtypeStruct(k2.shape, BF16)] * 2
        + [jax.ShapeDtypeStruct((1, width), f32)] * 2
        + work.out_shape,
        scratch_shapes=[pltpu.VMEM(matrix, f32)] * 3
        + [pltpu.VMEM((pairs, 2 * slots, 128), f32)] * 2
        + [
            pltpu.VMEM((TILE, width), BF16),
            pltpu.VMEM((pairs, 2 * slots, 128), BF16),
            pltpu.VMEM((pairs, 128, 2 * slots), BF16),
            pltpu.VMEM((pairs, 2 * slots, 128), BF16),
        ]
        + work.scratch,
        compiler_params=params(collective_id=collective_id, has_side_effects=True),
        name="cross_back",
    )(dx2, x1, a1, h2, q2, a2, k2, v2, mask, vectors, *weights, *work.arrays)
    return results[:9], work.results(results[9:])


def first_back_kernel(
    work, schedule, steps, x_ref, dx1_ref, given_ref, gain2_ref, bias2_ref, gain3_ref, bias3_ref, db_ref, ub_ref,
    wq_ref, wk_ref, wv_ref, dq_ref, dk_ref, dv_ref,
    x2_ref, act_ref, down_ref, *refs,
):
    n, m = len(work.in_specs), len(work.out_specs)
    sources, (dx_ref, out_ref, vector_sum_ref) = refs[:n], refs[n : n + 3]
    sums, rest = refs[n + 3 : n + 3 + m], refs[n + 3 + m :]
    stages = len(cube_dims())
    doubling = Doubling(rest[0], rest[1 : stages + 1], *rest[stages + 1 : stages + 3])
    halving = work.bind(sources, sums, rest[stages + 3 :])
    step = pl.program_id(0)
    vectors = doubling.buffers[0]

    @pl.when(step == 0)
    def _():
        greet_partners()
        tick(halving, -1)
        vectors[...] = jnp.zeros_like(vectors)
        for row, ref in enumerate((gain2_ref, bias2_ref, gain3_ref, bias3_ref, db_ref)):
            vectors[row + 2 : row + 3, :] = ref[...]
        width = vectors.shape[1]
        for part in range(ub_ref.shape[1] // width):
            vectors[part + 7 : part + 8, :] = ub_ref[:, width * part : width * (part + 1)]

    for at, place in enumerate(schedule):

        @pl.when(step == place)
        def _(at=at):
            tick(halving, at)

    grad_normed = (
        nt(dq_ref[...], wq_ref[...]) + nt(dk_ref[...], wk_ref[...]) + nt(dv_ref[...], wv_ref[...])
    )
    standard, rate = standardize(x_ref[...].astype(jnp.float32))
    dx_ref[...] = dx1_ref[...] + norm_back(standard, rate, given_ref[0:1, :], grad_normed)
    out = x2_ref[...] + nn(act_ref[...], down_ref[...]) + given_ref[7:8, :]
    out_ref[...] = out.astype(BF16)
    vectors[0:1, :] += column_sum(grad_normed * standard)
    vectors[1:2, :] += column_sum(grad_normed)

    @pl.when(step == steps - 1)
    def _():
        doubling.step(-1)
        for at in range(max(stages, work.ticks)):
            if at < stages:
                doubling.step(at)
            if len(schedule) + at < work.ticks:
                tick(halving, len(schedule) + at)
        vector_sum_ref[...] = doubling.buffers[-1][...]
        doubling.settle()
        settle(halving)


def first_back(
    tokens, dx1, given, vectors, weights, grads, x2, act, down, work, schedule, collective_id
):
    rows, width = tokens.shape
    steps = rows // TILE
    tile = pl.BlockSpec((TILE, width), lambda i: (i, 0))
    f32 = jnp.float32
    results = pl.pallas_call(
        functools.partial(first_back_kernel, work, schedule, steps),
        grid=(steps,),
        in_specs=[tile] * 2
        + [whole_block(v.shape) for v in (given, *vectors)]
        + [whole_block(w.shape) for w in weights]
        + [tile] * 4
        + [pl.BlockSpec((TILE, act.shape[1]), lambda i: (i, 0)), whole_block(down.shape)]
        + work.in_specs,
        out_specs=[tile, tile, whole_block((VECTOR_ROWS, width))] + work.out_specs,
        out_shape=[
            jax.ShapeDtypeStruct(tokens.shape, f32),
            jax.ShapeDtypeStruct(tokens.shape, BF16),
            jax.ShapeDtypeStruct((VECTOR_ROWS, width), f32),
        ]
        + work.out_shape,
        scratch_shapes=doubling_scratch((VECTOR_ROWS, width)) + work.scratch,
        compiler_params=params(collective_id=collective_id, has_side_effects=True),
        name="self_norm_back",
    )(tokens, dx1, given, *vectors, *weights, *grads, x2, act, down, *work.arrays)
    return results[:3], work.results(results[3:])


def hand_over_kernel(groups, *refs):
    ins, outs = refs[: sum(groups)], refs[sum(groups) :]
    at = 0
    for count, out in zip(groups, outs):
        width = out.shape[1] // count
        for part in range(count):
            out[:, width * part : width * (part + 1)] = ins[at + part][...]
        at += count


def hand_over(groups):
    arrays = [a for group in groups for a in group]
    return pl.pallas_call(
        functools.partial(hand_over_kernel, [len(group) for group in groups]),
        in_specs=[pl.BlockSpec(memory_space=pltpu.VMEM)] * len(arrays),
        out_specs=[pl.BlockSpec(memory_space=pltpu.VMEM)] * len(groups),
        out_shape=[
            jax.ShapeDtypeStruct((g[0].shape[0], sum(a.shape[1] for a in g)), g[0].dtype) for g in groups
        ],
        compiler_params=params(),
        name="hand_over",
    )(*arrays)


def cube_dims(axes=AXES):
    return [(axis, k) for axis in axes for k in reversed(range(axis_bits(axis)))]


def bits_of(dims):
    return [(lax.axis_index(axis) >> bit) & 1 for axis, bit in dims]


def partner(axis, bit):
    return {axis: lax.axis_index(axis) ^ (1 << bit)}


def halving_orders():
    x, y, near, far = ("narrow", 0), ("narrow", 1), ("wide", 1), ("wide", 2)
    core = ("wide", 0)
    six = (
        (far, x, y, near),
        (near, y, x, far),
        (y, far, x, near),
        (x, near, y, far),
        (x, y, far, near),
        (y, x, near, far),
    )
    rest = [d for d in cube_dims() if d not in (core, x, y, near, far)]
    return [[core, *order, *rest] for order in six]


def greet_partners():
    dims = cube_dims()
    barrier = pltpu.get_barrier_semaphore()
    for axis, bit in dims:
        pl.semaphore_signal(
            barrier, inc=1, device_id=partner(axis, bit), device_id_type=pl.DeviceIdType.MESH
        )
    pl.semaphore_wait(barrier, len(dims))


def runs_of(rows, step):
    step = step if rows % step == 0 else rows
    return [(start, step) for start in range(0, rows, step)]


def columns_of(columns, parts=6):
    if columns <= 1024:
        return [(0, columns)]
    cuts = [columns * k // parts // 128 * 128 for k in range(parts)] + [columns]
    return [(a, b - a) for a, b in zip(cuts[:-1], cuts[1:])]


def cut_up(groups):
    pieces = []
    for which, ((rows, columns), orders, (rounds, step)) in enumerate(groups):
        for start, size in runs_of(rows, step):
            for first, width in columns_of(columns):
                k = len(pieces)
                box = (which, slice(start, start + size), slice(first, first + width))
                pieces.append((box, orders[k % len(orders)], k // 6 % rounds))
    return pieces


def tick(mover, at, pieces=None):
    for piece in range(len(mover.pieces)) if pieces is None else pieces:
        _, order, late = mover.pieces[piece]
        stage = at - late
        if 0 <= stage < len(order):
            mover.finish(piece, stage)
        if -1 <= stage < len(order) - 1:
            mover.start(piece, stage + 1)


def settle(mover):
    for piece, (_, order, _) in enumerate(mover.pieces):
        for stage in range(len(order)):
            mover.send(piece, stage).wait_send()


def ticks_of(pieces):
    return max(len(order) + late for _, order, late in pieces)


def places_of(pieces):
    ends = [sum(len(p[1]) for p in pieces[:k]) for k in range(len(pieces) + 1)]
    return ends[:-1], ends[-1]


class Gathering:
    def __init__(self, pieces, dims, firsts, sources, outs, scratch):
        self.pieces, self.dims, self.firsts = pieces, dims, firsts
        self.sources, self.outs = sources, outs
        self.send_sems, self.recv_sems, self.own_sems = scratch
        self.base, _ = places_of(pieces)
        self.ready = set()

    def source(self, piece):
        (which, rows, columns), _, _ = self.pieces[piece]
        first = self.firsts[which]
        return self.sources[which].at[rows, slice(first + columns.start, first + columns.stop)]

    def own(self, piece):
        (which, *box), _, _ = self.pieces[piece]
        there = self.outs[which].at[(*bits_of(self.dims[which]), *box)]
        return pltpu.make_async_copy(self.source(piece), there, self.own_sems.at[piece])

    def send(self, piece, stage):
        (which, *box), order, _ = self.pieces[piece]
        held = order[:stage]
        dims = self.dims[which]
        at = [slice(None) if d in held else b for d, b in zip(dims, bits_of(dims))]
        there = self.outs[which].at[(*at, *box)]
        sem = self.base[piece] + stage
        return pltpu.make_async_remote_copy(
            src_ref=there if stage else self.source(piece),
            dst_ref=there,
            send_sem=self.send_sems.at[sem],
            recv_sem=self.recv_sems.at[sem],
            device_id=partner(*order[stage]),
            device_id_type=pl.DeviceIdType.MESH,
        )

    def start(self, piece, stage):
        if stage == 0:
            self.own(piece).start()
        if stage == 1:
            self.own(piece).wait()
        self.send(piece, stage).start()

    def finish(self, piece, stage):
        self.send(piece, stage).wait_recv()


class Gather:
    def __init__(self, groups):
        self.arrays, self.firsts, self.shapes, cuts = [], [], [], []
        for array, orders, rounds, *span in groups:
            first, last = span or (0, array.shape[1])
            self.arrays.append(array)
            self.firsts.append(first)
            self.shapes.append((array.shape[0], last - first))
            cuts.append((self.shapes[-1], orders, rounds))
        self.pieces = cut_up(cuts)
        self.dims = [[d for d in cube_dims() if d in group[1][0]] for group in groups]
        self.ticks = ticks_of(self.pieces)
        _, copies = places_of(self.pieces)
        self.in_specs = [pl.BlockSpec(memory_space=pl.ANY)] * len(groups)
        self.out_specs = self.in_specs
        self.blocks = [(2,) * len(d) + s for d, s in zip(self.dims, self.shapes)]
        self.out_shape = [
            jax.ShapeDtypeStruct(b, a.dtype) for b, a in zip(self.blocks, self.arrays)
        ]
        self.scratch = [pltpu.SemaphoreType.DMA((copies,))] * 2
        self.scratch += [pltpu.SemaphoreType.DMA((len(self.pieces),))]

    def bind(self, sources, outs, scratch):
        return Gathering(self.pieces, self.dims, self.firsts, sources, outs, scratch)

    def results(self, outs):
        return [out.reshape(-1, s[1]) for out, s in zip(outs, self.shapes)]


class Halving:
    def __init__(self, pieces, firsts, sources, outs, scratch, near=False):
        count = len(pieces)
        self.firsts = firsts
        self.pieces, self.sources, self.outs, self.near = pieces, sources, outs, near
        self.kept, rest = ([], scratch) if near else (scratch[:count], scratch[count:])
        self.base, _ = places_of(pieces)
        self.landed = []
        for _, order, _ in pieces:
            self.landed.append(rest[: len(order)])
            rest = rest[len(order) :]
        self.send_sems, self.recv_sems = rest[:2]
        self.kept_sems = None if near else rest[2]

    def half(self, piece, stage, other):
        (which, rows, columns), order, _ = self.pieces[piece]
        left = [d for d in cube_dims() if d in order[stage:]]
        bit = bits_of([order[stage]])[0]
        at = [(1 - bit if other else bit) if d == order[stage] else slice(None) for d in left]
        if stage == 0:
            first = self.firsts[which]
            at += [slice(first + rows.start, first + rows.stop), columns]
        return tuple(at)

    def before(self, piece, stage):
        return self.sources[self.pieces[piece][0][0]] if stage == 0 else self.landed[piece][stage - 1]

    def send(self, piece, stage):
        sem = self.base[piece] + stage
        return pltpu.make_async_remote_copy(
            src_ref=self.before(piece, stage).at[self.half(piece, stage, True)],
            dst_ref=self.landed[piece][stage],
            send_sem=self.send_sems.at[sem],
            recv_sem=self.recv_sems.at[sem],
            device_id=partner(*self.pieces[piece][1][stage]),
            device_id_type=pl.DeviceIdType.MESH,
        )

    def keep(self, piece):
        source = self.before(piece, 0).at[self.half(piece, 0, False)]
        return pltpu.make_async_copy(source, self.kept[piece], self.kept_sems.at[piece])

    def start(self, piece, stage):
        self.send(piece, stage).start()
        if stage == 0 and not self.near:
            self.keep(piece).start()

    def finish(self, piece, stage):
        (which, rows, columns), order, _ = self.pieces[piece]
        self.send(piece, stage).wait_recv()
        if stage == 0 and not self.near:
            self.keep(piece).wait()
        landed = self.landed[piece][stage]
        depth = len(order) - 1 - stage
        if stage == 0 and not self.near:
            other, chosen = self.kept[piece], (slice(None),) * depth
        else:
            other, chosen = self.before(piece, stage), self.half(piece, stage, False)
        if depth == 0:
            total = landed[...].astype(jnp.float32) + other[chosen].astype(jnp.float32)
            self.outs[which][rows, columns] = total
            return

        def add(block, carry):
            at = [(block >> k) & 1 for k in reversed(range(depth))]
            rest = iter(at)
            there = [next(rest, c) if isinstance(c, slice) else c for c in chosen]
            landed[tuple(at)] = landed[tuple(at)] + other[tuple(there)]
            return carry

        lax.fori_loop(0, 1 << depth, add, 0, unroll=min(4, 1 << depth))


class Scatter:
    def __init__(self, groups, near=False):
        self.near = near
        self.arrays, self.firsts, shapes, cuts = [], [], [], []
        for array, orders, rounds, *span in groups:
            columns = array.shape[-1]
            block = (array.size // columns >> len(orders[0]), columns)
            self.arrays.append(array if near else array.reshape((2,) * len(orders[0]) + block))
            first, last = span or (0, block[0])
            self.firsts.append(first)
            shapes.append((last - first, columns))
            cuts.append(((last - first, columns), orders, rounds))
        self.pieces = cut_up(cuts)
        self.ticks = ticks_of(self.pieces)
        like = [
            ((rows.stop - rows.start, columns.stop - columns.start), self.arrays[which].dtype, len(order))
            for (which, rows, columns), order, _ in self.pieces
        ]
        kept = [pltpu.VMEM((2,) * (n - 1) + s, d) for s, d, n in like]
        landed = [pltpu.VMEM((2,) * (n - 1 - k) + s, d) for s, d, n in like for k in range(n)]
        _, copies = places_of(self.pieces)
        self.in_specs = [] if near else [pl.BlockSpec(memory_space=pl.ANY)] * len(groups)
        self.out_specs = [whole_block(s) for s in shapes]
        self.out_shape = [jax.ShapeDtypeStruct(s, jnp.float32) for s in shapes]
        self.scratch = ([] if near else kept) + landed + [pltpu.SemaphoreType.DMA((copies,))] * 2
        if not near:
            self.scratch += [pltpu.SemaphoreType.DMA((len(self.pieces),))]

    def bind(self, sources, outs, scratch):
        return Halving(self.pieces, self.firsts, sources, outs, scratch, self.near)

    def results(self, outs):
        return list(outs)


def beside(kernel, work, counts, schedule, steps):
    n_in, n_out, n_scratch = counts

    def run(*refs):
        cuts = [0, n_in, len(work.in_specs), n_out, len(work.out_specs), n_scratch]
        at = [sum(cuts[: k + 1]) for k in range(len(cuts))]
        ins, sources, outs, sums, own = (refs[a:b] for a, b in zip(at[:-1], at[1:]))
        moving = work.bind(sources, sums, refs[at[-1] :])
        step = pl.program_id(0)

        def hook(place):
            for when in sorted({when for when, where in schedule if where == place}):

                @pl.when(step == when)
                def _(when=when):
                    for at, slot in enumerate(schedule):
                        if slot == (when, place):
                            tick(moving, at)

        @pl.when(step == 0)
        def _():
            greet_partners()
            tick(moving, -1)

        hook(0)
        kernel(*ins, *outs, *own, hook=hook)

        @pl.when(step == steps - 1)
        def _():
            for at in range(len(schedule), work.ticks):
                tick(moving, at)
            settle(moving)

    return run


def alone_kernel(work, *refs):
    n, m = len(work.in_specs), len(work.out_specs)
    moving = work.bind(refs[:n], refs[n : n + m], refs[n + m :])
    greet_partners()
    for at in range(-1, work.ticks):
        tick(moving, at)
    settle(moving)


def alone(work, collective_id):
    outs = pl.pallas_call(
        functools.partial(alone_kernel, work),
        in_specs=work.in_specs,
        out_specs=work.out_specs,
        out_shape=work.out_shape,
        scratch_shapes=work.scratch,
        compiler_params=params(collective_id=collective_id, has_side_effects=True),
        name="gather_weights",
    )(*work.arrays)
    return work.results(outs)


class Doubling:
    def __init__(self, source, landed, send_sems, recv_sems):
        self.buffers = [source, *landed]
        self.send_sems, self.recv_sems = send_sems, recv_sems

    def swap(self, stage):
        return pltpu.make_async_remote_copy(
            src_ref=self.buffers[stage],
            dst_ref=self.buffers[stage + 1],
            send_sem=self.send_sems.at[stage],
            recv_sem=self.recv_sems.at[stage],
            device_id=partner(*cube_dims()[stage]),
            device_id_type=pl.DeviceIdType.MESH,
        )

    def step(self, stage):
        if stage >= 0:
            self.swap(stage).wait_recv()
            self.buffers[stage + 1][...] += self.buffers[stage][...]
        if stage + 2 < len(self.buffers):
            self.swap(stage + 1).start()

    def settle(self):
        for stage in range(len(self.buffers) - 1):
            self.swap(stage).wait_send()


def doubling_scratch(shape):
    stages = len(cube_dims())
    return [pltpu.VMEM(shape, jnp.float32)] * (stages + 1) + [pltpu.SemaphoreType.DMA((stages,))] * 2


def on_device(
    image_tokens, text_states, text_segments, image_segment, out_grad,
    norm1_gain, norm1_bias, self_query, self_key, self_value, self_output,
    norm2_gain, norm2_bias, cross_query, cross_key, cross_value, cross_output,
    norm3_gain, norm3_bias, mlp_in, mlp_in_bias, mlp_out, mlp_out_bias,
):
    tokens = image_tokens[0]
    rows, width = tokens.shape
    hidden = mlp_in.shape[1]
    vectors = (
        norm1_gain, norm1_bias, norm2_gain, norm2_bias,
        norm3_gain, norm3_bias, mlp_in_bias, mlp_out_bias,
    )
    sizes = [v.shape[0] for v in vectors]
    shard = self_query.shape[0]
    owners = width // shard
    parts = hidden // width
    orders = halving_orders()
    spread = [order[::-1] for order in orders]
    w_query, w_key, w_value, shared, text_full = alone(
        Gather(
            [(w, spread, (1, 16)) for w in (self_query, self_key, self_value, pack_vectors(vectors))]
            + [(text_states[0], [cube_dims(("narrow",))], (1, 32))]
        ),
        1,
    )
    shared = shared.reshape(owners, -1, 128)
    given = shared[:, :, :shard].transpose(1, 0, 2).reshape(-1, width)
    up_bias = shared[:, 6, : sizes[6]].reshape(1, -1)
    mask = (text_segments[0] == image_segment[0, 0]).astype(jnp.int32)
    mask = jnp.concatenate([mask, mask]).reshape(-1, 1)

    late = parts // 2

    def part(k):
        return (mlp_in, spread, (2, 16), width * k, width * (k + 1))

    (normed_one, queries, keys, values, mixed_self, sums_self), (*weights_two, up_first) = attend(
        tokens, given, (w_query, w_key, w_value),
        Gather(
            [
                (w, spread, (2, 16))
                for w in (self_output, cross_query, cross_key, cross_value, cross_output)
            ]
            + [(mlp_in, spread, (2, 16), 0, width)]
        ),
        ((1, 0), (2, 0), (3, 0), (5, 0)), 2,
    )
    (x1, h2, q2, a2, x2, h3, k2, v2), (down, *up_more) = middle(
        tokens, mixed_self, text_full, mask, given, weights_two,
        Gather([(mlp_out, spread, (2, 16))] + [part(k) for k in range(1, parts - late)]),
        ((0, 1), (1, 1), (2, 0), (3, 0)), 3,
    )
    (
        dx2, grad_up_bias, grad_gain_three, grad_bias_three, grad_down_bias,
        grad_down, hidden_act, grad_up, near_sums,
    ) = mlp(
        x2, h3, out_grad[0], given, [up_first, *up_more],
        Gather([(mlp_in, spread, (1, 16), width * k, width * (k + 1)) for k in range(parts - late, parts)]),
        up_bias, down, 2, ((2, 3, 5, 7, 8), (0, 1, 3, 5, 6, 7)), orders[4:], 4,
    )
    w_output, c_query, c_key, c_value, c_output = weights_two
    (
        dx1, grad_mixed, grad_self_out, grad_cross_query, grad_cross_out, grad_k2, grad_v2,
        grad_gain_two, grad_bias_two,
    ), (grad_down,) = middle_back(
        dx2, x1, mixed_self, h2, q2, a2, k2, v2, mask, given, (w_output, c_query, c_output),
        Scatter([(grad_down, orders, (1, 16))]), ((0, 1), (2, 1), (3, 1)), 5,
    )
    (
        grad_queries, grad_keys, grad_values, *late, text_term,
    ), (*far_sums, grad_self_out, grad_cross_query, grad_cross_out) = attend_back(
        queries, keys, values, grad_mixed, sums_self, normed_one,
        (grad_k2, grad_v2, text_full, c_key, c_value),
        Scatter(
            [(g, orders, (1, 32)) for g in (*grad_up, grad_self_out, grad_cross_query, grad_cross_out)]
        ),
        ((1, 0), (4, 0), (6, 0), (7, 0)), 6,
    )
    self_terms = (grad_queries, grad_keys, grad_values)
    others = (
        grad_gain_two, grad_bias_two, grad_gain_three, grad_bias_three, grad_down_bias, grad_up_bias,
    )
    (image_grad, block_out, vector_sums), (
        grad_self_query, grad_self_key, grad_self_value, grad_cross_key, grad_cross_value, text_grad,
    ) = first_back(
        tokens, dx1, given, others, (w_query, w_key, w_value), self_terms, x2, hidden_act, down,
        Scatter(
            [(g, orders, (1, 16)) for g in late] + [(text_term, [cube_dims(("narrow",))], (1, 32))]
        ),
        (1,), 7,
    )
    (
        grad_self_query, grad_self_key, grad_self_value, grad_self_out,
        grad_cross_query, grad_cross_key, grad_cross_value, grad_cross_out,
        grad_up, grad_down, text_grad,
    ) = hand_over(
        [
            (g,)
            for g in (
                grad_self_query, grad_self_key, grad_self_value, grad_self_out,
                grad_cross_query, grad_cross_key, grad_cross_value, grad_cross_out,
            )
        ]
        + [(*near_sums, *far_sums), (grad_down,), (text_grad,)]
    )
    place = lax.axis_index(AXES)
    flat = vector_sums.reshape(-1)
    rows_of = (0, 1, 2, 3, 4, 5, 7, 6)
    vector_grads = [
        lax.dynamic_slice_in_dim(flat, row * width + place * size, size)
        for row, size in zip(rows_of, sizes)
    ]
    return (
        block_out[None], image_grad[None], text_grad[None],
        vector_grads[0], vector_grads[1],
        grad_self_query, grad_self_key, grad_self_value, grad_self_out,
        vector_grads[2], vector_grads[3],
        grad_cross_query, grad_cross_key, grad_cross_value, grad_cross_out,
        vector_grads[4], vector_grads[5],
        grad_up, vector_grads[6], grad_down, vector_grads[7],
    )


def solution(mesh):
    placed = (
        P(("wide", "narrow"), None, None),
        P("wide", "narrow", None),
        P("wide", None),
        P("wide", "narrow"),
        P(("wide", "narrow"), None, None),
        P(("wide", "narrow")),
        P(("wide", "narrow")),
        P(("wide", "narrow"), None),
        P(("wide", "narrow"), None),
        P(("wide", "narrow"), None),
        P(("wide", "narrow"), None),
        P(("wide", "narrow")),
        P(("wide", "narrow")),
        P(("wide", "narrow"), None),
        P(("wide", "narrow"), None),
        P(("wide", "narrow"), None),
        P(("wide", "narrow"), None),
        P(("wide", "narrow")),
        P(("wide", "narrow")),
        P(("wide", "narrow"), None),
        P(("wide", "narrow")),
        P(("wide", "narrow"), None),
        P(("wide", "narrow")),
    )
    return jax.shard_map(
        on_device,
        mesh=mesh,
        in_specs=placed,
        out_specs=(
            P(("wide", "narrow"), None, None),
            P(("wide", "narrow"), None, None),
            P("wide", "narrow", None),
            P(("wide", "narrow")),
            P(("wide", "narrow")),
            P(("wide", "narrow"), None),
            P(("wide", "narrow"), None),
            P(("wide", "narrow"), None),
            P(("wide", "narrow"), None),
            P(("wide", "narrow")),
            P(("wide", "narrow")),
            P(("wide", "narrow"), None),
            P(("wide", "narrow"), None),
            P(("wide", "narrow"), None),
            P(("wide", "narrow"), None),
            P(("wide", "narrow")),
            P(("wide", "narrow")),
            P(("wide", "narrow"), None),
            P(("wide", "narrow")),
            P(("wide", "narrow"), None),
            P(("wide", "narrow")),
        ),
        check_vma=False,
    )
```

```python
import functools
import math

import jax
import jax.numpy as jnp
from jax import lax
from jax.experimental import pallas as pl
from jax.experimental.pallas import tpu as pltpu
from jax.sharding import PartitionSpec as P

HEAD_DIM = 64
TILE = 256
BF16 = jnp.bfloat16
VMEM_LIMIT = 60 * 1024 * 1024
MLP_STEPS = 8
MLP_TILE = 1024
VECTOR_ROWS = 16

EPSILON = 1e-05
NEGATIVE = -1e30

AXES = ("wide", "narrow")


def axis_bits(axis):
    return lax.axis_size(axis).bit_length() - 1


def pack_vectors(vectors):
    room = 1024
    placed = [
        jnp.pad(v.astype(jnp.float32), (128 * k, room - 128 * k - v.shape[0]))
        for k, v in enumerate(vectors)
    ]
    return sum(placed).reshape(-1, 128)


def nn(a, b):
    return lax.dot_general(a, b, (((1,), (0,)), ((), ())), preferred_element_type=jnp.float32)


def nt(a, b):
    return lax.dot_general(a, b, (((1,), (1,)), ((), ())), preferred_element_type=jnp.float32)


def tn(a, b):
    return lax.dot_general(a, b, (((0,), (0,)), ((), ())), preferred_element_type=jnp.float32)


def standardize(values):
    center = jnp.mean(values, axis=-1, keepdims=True)
    offset = values - center
    rate = lax.rsqrt(jnp.mean(offset * offset, axis=-1, keepdims=True) + EPSILON)
    return offset * rate, rate


def norm_back(standard, rate, gain, grad):
    scaled = grad * gain
    return rate * (
        scaled
        - jnp.mean(scaled, axis=-1, keepdims=True)
        - standard * jnp.mean(scaled * standard, axis=-1, keepdims=True)
    )


def column_sum(values):
    return jnp.sum(values, axis=0, keepdims=True)


def head_lanes(block, head):
    lane = lax.broadcasted_iota(jnp.int32, block.shape, 1)
    inside = (lane >= HEAD_DIM) if head else (lane < HEAD_DIM)
    return jnp.where(inside, block, jnp.zeros_like(block))


def whole_block(shape):
    zeros = (0,) * len(shape)
    return pl.BlockSpec(shape, lambda *_: zeros, pipeline_mode=pl.Buffered(1))


def params(**extra):
    return pltpu.CompilerParams(vmem_limit_bytes=VMEM_LIMIT, **extra)


def attend_kernel(
    x_ref, vectors_ref, wq_ref, wk_ref, wv_ref, h_ref, q_ref, k_ref, v_ref, o_ref, sums_ref,
    hook,
):
    rows = x_ref.shape[0]

    @pl.when(pl.program_id(0) == 0)
    def _():
        for start in range(0, rows, TILE):
            at = slice(start, start + TILE)
            standard, _ = standardize(x_ref[at, :].astype(jnp.float32))
            h_ref[at, :] = (standard * vectors_ref[0:1, :] + vectors_ref[1:2, :]).astype(BF16)

    weights = jnp.concatenate([w[...] for w in (wq_ref, wk_ref, wv_ref)], axis=1)
    mapped = nn(h_ref[...], weights).astype(BF16)
    q_ref[...] = mapped[:, :128]
    k_ref[...] = mapped[:, 128:256]
    v_ref[...] = mapped[:, 256:]
    flipped = v_ref[...].T
    for start in range(0, rows, TILE):
        span = start + TILE
        queries = q_ref[start:span, :] * (HEAD_DIM**-0.5)
        keys = k_ref[:span, :]
        mixed, sums = [], []
        for head in range(2):
            scores = nt(keys, head_lanes(queries, head))
            key_at = lax.broadcasted_iota(jnp.int32, (TILE, TILE), 0)
            query_at = lax.broadcasted_iota(jnp.int32, (TILE, TILE), 1)
            corner = jnp.where(key_at <= query_at, scores[start:], NEGATIVE)
            scores = jnp.concatenate([scores[:start], corner], axis=0) if start else corner
            top = jnp.max(scores, axis=0, keepdims=True)
            powers = jnp.exp(scores - top)
            total = jnp.sum(powers, axis=0, keepdims=True)
            part = nn(flipped[HEAD_DIM * head : HEAD_DIM * (head + 1), :span], powers.astype(BF16))
            mixed.append(part * (1.0 / total))
            sums.append(top + jnp.log(total))
        o_ref[start:span, :] = jnp.concatenate(mixed, axis=0).T.astype(BF16)
        sums_ref[0, :, start:span] = jnp.concatenate(sums, axis=0)


def attend(tokens, vectors, weights, work, schedule, collective_id):
    rows, width = tokens.shape
    pairs = width // 128
    block = pl.BlockSpec((rows, 128), lambda p: (0, p))
    like = jax.ShapeDtypeStruct(tokens.shape, BF16)
    results = pl.pallas_call(
        beside(attend_kernel, work, (5, 6, 0), schedule, pairs),
        grid=(pairs,),
        in_specs=[whole_block(tokens.shape), whole_block(vectors.shape)]
        + [pl.BlockSpec((width, 128), lambda p: (0, p))] * 3
        + work.in_specs,
        out_specs=[whole_block(tokens.shape)]
        + [block] * 4
        + [pl.BlockSpec((1, 2, rows), lambda p: (p, 0, 0))]
        + work.out_specs,
        out_shape=[like] * 5
        + [jax.ShapeDtypeStruct((pairs, 2, rows), jnp.float32)]
        + work.out_shape,
        scratch_shapes=work.scratch,
        compiler_params=params(collective_id=collective_id, has_side_effects=True),
        name="self_attend",
    )(tokens, vectors, *weights, *work.arrays)
    return results[:6], work.results(results[6:])


def attend_back_kernel(
    q_ref, k_ref, v_ref, da_ref, sums_ref, h_ref, dk2_ref, dv2_ref, text_ref, ck_ref, cv_ref,
    dq_ref, dk_ref, dv_ref, dwq_ref, dwk_ref, dwv_ref, dck_ref, dcv_ref, dtext_ref,
    dk_sum, dv_sum, h_flip, hook,
):
    rows, width = q_ref.shape

    @pl.when(pl.program_id(0) == 0)
    def _():
        h_flip[...] = h_ref[...].T
        dck_ref[...] = tn(text_ref[...], dk2_ref[...]).astype(BF16)
        dcv_ref[...] = tn(text_ref[...], dv2_ref[...]).astype(BF16)
        dtext_ref[...] = nt(dk2_ref[...], ck_ref[...]) + nt(dv2_ref[...], cv_ref[...])

    flipped = k_ref[...].T
    for start in reversed(range(0, rows, TILE)):
        if start == TILE:
            hook(1)
        span = start + TILE
        queries = q_ref[start:span, :] * (HEAD_DIM**-0.5)
        grads = da_ref[start:span, :]
        keys = k_ref[:span, :]
        values = v_ref[:span, :]
        parts = []
        for head in range(2):
            own_queries = head_lanes(queries, head)
            own_grads = head_lanes(grads, head)
            scores = nt(keys, own_queries)
            key_at = lax.broadcasted_iota(jnp.int32, (TILE, TILE), 0)
            query_at = lax.broadcasted_iota(jnp.int32, (TILE, TILE), 1)
            corner = jnp.where(key_at <= query_at, scores[start:], NEGATIVE)
            scores = jnp.concatenate([scores[:start], corner], axis=0) if start else corner
            probs = jnp.exp(scores - sums_ref[0, head : head + 1, start:span])
            grad_probs = nt(values, own_grads)
            inner = jnp.sum(probs * grad_probs, axis=0, keepdims=True)
            grad_scores = (probs * (grad_probs - inner)).astype(BF16)
            value_term = nn(probs.astype(BF16), own_grads)
            key_term = nn(grad_scores, own_queries)
            if span == rows and head == 0:
                dv_sum[...] = value_term
                dk_sum[...] = key_term
            else:
                dv_sum[:span, :] += value_term
                dk_sum[:span, :] += key_term
            parts.append(nn(flipped[HEAD_DIM * head : HEAD_DIM * (head + 1), :span], grad_scores))
        dq = jnp.concatenate(parts, axis=0).T * (HEAD_DIM**-0.5)
        dq_ref[start:span, :] = dq.astype(BF16)
    dk_ref[...] = dk_sum[...].astype(BF16)
    dv_ref[...] = dv_sum[...].astype(BF16)
    grads = jnp.concatenate([dq_ref[...], dk_ref[...], dv_ref[...]], axis=1)
    weights = nn(h_flip[...], grads).astype(BF16)
    dwq_ref[...] = weights[:, :128]
    dwk_ref[...] = weights[:, 128:256]
    dwv_ref[...] = weights[:, 256:]


def attend_back(queries, keys, values, grads, sums, normed, cross, work, schedule, collective_id):
    rows, width = queries.shape
    steps = width // 128
    block = pl.BlockSpec((rows, 128), lambda p: (0, p))
    results = pl.pallas_call(
        beside(attend_back_kernel, work, (11, 9, 3), schedule, steps),
        grid=(steps,),
        in_specs=[block] * 4
        + [pl.BlockSpec((1, 2, rows), lambda p: (p, 0, 0)), whole_block(normed.shape)]
        + [whole_block(c.shape) for c in cross]
        + work.in_specs,
        out_specs=[block] * 6
        + [whole_block((width, width))] * 2
        + [whole_block(cross[2].shape)]
        + work.out_specs,
        out_shape=[jax.ShapeDtypeStruct(queries.shape, BF16)] * 3
        + [jax.ShapeDtypeStruct((width, width), BF16)] * 5
        + [jax.ShapeDtypeStruct(cross[2].shape, jnp.float32)]
        + work.out_shape,
        scratch_shapes=[pltpu.VMEM((rows, 128), jnp.float32)] * 2
        + [pltpu.VMEM((width, rows), BF16)]
        + work.scratch,
        compiler_params=params(collective_id=collective_id, has_side_effects=True),
        name="self_attend_back",
    )(queries, keys, values, grads, sums, normed, *cross, *work.arrays)
    return results[:9], work.results(results[9:])


def gelu_both(values):
    phi = 0.5 + 0.5 * lax.erf(values * (0.5**0.5))
    density = jnp.exp(-0.5 * values * values) * ((2.0 * math.pi) ** -0.5)
    return values * phi, phi + values * density


def mlp_kernel(
    near, far, paces, coming, work, x_ref, h_ref, g_ref, vectors_ref, ub_ref, down_ref, *refs
):
    parts = near + far
    late = len(coming.arrays)
    per = MLP_STEPS // parts
    early_refs, refs = refs[: parts - late], refs[parts - late :]
    shard_refs, refs = refs[:late], refs[late:]
    dx_ref, dub_ref, dgain_ref, dbias_ref, gsum_ref, ddown_ref, act = refs[:7]
    far_refs, refs = refs[7 : 7 + far], refs[7 + far :]
    sums, refs = refs[:near], refs[near:]
    dh_sum, h_flip, up, grad_act = refs[:4]
    near_refs, refs = refs[4 : 4 + near], refs[4 + near :]
    late_refs, refs = refs[:late], refs[late:]
    step, steps = pl.program_id(0), pl.num_programs(0)
    rows = h_ref.shape[0]
    chunk = up.shape[1]
    moving = work.bind(near_refs, sums, refs[: len(work.scratch)])
    arriving = coming.bind(shard_refs, late_refs, refs[len(work.scratch) :])

    @pl.when(step == 0)
    def _():
        greet_partners()
        tick(arriving, -1)
        h_flip[...] = h_ref[...].T
        dh_sum[...] = jnp.zeros_like(dh_sum)

    left, due = [], {}
    for at in range(coming.ticks):
        due.setdefault(paces[0][at], []).append((arriving, at, None))
    for part in range(near):
        pieces = [k for k, p in enumerate(work.pieces) if p[0][0] == part]
        for at in range(-1, work.ticks):
            place = 2 * per * (part + 1) + paces[1][at + 1]
            if place < 2 * MLP_STEPS:
                due.setdefault(place, []).append((moving, at, pieces))
            else:
                left.append((moving, at, pieces))

    def move(half):
        for place in due:
            if place % 2 == half:

                @pl.when(step == place // 2)
                def _(place=place):
                    for mover, at, pieces in due[place]:
                        tick(mover, at, pieces)

    move(0)
    for place in range(MLP_STEPS):

        @pl.when(step == place)
        def _(place=place):
            part, first = place // per, chunk * (place % per)
            if part < parts - late:
                up[...] = early_refs[part][...]
            else:
                ref = late_refs[part - parts + late]
                up[...] = ref[..., first : first + chunk].reshape(up.shape)

    down = down_ref[...]
    bias_sum = jnp.zeros_like(dub_ref)
    for start in range(0, rows, MLP_TILE):
        at = slice(start, start + MLP_TILE)
        hidden, slope = gelu_both(nn(h_ref[at, :], up[...]) + ub_ref[...])
        act[at, :] = hidden.astype(BF16)
        grad_pre = (nt(g_ref[at, :], down) * slope).astype(BF16)
        grad_act[at, :] = grad_pre
        bias_sum += column_sum(grad_pre.astype(jnp.float32))
        dh_sum[at, :] += nt(grad_pre, up[...])
    dub_ref[...] = bias_sum
    move(1)
    grad_up = nn(h_flip[...], grad_act[...]).astype(BF16)
    for part, ref in enumerate(far_refs):

        @pl.when(step // per == near + part)
        def _(ref=ref):
            ref[...] = grad_up

    for place in range(near * per):

        @pl.when(step == place)
        def _(place=place):
            ref = near_refs[place // per]
            first = chunk * (place % per)
            ref[..., first : first + chunk] = grad_up.reshape(ref.shape[:-1] + (chunk,))

    ddown_ref[...] = tn(act[...], g_ref[...]).astype(BF16)

    @pl.when(step == steps - 1)
    def _():
        gain_sum = jnp.zeros_like(dgain_ref)
        grad_sum = jnp.zeros_like(dbias_ref)
        tail_sum = jnp.zeros_like(gsum_ref)
        for start in range(0, rows, TILE):
            at = slice(start, start + TILE)
            standard, rate = standardize(x_ref[at, :])
            grad = dh_sum[at, :]
            tail = g_ref[at, :].astype(jnp.float32)
            dx_ref[at, :] = tail + norm_back(standard, rate, vectors_ref[4:5, :], grad)
            gain_sum += column_sum(grad * standard)
            grad_sum += column_sum(grad)
            tail_sum += column_sum(tail)
        dgain_ref[...] = gain_sum
        dbias_ref[...] = grad_sum
        gsum_ref[...] = tail_sum
        for mover, at, pieces in left:
            tick(mover, at, pieces)
        settle(moving)
        settle(arriving)


def mlp(x, h, g, vectors, early, coming, up_bias, down, near, paces, orders, collective_id):
    rows, width = x.shape
    hidden = up_bias.shape[1]
    chunk = hidden // MLP_STEPS
    f32 = jnp.float32
    row = (1, width)
    parts = hidden // width
    per = width // chunk
    lead = (2,) * len(cube_dims())
    block = lead + (width >> len(lead), width)
    source = jax.ShapeDtypeStruct(block, BF16)
    work = Scatter([(source, orders, (1, 16))] * near, near=True)
    far = parts - near
    more = range(1, 1 + len(cube_dims()))
    paces = [[*pace, *(pace[-1] + k for k in more)] for pace in paces]

    def part_of(k):
        return pl.BlockSpec((width, chunk), lambda c: (0, jnp.clip(c - per * k, 0, per - 1)))

    results = pl.pallas_call(
        functools.partial(mlp_kernel, near, far, paces, coming, work),
        grid=(MLP_STEPS,),
        in_specs=[
            whole_block(x.shape), whole_block(h.shape), whole_block(g.shape), whole_block(vectors.shape),
            pl.BlockSpec((1, chunk), lambda c: (0, c)),
            pl.BlockSpec((chunk, width), lambda c: (c, 0)),
        ]
        + [part_of(k) for k in range(len(early))]
        + coming.in_specs,
        out_specs=[
            whole_block(x.shape),
            pl.BlockSpec((1, chunk), lambda c: (0, c)),
            whole_block(row), whole_block(row), whole_block(row),
            pl.BlockSpec((chunk, width), lambda c: (c, 0)),
            pl.BlockSpec((rows, chunk), lambda c: (0, c)),
        ]
        + [part_of(k) for k in range(near, parts)]
        + work.out_specs,
        out_shape=[
            jax.ShapeDtypeStruct(x.shape, f32),
            jax.ShapeDtypeStruct((1, hidden), f32),
            jax.ShapeDtypeStruct(row, f32), jax.ShapeDtypeStruct(row, f32), jax.ShapeDtypeStruct(row, f32),
            jax.ShapeDtypeStruct((hidden, width), BF16),
            jax.ShapeDtypeStruct((rows, hidden), BF16),
        ]
        + [jax.ShapeDtypeStruct((width, width), BF16)] * far
        + work.out_shape,
        scratch_shapes=[
            pltpu.VMEM(x.shape, f32), pltpu.VMEM((width, rows), BF16),
            pltpu.VMEM((width, chunk), BF16), pltpu.VMEM((rows, chunk), BF16),
        ]
        + [pltpu.VMEM(block, BF16)] * near
        + [pltpu.VMEM(b, BF16) for b in coming.blocks]
        + work.scratch
        + coming.scratch,
        compiler_params=params(collective_id=collective_id, has_side_effects=True),
        name="mlp_both_ways",
    )(x, h, g, vectors, up_bias, down, *early, *coming.arrays)
    return *results[:7], results[7 : 7 + far], work.results(results[7 + far :])


def load_all(sources, buffers, sems):
    copies = [
        pltpu.make_async_copy(source, buffer, sems.at[k])
        for k, (source, buffer) in enumerate(zip(sources, buffers))
    ]
    for copy in copies:
        copy.start()
    for copy in copies:
        copy.wait()


def room_for(arrays):
    return [pltpu.VMEM(a.shape, a.dtype) for a in arrays] + [pltpu.SemaphoreType.DMA((len(arrays),))]


def stack_heads(pair):
    return jnp.concatenate([head_lanes(pair, 0), head_lanes(pair, 1)], axis=0)


def by_head(stacked):
    return stacked.reshape(2, stacked.shape[0] // 2, stacked.shape[1])


def caption_probs(keys, queries, mask):
    scores = by_head(jnp.where(mask != 0, nt(keys, queries), NEGATIVE))
    powers = jnp.exp(scores - jnp.max(scores, axis=1, keepdims=True))
    return powers * (1.0 / jnp.sum(powers, axis=1, keepdims=True))


def middle_kernel(
    x_ref, a_ref, text_ref, mask_ref, vectors_ref,
    wo_hbm, cq_hbm, ck_hbm, cv_hbm, co_hbm,
    x1_ref, h2_ref, q2_ref, a2_ref, x2_ref, h3_ref, k2_ref, v2_ref, keys, values_flip,
    wo_ref, cq_ref, ck_ref, cv_ref, co_ref, weight_sems,
    hook,
):
    @pl.when(pl.program_id(0) == 0)
    def _():
        load_all(
            (wo_hbm, cq_hbm, ck_hbm, cv_hbm, co_hbm),
            (wo_ref, cq_ref, ck_ref, cv_ref, co_ref),
            weight_sems,
        )
        k2_ref[...] = nn(text_ref[...], ck_ref[...]).astype(BF16)
        v2_ref[...] = nn(text_ref[...], cv_ref[...]).astype(BF16)
        for pair in range(keys.shape[0]):
            at = slice(128 * pair, 128 * (pair + 1))
            keys[pair] = stack_heads(k2_ref[:, at])
            values_flip[pair] = stack_heads(v2_ref[:, at]).T

    after_self = x_ref[...].astype(jnp.float32) + nn(a_ref[...], wo_ref[...])
    x1_ref[...] = after_self
    standard, _ = standardize(after_self)
    normed = (standard * vectors_ref[2:3, :] + vectors_ref[3:4, :]).astype(BF16)
    h2_ref[...] = normed
    q2_ref[...] = nn(normed, cq_ref[...]).astype(BF16)
    mask = mask_ref[...]
    for pair in range(q2_ref.shape[1] // 128):
        at = slice(128 * pair, 128 * (pair + 1))
        queries = q2_ref[:, at] * (HEAD_DIM**-0.5)
        probs = caption_probs(keys[pair], queries, mask).astype(BF16)
        mixed = nn(values_flip[pair], probs.reshape(-1, probs.shape[2]))
        a2_ref[:, at] = mixed.T.astype(BF16)
    hook(1)
    after_cross = after_self + nn(a2_ref[...], co_ref[...])
    x2_ref[...] = after_cross
    standard, _ = standardize(after_cross)
    h3_ref[...] = (standard * vectors_ref[4:5, :] + vectors_ref[5:6, :]).astype(BF16)


def middle(tokens, mixed, text, mask, vectors, weights, work, schedule, collective_id):
    rows, width = tokens.shape
    slots = text.shape[0]
    tile = pl.BlockSpec((TILE, width), lambda i: (i, 0))
    f32 = jnp.float32
    like = lambda dtype: jax.ShapeDtypeStruct(tokens.shape, dtype)
    results = pl.pallas_call(
        beside(middle_kernel, work, (10, 8, 8), schedule, rows // TILE),
        grid=(rows // TILE,),
        in_specs=[
            tile, tile, whole_block(text.shape), whole_block(mask.shape),
            whole_block(vectors.shape), *[pl.BlockSpec(memory_space=pl.ANY)] * 5, *work.in_specs,
        ],
        out_specs=[tile] * 6 + [whole_block(text.shape)] * 2 + work.out_specs,
        out_shape=[like(f32), like(BF16), like(BF16), like(BF16), like(f32), like(BF16)]
        + [jax.ShapeDtypeStruct(text.shape, BF16)] * 2
        + work.out_shape,
        scratch_shapes=[
            pltpu.VMEM((width // 128, 2 * slots, 128), BF16),
            pltpu.VMEM((width // 128, 128, 2 * slots), BF16),
        ]
        + room_for(weights)
        + work.scratch,
        compiler_params=params(collective_id=collective_id, has_side_effects=True),
        name="output_and_cross",
    )(tokens, mixed, text, mask, vectors, *weights, *work.arrays)
    return results[:8], work.results(results[8:])


def middle_back_kernel(
    dx2_ref, x1_ref, a1_ref, h2_ref, q2_ref, a2_ref, k2_ref, v2_ref, mask_ref, vectors_ref,
    wo_ref, cq_ref, co_ref,
    dx1_ref, da1_ref, dwo_ref, dcq_ref, dco_ref, dk2_ref, dv2_ref, dgain_ref, dbias_ref,
    wo_sum, cq_sum, co_sum, dk_sum, dv_sum, dq2, keys, keys_flip, values,
    hook,
):
    step, steps = pl.program_id(0), pl.num_programs(0)
    pairs = keys.shape[0]
    slots = k2_ref.shape[0]

    @pl.when(step == 0)
    def _():
        for ref in (wo_sum, cq_sum, co_sum, dk_sum, dv_sum, dgain_ref, dbias_ref):
            ref[...] = jnp.zeros_like(ref)
        for pair in range(pairs):
            at = slice(128 * pair, 128 * (pair + 1))
            keys[pair] = stack_heads(k2_ref[:, at])
            keys_flip[pair] = keys[pair].T
            values[pair] = stack_heads(v2_ref[:, at])

    grad_out = dx2_ref[...].astype(BF16)
    co_sum[...] += tn(a2_ref[...], grad_out)
    grad_mixed = nt(grad_out, co_ref[...]).astype(BF16)
    mask = mask_ref[...]
    for pair in range(pairs):
        at = slice(128 * pair, 128 * (pair + 1))
        queries = q2_ref[:, at] * (HEAD_DIM**-0.5)
        grads = grad_mixed[:, at]
        probs = caption_probs(keys[pair], queries, mask)
        grad_probs = by_head(nt(values[pair], grads))
        inner = jnp.sum(probs * grad_probs, axis=1, keepdims=True)
        grad_scores = (probs * (grad_probs - inner)).astype(BF16).reshape(2 * slots, -1)
        dv_sum[pair] += nn(probs.astype(BF16).reshape(2 * slots, -1), grads)
        dk_sum[pair] += nn(grad_scores, queries)
        dq2[:, at] = (nn(keys_flip[pair], grad_scores).T * (HEAD_DIM**-0.5)).astype(BF16)
    hook(1)
    cq_sum[...] += tn(h2_ref[...], dq2[...])
    grad_normed = nt(dq2[...], cq_ref[...])
    standard, rate = standardize(x1_ref[...])
    grad_after = dx2_ref[...] + norm_back(standard, rate, vectors_ref[2:3, :], grad_normed)
    dgain_ref[...] += column_sum(grad_normed * standard)
    dbias_ref[...] += column_sum(grad_normed)
    dx1_ref[...] = grad_after
    grad_self = grad_after.astype(BF16)
    wo_sum[...] += tn(a1_ref[...], grad_self)
    da1_ref[...] = nt(grad_self, wo_ref[...]).astype(BF16)

    @pl.when(step == steps - 1)
    def _():
        dwo_ref[...] = wo_sum[...].astype(BF16)
        dcq_ref[...] = cq_sum[...].astype(BF16)
        dco_ref[...] = co_sum[...].astype(BF16)
        for pair in range(pairs):
            at = slice(128 * pair, 128 * (pair + 1))
            for total, ref in ((dk_sum, dk2_ref), (dv_sum, dv2_ref)):
                upper, lower = total[pair, :slots], total[pair, slots:]
                ref[:, at] = (head_lanes(upper, 0) + head_lanes(lower, 1)).astype(BF16)


def middle_back(
    dx2, x1, a1, h2, q2, a2, k2, v2, mask, vectors, weights, work, schedule, collective_id
):
    rows, width = x1.shape
    slots = k2.shape[0]
    pairs = width // 128
    tile = pl.BlockSpec((TILE, width), lambda i: (i, 0))
    f32 = jnp.float32
    matrix = (width, width)
    results = pl.pallas_call(
        beside(middle_back_kernel, work, (13, 9, 9), schedule, rows // TILE),
        grid=(rows // TILE,),
        in_specs=[tile] * 6
        + [whole_block(v.shape) for v in (k2, v2, mask, vectors, *weights)]
        + work.in_specs,
        out_specs=[tile] * 2
        + [whole_block(matrix)] * 3
        + [whole_block(k2.shape)] * 2
        + [whole_block((1, width))] * 2
        + work.out_specs,
        out_shape=[jax.ShapeDtypeStruct(x1.shape, f32), jax.ShapeDtypeStruct(x1.shape, BF16)]
        + [jax.ShapeDtypeStruct(matrix, BF16)] * 3
        + [jax.ShapeDtypeStruct(k2.shape, BF16)] * 2
        + [jax.ShapeDtypeStruct((1, width), f32)] * 2
        + work.out_shape,
        scratch_shapes=[pltpu.VMEM(matrix, f32)] * 3
        + [pltpu.VMEM((pairs, 2 * slots, 128), f32)] * 2
        + [
            pltpu.VMEM((TILE, width), BF16),
            pltpu.VMEM((pairs, 2 * slots, 128), BF16),
            pltpu.VMEM((pairs, 128, 2 * slots), BF16),
            pltpu.VMEM((pairs, 2 * slots, 128), BF16),
        ]
        + work.scratch,
        compiler_params=params(collective_id=collective_id, has_side_effects=True),
        name="cross_back",
    )(dx2, x1, a1, h2, q2, a2, k2, v2, mask, vectors, *weights, *work.arrays)
    return results[:9], work.results(results[9:])


def first_back_kernel(
    work, schedule, steps, x_ref, dx1_ref, given_ref, gain2_ref, bias2_ref, gain3_ref, bias3_ref, db_ref, ub_ref,
    wq_ref, wk_ref, wv_ref, dq_ref, dk_ref, dv_ref,
    x2_ref, act_ref, down_ref, *refs,
):
    n, m = len(work.in_specs), len(work.out_specs)
    sources, (dx_ref, out_ref, vector_sum_ref) = refs[:n], refs[n : n + 3]
    sums, rest = refs[n + 3 : n + 3 + m], refs[n + 3 + m :]
    stages = len(cube_dims())
    doubling = Doubling(rest[0], rest[1 : stages + 1], *rest[stages + 1 : stages + 3])
    halving = work.bind(sources, sums, rest[stages + 3 :])
    step = pl.program_id(0)
    vectors = doubling.buffers[0]

    @pl.when(step == 0)
    def _():
        greet_partners()
        tick(halving, -1)
        vectors[...] = jnp.zeros_like(vectors)
        for row, ref in enumerate((gain2_ref, bias2_ref, gain3_ref, bias3_ref, db_ref)):
            vectors[row + 2 : row + 3, :] = ref[...]
        width = vectors.shape[1]
        for part in range(ub_ref.shape[1] // width):
            vectors[part + 7 : part + 8, :] = ub_ref[:, width * part : width * (part + 1)]

    for at, place in enumerate(schedule):

        @pl.when(step == place)
        def _(at=at):
            tick(halving, at)

    grad_normed = (
        nt(dq_ref[...], wq_ref[...]) + nt(dk_ref[...], wk_ref[...]) + nt(dv_ref[...], wv_ref[...])
    )
    standard, rate = standardize(x_ref[...].astype(jnp.float32))
    dx_ref[...] = dx1_ref[...] + norm_back(standard, rate, given_ref[0:1, :], grad_normed)
    out = x2_ref[...] + nn(act_ref[...], down_ref[...]) + given_ref[7:8, :]
    out_ref[...] = out.astype(BF16)
    vectors[0:1, :] += column_sum(grad_normed * standard)
    vectors[1:2, :] += column_sum(grad_normed)

    @pl.when(step == steps - 1)
    def _():
        doubling.step(-1)
        for at in range(max(stages, work.ticks)):
            if at < stages:
                doubling.step(at)
            if len(schedule) + at < work.ticks:
                tick(halving, len(schedule) + at)
        vector_sum_ref[...] = doubling.buffers[-1][...]
        doubling.settle()
        settle(halving)


def first_back(
    tokens, dx1, given, vectors, weights, grads, x2, act, down, work, schedule, collective_id
):
    rows, width = tokens.shape
    steps = rows // TILE
    tile = pl.BlockSpec((TILE, width), lambda i: (i, 0))
    f32 = jnp.float32
    results = pl.pallas_call(
        functools.partial(first_back_kernel, work, schedule, steps),
        grid=(steps,),
        in_specs=[tile] * 2
        + [whole_block(v.shape) for v in (given, *vectors)]
        + [whole_block(w.shape) for w in weights]
        + [tile] * 4
        + [pl.BlockSpec((TILE, act.shape[1]), lambda i: (i, 0)), whole_block(down.shape)]
        + work.in_specs,
        out_specs=[tile, tile, whole_block((VECTOR_ROWS, width))] + work.out_specs,
        out_shape=[
            jax.ShapeDtypeStruct(tokens.shape, f32),
            jax.ShapeDtypeStruct(tokens.shape, BF16),
            jax.ShapeDtypeStruct((VECTOR_ROWS, width), f32),
        ]
        + work.out_shape,
        scratch_shapes=doubling_scratch((VECTOR_ROWS, width)) + work.scratch,
        compiler_params=params(collective_id=collective_id, has_side_effects=True),
        name="self_norm_back",
    )(tokens, dx1, given, *vectors, *weights, *grads, x2, act, down, *work.arrays)
    return results[:3], work.results(results[3:])


def hand_over_kernel(groups, *refs):
    ins, outs = refs[: sum(groups)], refs[sum(groups) :]
    at = 0
    for count, out in zip(groups, outs):
        width = out.shape[1] // count
        for part in range(count):
            out[:, width * part : width * (part + 1)] = ins[at + part][...]
        at += count


def hand_over(groups):
    arrays = [a for group in groups for a in group]
    return pl.pallas_call(
        functools.partial(hand_over_kernel, [len(group) for group in groups]),
        in_specs=[pl.BlockSpec(memory_space=pltpu.VMEM)] * len(arrays),
        out_specs=[pl.BlockSpec(memory_space=pltpu.VMEM)] * len(groups),
        out_shape=[
            jax.ShapeDtypeStruct((g[0].shape[0], sum(a.shape[1] for a in g)), g[0].dtype) for g in groups
        ],
        compiler_params=params(),
        name="hand_over",
    )(*arrays)


def cube_dims(axes=AXES):
    return [(axis, k) for axis in axes for k in reversed(range(axis_bits(axis)))]


def bits_of(dims):
    return [(lax.axis_index(axis) >> bit) & 1 for axis, bit in dims]


def partner(axis, bit):
    return {axis: lax.axis_index(axis) ^ (1 << bit)}


def halving_orders():
    x, y, near, far = ("narrow", 0), ("narrow", 1), ("wide", 1), ("wide", 2)
    core = ("wide", 0)
    six = (
        (far, x, y, near),
        (near, y, x, far),
        (y, far, x, near),
        (x, near, y, far),
        (x, y, far, near),
        (y, x, near, far),
    )
    rest = [d for d in cube_dims() if d not in (core, x, y, near, far)]
    return [[core, *order, *rest] for order in six]


def greet_partners():
    dims = cube_dims()
    barrier = pltpu.get_barrier_semaphore()
    for axis, bit in dims:
        pl.semaphore_signal(
            barrier, inc=1, device_id=partner(axis, bit), device_id_type=pl.DeviceIdType.MESH
        )
    pl.semaphore_wait(barrier, len(dims))


def runs_of(rows, step):
    step = step if rows % step == 0 else rows
    return [(start, step) for start in range(0, rows, step)]


def columns_of(columns, parts=6):
    if columns <= 1024:
        return [(0, columns)]
    cuts = [columns * k // parts // 128 * 128 for k in range(parts)] + [columns]
    return [(a, b - a) for a, b in zip(cuts[:-1], cuts[1:])]


def cut_up(groups):
    pieces = []
    for which, ((rows, columns), orders, (rounds, step)) in enumerate(groups):
        for start, size in runs_of(rows, step):
            for first, width in columns_of(columns):
                k = len(pieces)
                box = (which, slice(start, start + size), slice(first, first + width))
                pieces.append((box, orders[k % len(orders)], k // 6 % rounds))
    return pieces


def tick(mover, at, pieces=None):
    for piece in range(len(mover.pieces)) if pieces is None else pieces:
        _, order, late = mover.pieces[piece]
        stage = at - late
        if 0 <= stage < len(order):
            mover.finish(piece, stage)
        if -1 <= stage < len(order) - 1:
            mover.start(piece, stage + 1)


def settle(mover):
    for piece, (_, order, _) in enumerate(mover.pieces):
        for stage in range(len(order)):
            mover.send(piece, stage).wait_send()


def ticks_of(pieces):
    return max(len(order) + late for _, order, late in pieces)


def places_of(pieces):
    ends = [sum(len(p[1]) for p in pieces[:k]) for k in range(len(pieces) + 1)]
    return ends[:-1], ends[-1]


class Gathering:
    def __init__(self, pieces, dims, firsts, sources, outs, scratch):
        self.pieces, self.dims, self.firsts = pieces, dims, firsts
        self.sources, self.outs = sources, outs
        self.send_sems, self.recv_sems, self.own_sems = scratch
        self.base, _ = places_of(pieces)
        self.ready = set()

    def source(self, piece):
        (which, rows, columns), _, _ = self.pieces[piece]
        first = self.firsts[which]
        return self.sources[which].at[rows, slice(first + columns.start, first + columns.stop)]

    def own(self, piece):
        (which, *box), _, _ = self.pieces[piece]
        there = self.outs[which].at[(*bits_of(self.dims[which]), *box)]
        return pltpu.make_async_copy(self.source(piece), there, self.own_sems.at[piece])

    def send(self, piece, stage):
        (which, *box), order, _ = self.pieces[piece]
        held = order[:stage]
        dims = self.dims[which]
        at = [slice(None) if d in held else b for d, b in zip(dims, bits_of(dims))]
        there = self.outs[which].at[(*at, *box)]
        sem = self.base[piece] + stage
        return pltpu.make_async_remote_copy(
            src_ref=there if stage else self.source(piece),
            dst_ref=there,
            send_sem=self.send_sems.at[sem],
            recv_sem=self.recv_sems.at[sem],
            device_id=partner(*order[stage]),
            device_id_type=pl.DeviceIdType.MESH,
        )

    def start(self, piece, stage):
        if stage == 0:
            self.own(piece).start()
        if stage == 1:
            self.own(piece).wait()
        self.send(piece, stage).start()

    def finish(self, piece, stage):
        self.send(piece, stage).wait_recv()


class Gather:
    def __init__(self, groups):
        self.arrays, self.firsts, self.shapes, cuts = [], [], [], []
        for array, orders, rounds, *span in groups:
            first, last = span or (0, array.shape[1])
            self.arrays.append(array)
            self.firsts.append(first)
            self.shapes.append((array.shape[0], last - first))
            cuts.append((self.shapes[-1], orders, rounds))
        self.pieces = cut_up(cuts)
        self.dims = [[d for d in cube_dims() if d in group[1][0]] for group in groups]
        self.ticks = ticks_of(self.pieces)
        _, copies = places_of(self.pieces)
        self.in_specs = [pl.BlockSpec(memory_space=pl.ANY)] * len(groups)
        self.out_specs = self.in_specs
        self.blocks = [(2,) * len(d) + s for d, s in zip(self.dims, self.shapes)]
        self.out_shape = [
            jax.ShapeDtypeStruct(b, a.dtype) for b, a in zip(self.blocks, self.arrays)
        ]
        self.scratch = [pltpu.SemaphoreType.DMA((copies,))] * 2
        self.scratch += [pltpu.SemaphoreType.DMA((len(self.pieces),))]

    def bind(self, sources, outs, scratch):
        return Gathering(self.pieces, self.dims, self.firsts, sources, outs, scratch)

    def results(self, outs):
        return [out.reshape(-1, s[1]) for out, s in zip(outs, self.shapes)]


class Halving:
    def __init__(self, pieces, firsts, sources, outs, scratch, near=False):
        count = len(pieces)
        self.firsts = firsts
        self.pieces, self.sources, self.outs, self.near = pieces, sources, outs, near
        self.kept, rest = ([], scratch) if near else (scratch[:count], scratch[count:])
        self.base, _ = places_of(pieces)
        self.landed = []
        for _, order, _ in pieces:
            self.landed.append(rest[: len(order)])
            rest = rest[len(order) :]
        self.send_sems, self.recv_sems = rest[:2]
        self.kept_sems = None if near else rest[2]

    def half(self, piece, stage, other):
        (which, rows, columns), order, _ = self.pieces[piece]
        left = [d for d in cube_dims() if d in order[stage:]]
        bit = bits_of([order[stage]])[0]
        at = [(1 - bit if other else bit) if d == order[stage] else slice(None) for d in left]
        if stage == 0:
            first = self.firsts[which]
            at += [slice(first + rows.start, first + rows.stop), columns]
        return tuple(at)

    def before(self, piece, stage):
        return self.sources[self.pieces[piece][0][0]] if stage == 0 else self.landed[piece][stage - 1]

    def send(self, piece, stage):
        sem = self.base[piece] + stage
        return pltpu.make_async_remote_copy(
            src_ref=self.before(piece, stage).at[self.half(piece, stage, True)],
            dst_ref=self.landed[piece][stage],
            send_sem=self.send_sems.at[sem],
            recv_sem=self.recv_sems.at[sem],
            device_id=partner(*self.pieces[piece][1][stage]),
            device_id_type=pl.DeviceIdType.MESH,
        )

    def keep(self, piece):
        source = self.before(piece, 0).at[self.half(piece, 0, False)]
        return pltpu.make_async_copy(source, self.kept[piece], self.kept_sems.at[piece])

    def start(self, piece, stage):
        self.send(piece, stage).start()
        if stage == 0 and not self.near:
            self.keep(piece).start()

    def finish(self, piece, stage):
        (which, rows, columns), order, _ = self.pieces[piece]
        self.send(piece, stage).wait_recv()
        if stage == 0 and not self.near:
            self.keep(piece).wait()
        landed = self.landed[piece][stage]
        depth = len(order) - 1 - stage
        if stage == 0 and not self.near:
            other, chosen = self.kept[piece], (slice(None),) * depth
        else:
            other, chosen = self.before(piece, stage), self.half(piece, stage, False)
        if depth == 0:
            total = landed[...].astype(jnp.float32) + other[chosen].astype(jnp.float32)
            self.outs[which][rows, columns] = total
            return

        def add(block, carry):
            at = [(block >> k) & 1 for k in reversed(range(depth))]
            rest = iter(at)
            there = [next(rest, c) if isinstance(c, slice) else c for c in chosen]
            landed[tuple(at)] = landed[tuple(at)] + other[tuple(there)]
            return carry

        lax.fori_loop(0, 1 << depth, add, 0, unroll=min(4, 1 << depth))


class Scatter:
    def __init__(self, groups, near=False):
        self.near = near
        self.arrays, self.firsts, shapes, cuts = [], [], [], []
        for array, orders, rounds, *span in groups:
            columns = array.shape[-1]
            block = (array.size // columns >> len(orders[0]), columns)
            self.arrays.append(array if near else array.reshape((2,) * len(orders[0]) + block))
            first, last = span or (0, block[0])
            self.firsts.append(first)
            shapes.append((last - first, columns))
            cuts.append(((last - first, columns), orders, rounds))
        self.pieces = cut_up(cuts)
        self.ticks = ticks_of(self.pieces)
        like = [
            ((rows.stop - rows.start, columns.stop - columns.start), self.arrays[which].dtype, len(order))
            for (which, rows, columns), order, _ in self.pieces
        ]
        kept = [pltpu.VMEM((2,) * (n - 1) + s, d) for s, d, n in like]
        landed = [pltpu.VMEM((2,) * (n - 1 - k) + s, d) for s, d, n in like for k in range(n)]
        _, copies = places_of(self.pieces)
        self.in_specs = [] if near else [pl.BlockSpec(memory_space=pl.ANY)] * len(groups)
        self.out_specs = [whole_block(s) for s in shapes]
        self.out_shape = [jax.ShapeDtypeStruct(s, jnp.float32) for s in shapes]
        self.scratch = ([] if near else kept) + landed + [pltpu.SemaphoreType.DMA((copies,))] * 2
        if not near:
            self.scratch += [pltpu.SemaphoreType.DMA((len(self.pieces),))]

    def bind(self, sources, outs, scratch):
        return Halving(self.pieces, self.firsts, sources, outs, scratch, self.near)

    def results(self, outs):
        return list(outs)


def beside(kernel, work, counts, schedule, steps):
    n_in, n_out, n_scratch = counts

    def run(*refs):
        cuts = [0, n_in, len(work.in_specs), n_out, len(work.out_specs), n_scratch]
        at = [sum(cuts[: k + 1]) for k in range(len(cuts))]
        ins, sources, outs, sums, own = (refs[a:b] for a, b in zip(at[:-1], at[1:]))
        moving = work.bind(sources, sums, refs[at[-1] :])
        step = pl.program_id(0)

        def hook(place):
            for when in sorted({when for when, where in schedule if where == place}):

                @pl.when(step == when)
                def _(when=when):
                    for at, slot in enumerate(schedule):
                        if slot == (when, place):
                            tick(moving, at)

        @pl.when(step == 0)
        def _():
            greet_partners()
            tick(moving, -1)

        hook(0)
        kernel(*ins, *outs, *own, hook=hook)

        @pl.when(step == steps - 1)
        def _():
            for at in range(len(schedule), work.ticks):
                tick(moving, at)
            settle(moving)

    return run


def alone_kernel(work, *refs):
    n, m = len(work.in_specs), len(work.out_specs)
    moving = work.bind(refs[:n], refs[n : n + m], refs[n + m :])
    greet_partners()
    for at in range(-1, work.ticks):
        tick(moving, at)
    settle(moving)


def alone(work, collective_id):
    outs = pl.pallas_call(
        functools.partial(alone_kernel, work),
        in_specs=work.in_specs,
        out_specs=work.out_specs,
        out_shape=work.out_shape,
        scratch_shapes=work.scratch,
        compiler_params=params(collective_id=collective_id, has_side_effects=True),
        name="gather_weights",
    )(*work.arrays)
    return work.results(outs)


class Doubling:
    def __init__(self, source, landed, send_sems, recv_sems):
        self.buffers = [source, *landed]
        self.send_sems, self.recv_sems = send_sems, recv_sems

    def swap(self, stage):
        return pltpu.make_async_remote_copy(
            src_ref=self.buffers[stage],
            dst_ref=self.buffers[stage + 1],
            send_sem=self.send_sems.at[stage],
            recv_sem=self.recv_sems.at[stage],
            device_id=partner(*cube_dims()[stage]),
            device_id_type=pl.DeviceIdType.MESH,
        )

    def step(self, stage):
        if stage >= 0:
            self.swap(stage).wait_recv()
            self.buffers[stage + 1][...] += self.buffers[stage][...]
        if stage + 2 < len(self.buffers):
            self.swap(stage + 1).start()

    def settle(self):
        for stage in range(len(self.buffers) - 1):
            self.swap(stage).wait_send()


def doubling_scratch(shape):
    stages = len(cube_dims())
    return [pltpu.VMEM(shape, jnp.float32)] * (stages + 1) + [pltpu.SemaphoreType.DMA((stages,))] * 2


def on_device(
    image_tokens, text_states, text_segments, image_segment, out_grad,
    norm1_gain, norm1_bias, self_query, self_key, self_value, self_output,
    norm2_gain, norm2_bias, cross_query, cross_key, cross_value, cross_output,
    norm3_gain, norm3_bias, mlp_in, mlp_in_bias, mlp_out, mlp_out_bias,
):
    tokens = image_tokens[0]
    rows, width = tokens.shape
    hidden = mlp_in.shape[1]
    vectors = (
        norm1_gain, norm1_bias, norm2_gain, norm2_bias,
        norm3_gain, norm3_bias, mlp_in_bias, mlp_out_bias,
    )
    sizes = [v.shape[0] for v in vectors]
    shard = self_query.shape[0]
    owners = width // shard
    parts = hidden // width
    orders = halving_orders()
    spread = [order[::-1] for order in orders]
    w_query, w_key, w_value, shared, text_full = alone(
        Gather(
            [(w, spread, (1, 16)) for w in (self_query, self_key, self_value, pack_vectors(vectors))]
            + [(text_states[0], [cube_dims(("narrow",))], (1, 32))]
        ),
        1,
    )
    shared = shared.reshape(owners, -1, 128)
    given = shared[:, :, :shard].transpose(1, 0, 2).reshape(-1, width)
    up_bias = shared[:, 6, : sizes[6]].reshape(1, -1)
    mask = (text_segments[0] == image_segment[0, 0]).astype(jnp.int32)
    mask = jnp.concatenate([mask, mask]).reshape(-1, 1)

    late = parts // 2

    def part(k):
        return (mlp_in, spread, (2, 16), width * k, width * (k + 1))

    (normed_one, queries, keys, values, mixed_self, sums_self), (*weights_two, up_first) = attend(
        tokens, given, (w_query, w_key, w_value),
        Gather(
            [
                (w, spread, (2, 16))
                for w in (self_output, cross_query, cross_key, cross_value, cross_output)
            ]
            + [(mlp_in, spread, (2, 16), 0, width)]
        ),
        ((1, 0), (2, 0), (3, 0), (5, 0)), 2,
    )
    (x1, h2, q2, a2, x2, h3, k2, v2), (down, *up_more) = middle(
        tokens, mixed_self, text_full, mask, given, weights_two,
        Gather([(mlp_out, spread, (2, 16))] + [part(k) for k in range(1, parts - late)]),
        ((0, 1), (1, 1), (2, 0), (3, 0)), 3,
    )
    (
        dx2, grad_up_bias, grad_gain_three, grad_bias_three, grad_down_bias,
        grad_down, hidden_act, grad_up, near_sums,
    ) = mlp(
        x2, h3, out_grad[0], given, [up_first, *up_more],
        Gather([(mlp_in, spread, (1, 16), width * k, width * (k + 1)) for k in range(parts - late, parts)]),
        up_bias, down, 2, ((2, 3, 5, 7, 8), (0, 1, 3, 5, 6, 7)), orders[4:], 4,
    )
    w_output, c_query, c_key, c_value, c_output = weights_two
    (
        dx1, grad_mixed, grad_self_out, grad_cross_query, grad_cross_out, grad_k2, grad_v2,
        grad_gain_two, grad_bias_two,
    ), (grad_down,) = middle_back(
        dx2, x1, mixed_self, h2, q2, a2, k2, v2, mask, given, (w_output, c_query, c_output),
        Scatter([(grad_down, orders, (1, 16))]), ((0, 1), (2, 1), (3, 1)), 5,
    )
    (
        grad_queries, grad_keys, grad_values, *late, text_term,
    ), (*far_sums, grad_self_out, grad_cross_query, grad_cross_out) = attend_back(
        queries, keys, values, grad_mixed, sums_self, normed_one,
        (grad_k2, grad_v2, text_full, c_key, c_value),
        Scatter(
            [(g, orders, (1, 32)) for g in (*grad_up, grad_self_out, grad_cross_query, grad_cross_out)]
        ),
        ((1, 0), (4, 0), (6, 0), (7, 0)), 6,
    )
    self_terms = (grad_queries, grad_keys, grad_values)
    others = (
        grad_gain_two, grad_bias_two, grad_gain_three, grad_bias_three, grad_down_bias, grad_up_bias,
    )
    (image_grad, block_out, vector_sums), (
        grad_self_query, grad_self_key, grad_self_value, grad_cross_key, grad_cross_value, text_grad,
    ) = first_back(
        tokens, dx1, given, others, (w_query, w_key, w_value), self_terms, x2, hidden_act, down,
        Scatter(
            [(g, orders, (1, 16)) for g in late] + [(text_term, [cube_dims(("narrow",))], (1, 32))]
        ),
        (1,), 7,
    )
    (
        grad_self_query, grad_self_key, grad_self_value, grad_self_out,
        grad_cross_query, grad_cross_key, grad_cross_value, grad_cross_out,
        grad_up, grad_down, text_grad,
    ) = hand_over(
        [
            (g,)
            for g in (
                grad_self_query, grad_self_key, grad_self_value, grad_self_out,
                grad_cross_query, grad_cross_key, grad_cross_value, grad_cross_out,
            )
        ]
        + [(*near_sums, *far_sums), (grad_down,), (text_grad,)]
    )
    place = lax.axis_index(AXES)
    flat = vector_sums.reshape(-1)
    rows_of = (0, 1, 2, 3, 4, 5, 7, 6)
    vector_grads = [
        lax.dynamic_slice_in_dim(flat, row * width + place * size, size)
        for row, size in zip(rows_of, sizes)
    ]
    return (
        block_out[None], image_grad[None], text_grad[None],
        vector_grads[0], vector_grads[1],
        grad_self_query, grad_self_key, grad_self_value, grad_self_out,
        vector_grads[2], vector_grads[3],
        grad_cross_query, grad_cross_key, grad_cross_value, grad_cross_out,
        vector_grads[4], vector_grads[5],
        grad_up, vector_grads[6], grad_down, vector_grads[7],
    )


def solution(mesh):
    placed = (
        P(("wide", "narrow"), None, None),
        P("wide", "narrow", None),
        P("wide", None),
        P("wide", "narrow"),
        P(("wide", "narrow"), None, None),
        P(("wide", "narrow")),
        P(("wide", "narrow")),
        P(("wide", "narrow"), None),
        P(("wide", "narrow"), None),
        P(("wide", "narrow"), None),
        P(("wide", "narrow"), None),
        P(("wide", "narrow")),
        P(("wide", "narrow")),
        P(("wide", "narrow"), None),
        P(("wide", "narrow"), None),
        P(("wide", "narrow"), None),
        P(("wide", "narrow"), None),
        P(("wide", "narrow")),
        P(("wide", "narrow")),
        P(("wide", "narrow"), None),
        P(("wide", "narrow")),
        P(("wide", "narrow"), None),
        P(("wide", "narrow")),
    )
    return jax.shard_map(
        on_device,
        mesh=mesh,
        in_specs=placed,
        out_specs=(
            P(("wide", "narrow"), None, None),
            P(("wide", "narrow"), None, None),
            P("wide", "narrow", None),
            P(("wide", "narrow")),
            P(("wide", "narrow")),
            P(("wide", "narrow"), None),
            P(("wide", "narrow"), None),
            P(("wide", "narrow"), None),
            P(("wide", "narrow"), None),
            P(("wide", "narrow")),
            P(("wide", "narrow")),
            P(("wide", "narrow"), None),
            P(("wide", "narrow"), None),
            P(("wide", "narrow"), None),
            P(("wide", "narrow"), None),
            P(("wide", "narrow")),
            P(("wide", "narrow")),
            P(("wide", "narrow"), None),
            P(("wide", "narrow")),
            P(("wide", "narrow"), None),
            P(("wide", "narrow")),
        ),
        check_vma=False,
    )
```
